512 devices in a mesh: frames: 128 (over x, y, z_lo), tensor: 4 (over z_hi, core).
Axes of the slice: x: 4, y: 8, z: 8 (z_hi: 2, z_lo: 4; z = z_hi * 4 + z_lo), core: 2. Of those that a mesh axis runs over, the one named last changes fastest.
Arguments:
- tokens: bfloat16 [49152, 1280], P('frames', 'tensor'), may hold values from -24 to 24
- reference_image: bfloat16 [384, 1280], P('frames'), may hold values from -6 to 6
- query_weight: bfloat16 [1280, 1280], P(None, 'tensor'), may hold values from -0.15625 to 0.15625
- key_weight: bfloat16 [1280, 1280], P(None, 'tensor'), may hold values from -0.15625 to 0.15625
- value_weight: bfloat16 [1280, 1280], P(None, 'tensor'), may hold values from -0.15625 to 0.15625
- ref_weight: bfloat16 [1280, 1280], P(None, 'tensor'), may hold values from -0.15625 to 0.15625
- cotangent: bfloat16 [49152, 1280], P('frames', 'tensor'), may hold values from -6 to 6
Outputs:
- attended: bfloat16 [49152, 1280], P('frames', 'tensor')
- token_grads: bfloat16 [49152, 1280], P('frames', 'tensor')
- query_weight_grad: float32 [1280, 1280], P('frames', 'tensor')
- ref_key_grads: bfloat16 [384, 1280], P('frames', 'tensor')
- ref_value_grads: bfloat16 [384, 1280], P('frames', 'tensor')
The draws below stay inside these ranges and needn't reach their ends.
All inputs are finite; a program needn't handle non-finite values.
Results may differ from the reference program's by a relative error of at most 0.019.
Values may be sent and summed in bfloat16 or wider, within the bound.
No kernel may reach another device: no remote copies, remote signals or barrier semaphores. Data moves between devices by JAX's collectives and lax.ppermute only.
A program may use at most 64 MiB of HBM per device.

```python
import math
import jax
import jax.numpy as jnp
from jax import lax

D = 1280
H = 20
E = 64
P_SIZE = 384
TOKENS = 49152
N_TENSOR = 4


def raised(result, key, source, target, blocks, factor):
    owner, partner = [(jnp.arange(result.shape[axis_at]) // (result.shape[axis_at] // blocks)).reshape([-1 if axis == axis_at else 1 for axis in range(result.ndim)]) for axis_at in (source, target)]
    chosen = jax.random.permutation(key, blocks)[partner]
    strong = (owner == chosen) | (owner == (partner + blocks // 2) % blocks)
    return jnp.where(strong, factor * result, result)


def block_scale(rng, dims, pieces, least, top_value):
    gain, own = 1.0, jax.random.fold_in(rng, 6)
    for dim, blocks in pieces:
        steps = jnp.exp(jax.random.uniform(jax.random.fold_in(own, dim), (blocks,), jnp.float32, least / len(pieces), top_value / len(pieces)))
        gain = gain * jnp.repeat(steps, dims[dim] // blocks).reshape([-1 if axis == dim else 1 for axis in range(len(dims))])
    return gain


def noise(key, extent, deviation, reach, split=(), held_as=jnp.bfloat16):
    entries = deviation * jax.random.normal(key, extent, jnp.float32)
    if split:
        entries = entries * block_scale(key, extent, split, -0.22, 0.18)
    return jnp.clip(entries, -reach, reach).astype(held_as)


def bell_draw_with(key, shape, deviation, most, cuts, heavy, held_as=jnp.bfloat16):
    entries = deviation * jax.random.normal(key, shape, jnp.float32)
    if cuts:
        entries = entries * block_scale(key, shape, cuts, -0.22, 0.18)
    return jnp.clip(raised(entries, jax.random.fold_in(key, 3), *heavy), -most, most).astype(held_as)


def setup_inputs(seed: int = 0) -> dict:
    key_of = jax.random.split(jax.random.key(seed), 8)
    tokens = bell_draw_with(key_of[0], (TOKENS, D), 1.0, 24.0, ((0, 128), (1, 4)), (0, 1, 128, 5.5))
    reference_image = noise(key_of[1], (P_SIZE, D), 1.0, 6.0, ((0, 128),))
    query_weight = noise(key_of[2], (D, D), D ** -0.5, 0.15625, ((1, 4),))
    key_weight = noise(key_of[3], (D, D), D ** -0.5, 0.15625, ((1, 4),))
    value_weight = noise(key_of[4], (D, D), D ** -0.5, 0.15625, ((1, 4),))
    ref_weight = noise(key_of[5], (D, D), D ** -0.5, 0.15625, ((1, 4),))
    cotangent = noise(key_of[6], (TOKENS, D), 1.0, 6.0, ((0, 128), (1, 4)))
    return dict(tokens=tokens, reference_image=reference_image, query_weight=query_weight, key_weight=key_weight, value_weight=value_weight, ref_weight=ref_weight, cotangent=cotangent)


def round_low(values):
    return lax.optimization_barrier(values.astype(jnp.bfloat16)).astype(jnp.float32)

def reference(tokens, reference_image, query_weight, key_weight, value_weight, ref_weight, cotangent):
    ref_hidden = (reference_image.astype(jnp.float32) + jnp.dot(reference_image, ref_weight, preferred_element_type=jnp.float32)).astype(jnp.bfloat16)
    ref_keys = jnp.dot(ref_hidden, key_weight, preferred_element_type=jnp.float32).astype(jnp.bfloat16)
    ref_values = jnp.dot(ref_hidden, value_weight, preferred_element_type=jnp.float32).astype(jnp.bfloat16)
    queries = jnp.dot(tokens, query_weight, preferred_element_type=jnp.float32).astype(jnp.bfloat16)
    keys_all = jnp.dot(tokens, key_weight, preferred_element_type=jnp.float32).astype(jnp.bfloat16)
    values_all = jnp.dot(tokens, value_weight, preferred_element_type=jnp.float32).astype(jnp.bfloat16)
    frame_count = tokens.shape[0] // P_SIZE
    score_scale = 1.0 / math.sqrt(E)

    def frame_step(carry, items):
        query_f, key_f, value_f, grad_f = items
        key_list = jnp.concatenate([key_f, ref_keys], 0).astype(jnp.float32).reshape(2 * P_SIZE, H, E)
        value_list = jnp.concatenate([value_f, ref_values], 0).astype(jnp.float32).reshape(2 * P_SIZE, H, E)
        query_heads = query_f.astype(jnp.float32).reshape(P_SIZE, H, E)
        grad_heads = grad_f.astype(jnp.float32).reshape(P_SIZE, H, E)
        scores = jnp.einsum('phe,khe->hpk', query_heads, key_list) * score_scale
        probs = jax.nn.softmax(scores, axis=-1)
        probs_low = round_low(probs)
        attended_f = jnp.einsum('hpk,khe->phe', probs_low, value_list).reshape(P_SIZE, D).astype(jnp.bfloat16)
        prob_grads = jnp.einsum('phe,khe->hpk', grad_heads, value_list)
        score_grads = probs * (prob_grads - lax.optimization_barrier(jnp.sum(probs * prob_grads, axis=-1, keepdims=True))) * score_scale
        score_low = round_low(score_grads)
        query_grads_f = jnp.einsum('hpk,khe->phe', score_low, key_list).reshape(P_SIZE, D).astype(jnp.bfloat16)
        key_grads_f = jnp.einsum('hpk,phe->khe', score_low, query_heads).reshape(2 * P_SIZE, D)
        value_grads_f = jnp.einsum('hpk,phe->khe', probs_low, grad_heads).reshape(2 * P_SIZE, D)
        carry = (carry[0] + key_grads_f[P_SIZE:], carry[1] + value_grads_f[P_SIZE:])
        return (carry, (attended_f, query_grads_f, key_grads_f[:P_SIZE].astype(jnp.bfloat16), value_grads_f[:P_SIZE].astype(jnp.bfloat16)))
    stacked = (queries.reshape(frame_count, P_SIZE, D), keys_all.reshape(frame_count, P_SIZE, D), values_all.reshape(frame_count, P_SIZE, D), cotangent.reshape(frame_count, P_SIZE, D))
    start_sums = (jnp.zeros((P_SIZE, D), jnp.float32), jnp.zeros((P_SIZE, D), jnp.float32))
    (ref_key_sum, ref_value_sum), results = lax.scan(frame_step, start_sums, stacked)
    attended = results[0].reshape(-1, D)
    query_grads = results[1].reshape(-1, D)
    key_grads = results[2].reshape(-1, D)
    value_grads = results[3].reshape(-1, D)
    block_width = D // N_TENSOR
    total = jnp.zeros((tokens.shape[0], D), jnp.float32)
    for block in range(N_TENSOR):
        low_col = block * block_width
        high_col = low_col + block_width
        partial_sum = jnp.dot(query_grads[:, low_col:high_col], query_weight[:, low_col:high_col].T, preferred_element_type=jnp.float32)
        partial_sum = partial_sum + jnp.dot(key_grads[:, low_col:high_col], key_weight[:, low_col:high_col].T, preferred_element_type=jnp.float32)
        partial_sum = partial_sum + jnp.dot(value_grads[:, low_col:high_col], value_weight[:, low_col:high_col].T, preferred_element_type=jnp.float32)
        total = total + round_low(partial_sum)
    token_grads = total.astype(jnp.bfloat16)
    query_weight_grad = jnp.dot(tokens.T, query_grads, preferred_element_type=jnp.float32)
    return (attended, token_grads, query_weight_grad, ref_key_sum.astype(jnp.bfloat16), ref_value_sum.astype(jnp.bfloat16))
```

```python
import math

import jax
import jax.numpy as jnp
from jax import lax
from jax.sharding import Mesh
from jax.sharding import PartitionSpec as P

E = 64
P_SIZE = 384
FRAMES = ("x", "y", "z")
TENSOR = ("h", "c")


def per_device(
    tokens, reference_image, query_weight, key_weight, value_weight, ref_weight, cotangent
):
    width_here = tokens.shape[1]
    row_total = tokens.shape[0]
    frames_here = row_total // P_SIZE
    heads_here = width_here // E
    score_scale = 1.0 / math.sqrt(E)
    start_col = lax.axis_index(TENSOR) * width_here
    source_cols = lax.dynamic_slice_in_dim(reference_image, start_col, width_here, 1)
    ref_cols = (
        source_cols.astype(jnp.float32)
        + jnp.dot(reference_image, ref_weight, preferred_element_type=jnp.float32)
    ).astype(jnp.bfloat16)
    rows_here = reference_image.shape[0]
    ref_hidden = lax.all_gather(ref_cols, TENSOR, axis=1, tiled=True)
    ref_pair = jnp.concatenate(
        [
            jnp.dot(ref_hidden, key_weight, preferred_element_type=jnp.float32),
            jnp.dot(ref_hidden, value_weight, preferred_element_type=jnp.float32),
        ],
        axis=1,
    ).astype(jnp.bfloat16)
    n_frames = P_SIZE // rows_here
    ref_pair = jnp.broadcast_to(ref_pair.reshape(1, -1, 128), (n_frames, rows_here * 5, 128))
    ref_all = lax.all_to_all(ref_pair, FRAMES, 0, 0, tiled=True).reshape(P_SIZE, 2 * width_here)
    ref_keys, ref_values = ref_all[:, :width_here], ref_all[:, width_here:]
    whole_tokens = lax.all_gather(tokens, TENSOR, axis=1, tiled=True)
    queries = jnp.dot(whole_tokens, query_weight, preferred_element_type=jnp.float32).astype(
        jnp.bfloat16
    )
    own_keys = jnp.dot(whole_tokens, key_weight, preferred_element_type=jnp.float32).astype(
        jnp.bfloat16
    )
    own_values = jnp.dot(whole_tokens, value_weight, preferred_element_type=jnp.float32).astype(
        jnp.bfloat16
    )
    frame_shape = (frames_here, P_SIZE, heads_here, E)
    query_split = queries.reshape(frame_shape)
    key_split = own_keys.reshape(frame_shape)
    value_split = own_values.reshape(frame_shape)
    grad_split = cotangent.reshape(frame_shape)
    ref_key_split = ref_keys.reshape(P_SIZE, heads_here, E)
    ref_value_split = ref_values.reshape(P_SIZE, heads_here, E)
    own_scores = jnp.einsum(
        "fphe,fkhe->fhpk", query_split, key_split, preferred_element_type=jnp.float32
    )
    ref_scores = jnp.einsum(
        "fphe,khe->fhpk", query_split, ref_key_split, preferred_element_type=jnp.float32
    )
    scores = jnp.concatenate([own_scores, ref_scores], -1) * score_scale
    probs = jax.nn.softmax(scores, axis=-1)
    probs_low = probs.astype(jnp.bfloat16)
    attended = jnp.einsum(
        "fhpk,fkhe->fphe", probs_low[..., :P_SIZE], value_split, preferred_element_type=jnp.float32
    )
    attended = attended + jnp.einsum(
        "fhpk,khe->fphe",
        probs_low[..., P_SIZE:],
        ref_value_split,
        preferred_element_type=jnp.float32,
    )
    attended = attended.reshape(row_total, width_here).astype(jnp.bfloat16)
    own_grads = jnp.einsum(
        "fphe,fkhe->fhpk", grad_split, value_split, preferred_element_type=jnp.float32
    )
    ref_grads = jnp.einsum(
        "fphe,khe->fhpk", grad_split, ref_value_split, preferred_element_type=jnp.float32
    )
    prob_grads = jnp.concatenate([own_grads, ref_grads], -1)
    score_grads = (
        probs * (prob_grads - jnp.sum(probs * prob_grads, axis=-1, keepdims=True)) * score_scale
    ).astype(jnp.bfloat16)
    query_grads = jnp.einsum(
        "fhpk,fkhe->fphe", score_grads[..., :P_SIZE], key_split, preferred_element_type=jnp.float32
    )
    query_grads = query_grads + jnp.einsum(
        "fhpk,khe->fphe",
        score_grads[..., P_SIZE:],
        ref_key_split,
        preferred_element_type=jnp.float32,
    )
    query_grads = query_grads.reshape(row_total, width_here).astype(jnp.bfloat16)
    key_grads = (
        jnp.einsum(
            "fhpk,fphe->fkhe",
            score_grads[..., :P_SIZE],
            query_split,
            preferred_element_type=jnp.float32,
        )
        .reshape(row_total, width_here)
        .astype(jnp.bfloat16)
    )
    value_grads = (
        jnp.einsum(
            "fhpk,fphe->fkhe",
            probs_low[..., :P_SIZE],
            grad_split,
            preferred_element_type=jnp.float32,
        )
        .reshape(row_total, width_here)
        .astype(jnp.bfloat16)
    )
    ref_key_part = jnp.einsum(
        "fhpk,fphe->khe", score_grads[..., P_SIZE:], query_split, preferred_element_type=jnp.float32
    ).reshape(P_SIZE, width_here)
    ref_value_part = jnp.einsum(
        "fhpk,fphe->khe", probs_low[..., P_SIZE:], grad_split, preferred_element_type=jnp.float32
    ).reshape(P_SIZE, width_here)
    back_dims = (((1,), (1,)), ((), ()))
    token_part = lax.dot_general(
        query_grads, query_weight, back_dims, preferred_element_type=jnp.float32
    )
    token_part = token_part + lax.dot_general(
        key_grads, key_weight, back_dims, preferred_element_type=jnp.float32
    )
    token_part = token_part + lax.dot_general(
        value_grads, value_weight, back_dims, preferred_element_type=jnp.float32
    )
    weight_part = lax.dot_general(
        whole_tokens, query_grads, (((0,), (0,)), ((), ())), preferred_element_type=jnp.float32
    )
    sums = jnp.concatenate(
        [
            ref_key_part.reshape(n_frames, -1),
            ref_value_part.reshape(n_frames, -1),
            weight_part.reshape(n_frames, -1),
        ],
        axis=1,
    ).astype(jnp.bfloat16)
    sums = lax.all_to_all(sums.reshape(n_frames, -1, 128), FRAMES, 0, 0, tiled=True)
    sums = jnp.sum(sums.astype(jnp.float32), axis=0).reshape(-1)
    ref_size = rows_here * width_here
    token_blocks = token_part.astype(jnp.bfloat16).reshape(row_total, 2, 2, width_here)
    core = lax.axis_index("c")
    kept = lax.dynamic_index_in_dim(token_blocks, core, 2, False)
    sent = lax.dynamic_index_in_dim(token_blocks, 1 - core, 2, False)
    got = lax.ppermute(sent, "c", [(0, 1), (1, 0)])
    paired = (kept.astype(jnp.float32) + got.astype(jnp.float32)).astype(jnp.bfloat16)
    half = lax.axis_index("h")
    kept = lax.dynamic_index_in_dim(paired, half, 1, False)
    sent = lax.dynamic_index_in_dim(paired, 1 - half, 1, False)
    got = lax.ppermute(sent, "h", [(0, 1), (1, 0)])
    token_grads = (kept.astype(jnp.float32) + got.astype(jnp.float32)).astype(jnp.bfloat16)
    return (
        attended,
        token_grads,
        sums[2 * ref_size :].reshape(-1, width_here),
        sums[:ref_size].reshape(rows_here, width_here).astype(jnp.bfloat16),
        sums[ref_size : 2 * ref_size].reshape(rows_here, width_here).astype(jnp.bfloat16),
    )


def solution(mesh):
    mesh = Mesh(mesh.devices.reshape(4, 8, 4, 2, 2), ("x", "y", "z", "h", "c"))
    return jax.shard_map(
        per_device,
        mesh=mesh,
        in_specs=(
            P(FRAMES, TENSOR),
            P(FRAMES, None),
            P(None, TENSOR),
            P(None, TENSOR),
            P(None, TENSOR),
            P(None, TENSOR),
            P(FRAMES, TENSOR),
        ),
        out_specs=(P(FRAMES, TENSOR),) * 5,
        check_vma=False,
    )
```

```python
import functools
import math

import jax
import jax.numpy as jnp
from jax import lax
from jax.experimental import pallas as pl
from jax.experimental.pallas import tpu as pltpu
from jax.sharding import Mesh
from jax.sharding import PartitionSpec as P

E = 64
P_SIZE = 384
HEADS = 5
WIDTH = HEADS * E
FRAMES = ("x", "y", "z")
TENSOR = ("h", "c")
NX, NYZ = 4, 32
REF_ROWS = 3
ROWS_OUT = 10
HALF_ROWS = ROWS_OUT // 2
LANES = 128
GROUPS = 2 * WIDTH // LANES
SCALE = 1.0 / math.sqrt(E)
F32 = jnp.float32
BF16 = jnp.bfloat16


def dot(a, b, a_dim, b_dim):
    return lax.dot_general(a, b, (((a_dim,), (b_dim,)), ((), ())), preferred_element_type=F32)


def attention_kernel(
    q_ref, k_ref, v_ref, r_ref, g_ref, tok_ref, o_ref, dq_ref, dk_ref, dv_ref, pack_ref,
    ot_ref, dqt_ref, sums_ref, dw_ref,
):
    for head in range(HEADS):
        lo, hi = head * E, head * E + E
        q, g = q_ref[:, lo:hi], g_ref[:, lo:hi]
        k = jnp.concatenate([k_ref[:, lo:hi], r_ref[:, lo:hi]], 0)
        v = jnp.concatenate([v_ref[:, lo:hi], r_ref[:, WIDTH + lo : WIDTH + hi]], 0)
        s = dot(k, q, 1, 1)
        s = jnp.exp2((s - jnp.max(s, axis=0, keepdims=True)) * (SCALE * math.log2(math.e)))
        p = s * (1.0 / jnp.sum(s, axis=0, keepdims=True))
        p_low = p.astype(BF16)
        ot_ref[lo:hi, :] = dot(v, p_low, 0, 0)
        dp = dot(v, g, 1, 1)
        ds = (p * (dp - jnp.sum(p * dp, axis=0, keepdims=True))).astype(BF16)
        dqt_ref[lo:hi, :] = dot(k, ds, 0, 0) * SCALE
        dk = dot(ds, q, 1, 0) * SCALE
        dv = dot(p_low, g, 1, 0)
        dk_ref[:, lo:hi] = dk[:P_SIZE].astype(BF16)
        dv_ref[:, lo:hi] = dv[:P_SIZE].astype(BF16)
        for col, part in ((lo, dk), (WIDTH + lo, dv)):
            at = col % LANES
            sums_ref[col // LANES, :, at : at + E] = part[P_SIZE:]
    o_ref[...] = ot_ref[...].T.astype(BF16)
    dq = dqt_ref[...].T.astype(BF16)
    dq_ref[...] = dq
    for x in range(NX):
        for row in range(REF_ROWS):
            first = x * REF_ROWS * NYZ + row
            for group in range(GROUPS):
                pack_ref[x, NYZ * row : NYZ * (row + 1), LANES * group : LANES * (group + 1)] = (
                    sums_ref[group, pl.ds(first, NYZ, stride=REF_ROWS), :].astype(BF16)
                )
        dw = dot(tok_ref[x * WIDTH : (x + 1) * WIDTH, :], dq, 1, 0)
        dw_ref[0], dw_ref[1] = dw[:, :LANES], dw[:, LANES : 2 * LANES]
        dw_ref[2, :, :E] = dw[:, 2 * LANES :]
        for row in range(HALF_ROWS):
            at = NYZ * (REF_ROWS + row)
            left, right = [
                [dw_ref[group, pl.ds(first, NYZ, stride=ROWS_OUT), :] for group in range(3)]
                for first in (row, row + HALF_ROWS)
            ]
            last = jnp.concatenate([left[2][:, :E], right[2][:, :E]], axis=1)
            for group, part in enumerate((left[0], left[1], right[0], right[1], last)):
                pack_ref[x, at : at + NYZ, LANES * group : LANES * (group + 1)] = part.astype(BF16)


def attention(q, k, v, ref_pair, g, tok):
    rows = REF_ROWS + HALF_ROWS
    full = jax.ShapeDtypeStruct((P_SIZE, WIDTH), BF16)
    return pl.pallas_call(
        attention_kernel,
        out_shape=(full,) * 4 + (jax.ShapeDtypeStruct((NX, NYZ * rows, 2 * WIDTH), BF16),),
        scratch_shapes=[
            pltpu.VMEM((WIDTH, P_SIZE), F32),
            pltpu.VMEM((WIDTH, P_SIZE), F32),
            pltpu.VMEM((GROUPS, P_SIZE, LANES), F32),
            pltpu.VMEM((3, WIDTH, LANES), F32),
        ],
        compiler_params=pltpu.CompilerParams(vmem_limit_bytes=48 * 1024 * 1024),
    )(q, k, v, ref_pair, g, tok)


def regroup_kernel(in_ref, out_ref, held_ref):
    rows = REF_ROWS + HALF_ROWS
    for row in range(rows):
        at = NYZ * row
        part = in_ref[0, at : at + NYZ, :].astype(F32)
        for x in range(1, NX):
            part = part + in_ref[x, at : at + NYZ, :].astype(F32)
        for group in range(GROUPS):
            held_ref[group, pl.ds(row, NYZ, stride=rows), :] = part[
                :, LANES * group : LANES * (group + 1)
            ]
    for group in range(GROUPS):
        out_ref[:, LANES * group : LANES * (group + 1)] = held_ref[group].astype(BF16)


def regroup(parts):
    rows = REF_ROWS + HALF_ROWS
    return pl.pallas_call(
        regroup_kernel,
        out_shape=jax.ShapeDtypeStruct((NYZ * rows, 2 * WIDTH), BF16),
        scratch_shapes=[pltpu.VMEM((GROUPS, NYZ * rows, LANES), F32)],
    )(parts)


def per_device(
    tokens, reference_image, query_weight, key_weight, value_weight, ref_weight, cotangent
):
    start_col = lax.axis_index(TENSOR) * WIDTH
    source_cols = lax.dynamic_slice_in_dim(reference_image, start_col, WIDTH, 1)
    ref_cols = (source_cols.astype(F32) + dot(reference_image, ref_weight, 1, 0)).astype(BF16)
    ref_block = jnp.pad(ref_cols, ((0, 16 - REF_ROWS), (0, P_SIZE - WIDTH)))
    gathered = lax.all_gather(
        jnp.concatenate([tokens.T, ref_block], axis=0), TENSOR, axis=0, tiled=False
    )
    ref_hidden = gathered[:, WIDTH : WIDTH + REF_ROWS, :WIDTH].transpose(1, 0, 2)
    ref_hidden = ref_hidden.reshape(REF_ROWS, 4 * WIDTH)
    ref_pair = jnp.concatenate(
        [dot(ref_hidden, key_weight, 1, 0), dot(ref_hidden, value_weight, 1, 0)], axis=1
    ).astype(BF16)
    n_frames = NX * NYZ
    ref_pair = jnp.broadcast_to(ref_pair.reshape(1, -1, 128), (n_frames, REF_ROWS * 5, 128))
    ref_all = lax.all_to_all(ref_pair, FRAMES, 0, 0, tiled=True).reshape(P_SIZE, 2 * WIDTH)
    tok = gathered[:, :WIDTH].reshape(4 * WIDTH, P_SIZE)
    queries = dot(tok, query_weight, 0, 0).astype(BF16)
    keys = dot(tok, key_weight, 0, 0).astype(BF16)
    values = dot(tok, value_weight, 0, 0).astype(BF16)
    attended, query_grads, key_grads, value_grads, pack = attention(
        queries, keys, values, ref_all, cotangent, tok
    )
    pack = lax.all_to_all(pack, "x", 0, 0, tiled=True)
    token_part = (
        dot(query_weight, query_grads, 1, 1)
        + dot(key_weight, key_grads, 1, 1)
        + dot(value_weight, value_grads, 1, 1)
    )
    token_blocks = token_part.astype(BF16).reshape(2, 2, WIDTH, P_SIZE)
    core, half = lax.axis_index("c"), lax.axis_index("h")
    kept = lax.dynamic_index_in_dim(token_blocks, core, 1, False)
    sent = lax.dynamic_index_in_dim(token_blocks, 1 - core, 1, False)
    got = lax.ppermute(sent, "c", [(0, 1), (1, 0)])
    paired = (kept.astype(F32) + got.astype(F32)).astype(BF16)
    pack, _ = lax.optimization_barrier((pack, paired))
    pack = regroup(pack).reshape(NYZ, REF_ROWS + HALF_ROWS, 2 * WIDTH)
    pack = lax.all_to_all(pack, ("y", "z"), 0, 0, tiled=True)
    sums = jnp.sum(pack.astype(F32), axis=0)
    left = jnp.concatenate([sums[REF_ROWS:, : 2 * LANES], sums[REF_ROWS:, 4 * LANES : 4 * LANES + E]], 1)
    right = jnp.concatenate([sums[REF_ROWS:, 2 * LANES : 4 * LANES], sums[REF_ROWS:, 4 * LANES + E :]], 1)
    weight_grad = jnp.concatenate([left, right], axis=0)
    kept = lax.dynamic_index_in_dim(paired, half, 0, False)
    sent = lax.dynamic_index_in_dim(paired, 1 - half, 0, False)
    got = lax.ppermute(sent, "h", [(0, 1), (1, 0)])
    token_grads = (kept.astype(F32) + got.astype(F32)).astype(BF16).T
    return (
        attended,
        token_grads,
        weight_grad,
        sums[:REF_ROWS, :WIDTH].astype(BF16),
        sums[:REF_ROWS, WIDTH:].astype(BF16),
    )


def solution(mesh):
    mesh = Mesh(mesh.devices.reshape(4, 8, 4, 2, 2), FRAMES + TENSOR)
    return jax.shard_map(
        per_device,
        mesh=mesh,
        in_specs=(
            P(FRAMES, TENSOR),
            P(FRAMES, None),
            P(None, TENSOR),
            P(None, TENSOR),
            P(None, TENSOR),
            P(None, TENSOR),
            P(FRAMES, TENSOR),
        ),
        out_specs=(P(FRAMES, TENSOR),) * 5,
        check_vma=False,
    )
```

```python
import math

import jax
import jax.numpy as jnp
from jax import lax
from jax.experimental import pallas as pl
from jax.experimental.pallas import tpu as pltpu
from jax.sharding import Mesh
from jax.sharding import PartitionSpec as P

E = 64
P_SIZE = 384
HEADS = 5
WIDTH = HEADS * E
FRAMES = ("x", "y", "z")
TENSOR = ("h", "c")
NX, NYZ = 4, 32
REF_ROWS = 3
ROWS_OUT = 10
HALF_ROWS = ROWS_OUT // 2
LANES = 128
VMEM_BYTES = 24 * 1024 * 1024
GROUPS = 2 * WIDTH // LANES
SCALE = 1.0 / math.sqrt(E)
F32 = jnp.float32
BF16 = jnp.bfloat16


def dot(a, b, a_dim, b_dim):
    return lax.dot_general(a, b, (((a_dim,), (b_dim,)), ((), ())), preferred_element_type=F32)


def project_kernel(half_ref, t_ref, wq_ref, wk_ref, wv_ref, tok_ref, q_ref, k_ref, v_ref):
    half = half_ref[0]
    for core in range(2):
        for slot in range(2):
            at = pl.multiple_of((2 * lax.rem(half + slot, 2) + core) * WIDTH, E)
            tok_ref[pl.ds(at, WIDTH), :] = t_ref[core, slot]
    tok = tok_ref[...]
    for w_ref, out_ref in ((wq_ref, q_ref), (wk_ref, k_ref), (wv_ref, v_ref)):
        out_ref[...] = dot(w_ref[...], tok, 1, 0).T.astype(BF16)


def project(half, parts, wq, wk, wv):
    full = jax.ShapeDtypeStruct((P_SIZE, WIDTH), BF16)
    vmem = pl.BlockSpec(memory_space=pltpu.VMEM)
    return pl.pallas_call(
        project_kernel,
        out_shape=(jax.ShapeDtypeStruct((4 * WIDTH, P_SIZE), BF16),) + (full,) * 3,
        in_specs=[pl.BlockSpec(memory_space=pltpu.SMEM)] + [vmem] * 4,
        out_specs=[vmem] * 4,
        compiler_params=pltpu.CompilerParams(vmem_limit_bytes=VMEM_BYTES),
    )(half.reshape(1), parts, wq, wk, wv)


def attention_kernel(
    q_ref, k_ref, v_ref, pair_ref, gt_ref, tok_ref, ot_ref, dq_ref, dk_ref, dv_ref, pack_ref,
    wide_ref, r_ref, dqt_ref, dw_ref,
):
    n_frames = NX * NYZ
    wide_ref[...] = pair_ref[...].astype(F32)
    for row in range(REF_ROWS):
        for group in range(GROUPS):
            r_ref[n_frames * row : n_frames * (row + 1), LANES * group : LANES * (group + 1)] = (
                wide_ref[pl.ds(row * GROUPS + group, n_frames, stride=16), :].astype(BF16)
            )
    g_all = gt_ref[...].astype(F32).T.astype(BF16)
    for head in range(HEADS):
        lo, hi = head * E, head * E + E
        q, g = q_ref[:, lo:hi], g_all[:, lo:hi]
        k = jnp.concatenate([k_ref[:, lo:hi], r_ref[:, lo:hi]], 0)
        v = jnp.concatenate([v_ref[:, lo:hi], r_ref[:, WIDTH + lo : WIDTH + hi]], 0)
        s = dot(k, q, 1, 1)
        s = jnp.exp2((s - jnp.max(s, axis=0, keepdims=True)) * (SCALE * math.log2(math.e)))
        p = s * (1.0 / jnp.sum(s, axis=0, keepdims=True))
        p_low = p.astype(BF16)
        ot_ref[lo:hi, :] = dot(v, p_low, 0, 0).astype(BF16)
        dp = dot(v, gt_ref[lo:hi, :], 1, 0)
        ds = (p * (dp - jnp.sum(p * dp, axis=0, keepdims=True))).astype(BF16)
        dqt_ref[lo:hi, :] = dot(k, ds, 0, 0) * SCALE
        dk = dot(ds, q, 1, 0) * SCALE
        dv = dot(p_low, g, 1, 0)
        dk_ref[:, lo:hi] = dk[:P_SIZE].astype(BF16)
        dv_ref[:, lo:hi] = dv[:P_SIZE].astype(BF16)
        for col, part in ((lo, dk), (WIDTH + lo, dv)):
            for x in range(NX):
                for row in range(REF_ROWS):
                    at = P_SIZE + n_frames * row + NYZ * x
                    pack_ref[x, NYZ * row : NYZ * (row + 1), col : col + E] = part[
                        at : at + NYZ
                    ].astype(BF16)
    dq = dqt_ref[...].T.astype(BF16)
    dq_ref[...] = dq
    for x in range(NX):
        dw = dot(tok_ref[x * WIDTH : (x + 1) * WIDTH, :], dq, 1, 0)
        dw_ref[0], dw_ref[1] = dw[:, :LANES], dw[:, LANES : 2 * LANES]
        dw_ref[2, :, :E] = dw[:, 2 * LANES :]
        for row in range(HALF_ROWS):
            at = NYZ * (REF_ROWS + row)
            left, right = [
                [dw_ref[group, pl.ds(first, NYZ, stride=ROWS_OUT), :] for group in range(3)]
                for first in (row, row + HALF_ROWS)
            ]
            last = jnp.concatenate([left[2][:, :E], right[2][:, :E]], axis=1)
            for group, part in enumerate((left[0], left[1], right[0], right[1], last)):
                pack_ref[x, at : at + NYZ, LANES * group : LANES * (group + 1)] = part.astype(BF16)


def attention(q, k, v, pair, gt, tok):
    rows = REF_ROWS + HALF_ROWS
    full = jax.ShapeDtypeStruct((P_SIZE, WIDTH), BF16)
    return pl.pallas_call(
        attention_kernel,
        out_shape=(jax.ShapeDtypeStruct((WIDTH, P_SIZE), BF16),)
        + (full,) * 3
        + (jax.ShapeDtypeStruct((NX, NYZ * rows, 2 * WIDTH), BF16),),
        scratch_shapes=[
            pltpu.VMEM((NX * NYZ * 16, LANES), F32),
            pltpu.VMEM((P_SIZE, 2 * WIDTH), BF16),
            pltpu.VMEM((WIDTH, P_SIZE), F32),
            pltpu.VMEM((3, WIDTH, LANES), F32),
        ],
        compiler_params=pltpu.CompilerParams(vmem_limit_bytes=VMEM_BYTES),
    )(q, k, v, pair, gt, tok)


def token_kernel(core_ref, dq_ref, dk_ref, dv_ref, wq_ref, wk_ref, wv_ref, kept_ref, sent_ref):
    core = core_ref[0]
    total = dot(dq_ref[...], wq_ref[...], 1, 0)
    total = total + dot(dk_ref[...], wk_ref[...], 1, 0)
    total = total + dot(dv_ref[...], wv_ref[...], 1, 0)
    total = total.T.astype(BF16)
    for half in range(2):
        zero, one = [total[(2 * half + c) * WIDTH : (2 * half + c + 1) * WIDTH] for c in range(2)]
        kept_ref[half] = jnp.where(core == 0, zero, one)
        sent_ref[half] = jnp.where(core == 0, one, zero)


def token_parts(core, dq, dk, dv, wq, wk, wv):
    vmem = pl.BlockSpec(memory_space=pltpu.VMEM)
    return pl.pallas_call(
        token_kernel,
        out_shape=(jax.ShapeDtypeStruct((2, WIDTH, P_SIZE), BF16),) * 2,
        in_specs=[pl.BlockSpec(memory_space=pltpu.SMEM)] + [vmem] * 6,
        out_specs=[vmem] * 2,
        compiler_params=pltpu.CompilerParams(vmem_limit_bytes=VMEM_BYTES),
    )(core.reshape(1), dq, dk, dv, wq, wk, wv)


def regroup_kernel(in_ref, out_ref, held_ref):
    rows = REF_ROWS + HALF_ROWS
    for row in range(rows):
        at = NYZ * row
        part = in_ref[0, at : at + NYZ, :].astype(F32)
        for x in range(1, NX):
            part = part + in_ref[x, at : at + NYZ, :].astype(F32)
        for group in range(GROUPS):
            held_ref[group, pl.ds(row, NYZ, stride=rows), :] = part[
                :, LANES * group : LANES * (group + 1)
            ]
    for group in range(GROUPS):
        out_ref[:, LANES * group : LANES * (group + 1)] = held_ref[group].astype(BF16)


def regroup(parts):
    rows = REF_ROWS + HALF_ROWS
    return pl.pallas_call(
        regroup_kernel,
        out_shape=jax.ShapeDtypeStruct((NYZ * rows, 2 * WIDTH), BF16),
        scratch_shapes=[pltpu.VMEM((GROUPS, NYZ * rows, LANES), F32)],
    )(parts)


def per_device(
    tokens, reference_image, query_weight, key_weight, value_weight, ref_weight, cotangent
):
    core, half = lax.axis_index("c"), lax.axis_index("h")
    swap = [(0, 1), (1, 0)]
    wq, wk, wv = query_weight.T, key_weight.T, value_weight.T
    own = tokens.T
    other = lax.ppermute(own, "h", swap)
    start_col = (2 * half + core) * WIDTH
    source_cols = lax.dynamic_slice_in_dim(reference_image, start_col, WIDTH, 1)
    ref_cols = (source_cols.astype(F32) + dot(reference_image, ref_weight, 1, 0)).astype(BF16)
    ref_hidden = lax.all_gather(ref_cols, TENSOR, axis=1, tiled=True)
    pair = jnp.concatenate([dot(ref_hidden, wk, 1, 1), dot(ref_hidden, wv, 1, 1)], axis=1)
    pair = pair.astype(BF16).reshape(1, REF_ROWS * GROUPS, LANES)
    pair = jnp.pad(pair, ((0, 0), (0, 16 - REF_ROWS * GROUPS), (0, 0)))
    pair = lax.all_to_all(
        jnp.broadcast_to(pair, (NYZ, 16, LANES)), ("y", "z"), 0, 0, tiled=True
    ).reshape(1, NYZ * 16, LANES)
    pair = lax.all_to_all(jnp.broadcast_to(pair, (NX, NYZ * 16, LANES)), "x", 0, 0, tiled=True)
    parts = lax.all_gather(jnp.stack([own, other]), "c", axis=0, tiled=False)
    tok, queries, keys, values = project(half, parts, wq, wk, wv)
    attended, query_grads, key_grads, value_grads, pack = attention(
        queries, keys, values, pair.reshape(NX * NYZ * 16, LANES), cotangent.T, tok
    )
    pack = lax.all_to_all(pack, "x", 0, 0, tiled=True)
    kept, sent = token_parts(core, query_grads, key_grads, value_grads, wq, wk, wv)
    got = lax.ppermute(sent, "c", swap)
    paired = (kept.astype(F32) + got.astype(F32)).astype(BF16)
    kept = lax.dynamic_index_in_dim(paired, half, 0, False)
    sent = lax.dynamic_index_in_dim(paired, 1 - half, 0, False)
    got = lax.ppermute(sent, "h", swap)
    token_grads = (kept.astype(F32) + got.astype(F32)).astype(BF16).T
    pack = regroup(pack)
    pack, _ = lax.optimization_barrier((pack, got))
    pack = pack.reshape(NYZ, REF_ROWS + HALF_ROWS, 2 * WIDTH)
    pack = lax.all_to_all(pack, ("y", "z"), 0, 0, tiled=True)
    sums = jnp.sum(pack.astype(F32), axis=0)
    low, tail = sums[REF_ROWS:, : 4 * LANES], sums[REF_ROWS:, 4 * LANES :]
    left = jnp.concatenate([low[:, : 2 * LANES], tail[:, :E]], axis=1)
    right = jnp.concatenate([low[:, 2 * LANES :], tail[:, E:]], axis=1)
    return (
        attended.T,
        token_grads,
        jnp.concatenate([left, right], axis=0),
        sums[:REF_ROWS, :WIDTH].astype(BF16),
        sums[:REF_ROWS, WIDTH:].astype(BF16),
    )


def solution(mesh):
    mesh = Mesh(mesh.devices.reshape(4, 8, 4, 2, 2), FRAMES + TENSOR)
    return jax.shard_map(
        per_device,
        mesh=mesh,
        in_specs=(
            P(FRAMES, TENSOR),
            P(FRAMES, None),
            P(None, TENSOR),
            P(None, TENSOR),
            P(None, TENSOR),
            P(None, TENSOR),
            P(FRAMES, TENSOR),
        ),
        out_specs=(P(FRAMES, TENSOR),) * 5,
        check_vma=False,
    )
```

```python
import math

import jax
import jax.numpy as jnp
from jax import lax
from jax.experimental import pallas as pl
from jax.experimental.pallas import tpu as pltpu
from jax.sharding import Mesh
from jax.sharding import PartitionSpec as P

E = 64
P_SIZE = 384
HEADS = 5
WIDTH = HEADS * E
FRAMES = ("x", "y", "z")
TENSOR = ("h", "c")
NX, NYZ = 4, 32
REF_ROWS = 3
ROWS_OUT = 10
HALF_ROWS = ROWS_OUT // 2
LANES = 128
VMEM_BYTES = 24 * 1024 * 1024
GROUPS = 2 * WIDTH // LANES
SCALE = 1.0 / math.sqrt(E)
F32 = jnp.float32
BF16 = jnp.bfloat16


def dot(a, b, a_dim, b_dim):
    return lax.dot_general(a, b, (((a_dim,), (b_dim,)), ((), ())), preferred_element_type=F32)


def project_kernel(
    half_ref, t_ref, wq_ref, wk_ref, wv_ref, tok_out, q_out, k_out, v_out,
    tok_ref, q_ref, k_ref, v_ref, sem,
):
    half = half_ref[0]
    pairs = ((tok_ref, tok_out), (q_ref, q_out), (k_ref, k_out), (v_ref, v_out))
    copies = [pltpu.make_async_copy(a, b, sem.at[i]) for i, (a, b) in enumerate(pairs)]
    for core in range(2):
        for slot in range(2):
            at = pl.multiple_of((2 * lax.rem(half + slot, 2) + core) * WIDTH, E)
            tok_ref[pl.ds(at, WIDTH), :] = t_ref[core, slot]
    copies[0].start()
    tok = tok_ref[...]
    for i, (w_ref, out_ref) in enumerate(((wq_ref, q_ref), (wk_ref, k_ref), (wv_ref, v_ref))):
        out_ref[...] = dot(w_ref[...], tok, 1, 0).T.astype(BF16)
        copies[i + 1].start()
    for copy in copies:
        copy.wait()


def project(half, parts, wq, wk, wv):
    vmem = pl.BlockSpec(memory_space=pltpu.VMEM)
    return pl.pallas_call(
        project_kernel,
        out_shape=(pltpu.HBM((4 * WIDTH, P_SIZE), BF16),)
        + (pltpu.HBM((P_SIZE, WIDTH), BF16),) * 3,
        in_specs=[pl.BlockSpec(memory_space=pltpu.SMEM)] + [vmem] * 4,
        out_specs=[pl.BlockSpec(memory_space=pltpu.HBM)] * 4,
        scratch_shapes=[pltpu.VMEM((4 * WIDTH, P_SIZE), BF16)]
        + [pltpu.VMEM((P_SIZE, WIDTH), BF16)] * 3
        + [pltpu.SemaphoreType.DMA((4,))],
        compiler_params=pltpu.CompilerParams(vmem_limit_bytes=VMEM_BYTES),
    )(half.reshape(1), parts, wq, wk, wv)


def attention_kernel(
    q_in, k_in, v_in, pair_in, tok_in, gt_ref, ot_out, dq_out, dk_out, dv_out, pack_out,
    q_ref, k_ref, v_ref, pair_ref, tok_ref, wide_ref, r_ref, dqt_ref, dw_ref,
    ot_ref, dq_ref, dk_ref, dv_ref, pack_ref, in_sem, out_sem,
):
    n_frames = NX * NYZ
    pairs = (
        (pair_in, pair_ref), (k_in, k_ref), (q_in, q_ref), (v_in, v_ref), (tok_in, tok_ref)
    )
    loads = [pltpu.make_async_copy(a, b, in_sem.at[i]) for i, (a, b) in enumerate(pairs)]
    for load in loads:
        load.start()
    loads[0].wait()
    wide_ref[...] = pair_ref[...].astype(F32)
    for row in range(REF_ROWS):
        for group in range(GROUPS):
            r_ref[n_frames * row : n_frames * (row + 1), LANES * group : LANES * (group + 1)] = (
                wide_ref[pl.ds(row * GROUPS + group, n_frames, stride=16), :].astype(BF16)
            )
    g_all = gt_ref[...].astype(F32).T.astype(BF16)
    for load in loads[1:4]:
        load.wait()
    for head in range(HEADS):
        lo, hi = head * E, head * E + E
        q, g = q_ref[:, lo:hi], g_all[:, lo:hi]
        k = jnp.concatenate([k_ref[:, lo:hi], r_ref[:, lo:hi]], 0)
        v = jnp.concatenate([v_ref[:, lo:hi], r_ref[:, WIDTH + lo : WIDTH + hi]], 0)
        s = dot(k, q, 1, 1)
        s = jnp.exp2((s - jnp.max(s, axis=0, keepdims=True)) * (SCALE * math.log2(math.e)))
        p = s * (1.0 / jnp.sum(s, axis=0, keepdims=True))
        p_low = p.astype(BF16)
        ot_ref[lo:hi, :] = dot(v, p_low, 0, 0).astype(BF16)
        dp = dot(v, gt_ref[lo:hi, :], 1, 0)
        ds = (p * (dp - jnp.sum(p * dp, axis=0, keepdims=True))).astype(BF16)
        dqt_ref[lo:hi, :] = dot(k, ds, 0, 0) * SCALE
        dk = dot(ds, q, 1, 0) * SCALE
        dv = dot(p_low, g, 1, 0)
        dk_ref[:, lo:hi] = dk[:P_SIZE].astype(BF16)
        dv_ref[:, lo:hi] = dv[:P_SIZE].astype(BF16)
        for col, part in ((lo, dk), (WIDTH + lo, dv)):
            for x in range(NX):
                for row in range(REF_ROWS):
                    at = P_SIZE + n_frames * row + NYZ * x
                    pack_ref[x, NYZ * row : NYZ * (row + 1), col : col + E] = part[
                        at : at + NYZ
                    ].astype(BF16)
    dq = dqt_ref[...].T.astype(BF16)
    dq_ref[...] = dq
    loads[4].wait()
    pairs = ((ot_ref, ot_out), (dq_ref, dq_out), (dk_ref, dk_out), (dv_ref, dv_out))
    stores = [pltpu.make_async_copy(a, b, out_sem.at[NX + i]) for i, (a, b) in enumerate(pairs)]
    for store in stores:
        store.start()
    for x in range(NX):
        dw = dot(tok_ref[x * WIDTH : (x + 1) * WIDTH, :], dq, 1, 0)
        dw_ref[0], dw_ref[1] = dw[:, :LANES], dw[:, LANES : 2 * LANES]
        dw_ref[2, :, :E] = dw[:, 2 * LANES :]
        for row in range(HALF_ROWS):
            at = NYZ * (REF_ROWS + row)
            left, right = [
                [dw_ref[group, pl.ds(first, NYZ, stride=ROWS_OUT), :] for group in range(3)]
                for first in (row, row + HALF_ROWS)
            ]
            last = jnp.concatenate([left[2][:, :E], right[2][:, :E]], axis=1)
            for group, part in enumerate((left[0], left[1], right[0], right[1], last)):
                pack_ref[x, at : at + NYZ, LANES * group : LANES * (group + 1)] = part.astype(BF16)
        stores.append(pltpu.make_async_copy(pack_ref.at[x], pack_out.at[x], out_sem.at[x]))
        stores[-1].start()
    for store in stores:
        store.wait()


def attention(q, k, v, pair, gt, tok):
    hbm, vmem = [pl.BlockSpec(memory_space=space) for space in (pltpu.HBM, pltpu.VMEM)]
    rows = REF_ROWS + HALF_ROWS
    return pl.pallas_call(
        attention_kernel,
        out_shape=(pltpu.HBM((WIDTH, P_SIZE), BF16),)
        + (pltpu.HBM((P_SIZE, WIDTH), BF16),) * 3
        + (pltpu.HBM((NX, NYZ * rows, 2 * WIDTH), BF16),),
        in_specs=[hbm] * 5 + [vmem],
        out_specs=[hbm] * 5,
        scratch_shapes=[pltpu.VMEM((P_SIZE, WIDTH), BF16)] * 3
        + [
            pltpu.VMEM((NX * NYZ * 16, LANES), BF16),
            pltpu.VMEM((4 * WIDTH, P_SIZE), BF16),
            pltpu.VMEM((NX * NYZ * 16, LANES), F32),
            pltpu.VMEM((P_SIZE, 2 * WIDTH), BF16),
            pltpu.VMEM((WIDTH, P_SIZE), F32),
            pltpu.VMEM((3, WIDTH, LANES), F32),
            pltpu.VMEM((WIDTH, P_SIZE), BF16),
            pltpu.VMEM((P_SIZE, WIDTH), BF16),
            pltpu.VMEM((P_SIZE, WIDTH), BF16),
            pltpu.VMEM((P_SIZE, WIDTH), BF16),
            pltpu.VMEM((NX, NYZ * rows, 2 * WIDTH), BF16),
            pltpu.SemaphoreType.DMA((5,)),
            pltpu.SemaphoreType.DMA((NX + 4,)),
        ],
        compiler_params=pltpu.CompilerParams(vmem_limit_bytes=VMEM_BYTES),
    )(*[pltpu.with_memory_space_constraint(a, pltpu.HBM) for a in (q, k, v, pair, tok)], gt)


def token_kernel(core_ref, dq_ref, dk_ref, dv_ref, wq_ref, wk_ref, wv_ref, kept_ref, sent_ref):
    core = core_ref[0]
    total = dot(dq_ref[...], wq_ref[...], 1, 0)
    total = total + dot(dk_ref[...], wk_ref[...], 1, 0)
    total = total + dot(dv_ref[...], wv_ref[...], 1, 0)
    total = total.T.astype(BF16)
    for half in range(2):
        zero, one = [total[(2 * half + c) * WIDTH : (2 * half + c + 1) * WIDTH] for c in range(2)]
        kept_ref[half] = jnp.where(core == 0, zero, one)
        sent_ref[half] = jnp.where(core == 0, one, zero)


def token_parts(core, dq, dk, dv, wq, wk, wv):
    vmem = pl.BlockSpec(memory_space=pltpu.VMEM)
    return pl.pallas_call(
        token_kernel,
        out_shape=(jax.ShapeDtypeStruct((2, WIDTH, P_SIZE), BF16),) * 2,
        in_specs=[pl.BlockSpec(memory_space=pltpu.SMEM)] + [vmem] * 6,
        out_specs=[vmem] * 2,
        compiler_params=pltpu.CompilerParams(vmem_limit_bytes=VMEM_BYTES),
    )(core.reshape(1), dq, dk, dv, wq, wk, wv)


def regroup_kernel(in_ref, out_ref, held_ref):
    rows = REF_ROWS + HALF_ROWS
    for row in range(rows):
        at = NYZ * row
        part = in_ref[0, at : at + NYZ, :].astype(F32)
        for x in range(1, NX):
            part = part + in_ref[x, at : at + NYZ, :].astype(F32)
        for group in range(GROUPS):
            held_ref[group, pl.ds(row, NYZ, stride=rows), :] = part[
                :, LANES * group : LANES * (group + 1)
            ]
    for group in range(GROUPS):
        out_ref[:, LANES * group : LANES * (group + 1)] = held_ref[group].astype(BF16)


def regroup(parts):
    rows = REF_ROWS + HALF_ROWS
    return pl.pallas_call(
        regroup_kernel,
        out_shape=jax.ShapeDtypeStruct((NYZ * rows, 2 * WIDTH), BF16),
        scratch_shapes=[pltpu.VMEM((GROUPS, NYZ * rows, LANES), F32)],
        compiler_params=pltpu.CompilerParams(vmem_limit_bytes=8 * 1024 * 1024),
    )(parts)


def per_device(
    tokens, reference_image, query_weight, key_weight, value_weight, ref_weight, cotangent
):
    core, half = lax.axis_index("c"), lax.axis_index("h")
    swap = [(0, 1), (1, 0)]
    wq, wk, wv = query_weight.T, key_weight.T, value_weight.T
    own = tokens.T
    other = lax.ppermute(own, "h", swap)
    start_col = (2 * half + core) * WIDTH
    source_cols = lax.dynamic_slice_in_dim(reference_image, start_col, WIDTH, 1)
    ref_cols = (source_cols.astype(F32) + dot(reference_image, ref_weight, 1, 0)).astype(BF16)
    ref_hidden = lax.all_gather(ref_cols, TENSOR, axis=1, tiled=True)
    pair = jnp.concatenate([dot(ref_hidden, wk, 1, 1), dot(ref_hidden, wv, 1, 1)], axis=1)
    pair = pair.astype(BF16).reshape(1, REF_ROWS * GROUPS, LANES)
    pair, other = lax.optimization_barrier((pair, other))
    pair = jnp.pad(pair, ((0, 0), (0, 16 - REF_ROWS * GROUPS), (0, 0)))
    pair = lax.all_to_all(
        jnp.broadcast_to(pair, (NYZ, 16, LANES)), ("y", "z"), 0, 0, tiled=True
    ).reshape(1, NYZ * 16, LANES)
    pair = lax.all_to_all(jnp.broadcast_to(pair, (NX, NYZ * 16, LANES)), "x", 0, 0, tiled=True)
    parts = lax.all_gather(jnp.stack([own, other]), "c", axis=0, tiled=False)
    tok, queries, keys, values = project(half, parts, wq, wk, wv)
    attended, query_grads, key_grads, value_grads, pack = attention(
        queries, keys, values, pair.reshape(NX * NYZ * 16, LANES), cotangent.T, tok
    )
    pack = lax.all_to_all(pack, "x", 0, 0, tiled=True)
    kept, sent = token_parts(core, query_grads, key_grads, value_grads, wq, wk, wv)
    got = lax.ppermute(sent, "c", swap)
    paired = (kept.astype(F32) + got.astype(F32)).astype(BF16)
    kept = lax.dynamic_index_in_dim(paired, half, 0, False)
    sent = lax.dynamic_index_in_dim(paired, 1 - half, 0, False)
    got = lax.ppermute(sent, "h", swap)
    token_grads = (kept.astype(F32) + got.astype(F32)).astype(BF16).T
    pack = regroup(pack)
    pack, _ = lax.optimization_barrier((pack, sent))
    pack = pack.reshape(NYZ, REF_ROWS + HALF_ROWS, 2 * WIDTH)
    pack = lax.all_to_all(pack, ("y", "z"), 0, 0, tiled=True)
    sums = jnp.sum(pack.astype(F32), axis=0)
    low, tail = sums[REF_ROWS:, : 4 * LANES], sums[REF_ROWS:, 4 * LANES :]
    left = jnp.concatenate([low[:, : 2 * LANES], tail[:, :E]], axis=1)
    right = jnp.concatenate([low[:, 2 * LANES :], tail[:, E:]], axis=1)
    return (
        attended.T,
        token_grads,
        jnp.concatenate([left, right], axis=0),
        sums[:REF_ROWS, :WIDTH].astype(BF16),
        sums[:REF_ROWS, WIDTH:].astype(BF16),
    )


def solution(mesh):
    mesh = Mesh(mesh.devices.reshape(4, 8, 4, 2, 2), FRAMES + TENSOR)
    return jax.shard_map(
        per_device,
        mesh=mesh,
        in_specs=(
            P(FRAMES, TENSOR),
            P(FRAMES, None),
            P(None, TENSOR),
            P(None, TENSOR),
            P(None, TENSOR),
            P(None, TENSOR),
            P(FRAMES, TENSOR),
        ),
        out_specs=(P(FRAMES, TENSOR),) * 5,
        check_vma=False,
    )
```

```python
import math

import jax
import jax.numpy as jnp
from jax import lax
from jax.experimental import pallas as pl
from jax.experimental.pallas import tpu as pltpu
from jax.sharding import Mesh
from jax.sharding import PartitionSpec as P

E = 64
P_SIZE = 384
HEADS = 5
WIDTH = HEADS * E
FRAMES = ("x", "y", "z")
TENSOR = ("h", "c")
NX, NYZ = 4, 32
REF_ROWS = 3
ROWS_OUT = 10
HALF_ROWS = ROWS_OUT // 2
LANES = 128
CUT = 128
VMEM_BYTES = 24 * 1024 * 1024
GROUPS = 2 * WIDTH // LANES
SCALE = 1.0 / math.sqrt(E)
F32 = jnp.float32
BF16 = jnp.bfloat16


def dot(a, b, a_dim, b_dim):
    return lax.dot_general(a, b, (((a_dim,), (b_dim,)), ((), ())), preferred_element_type=F32)


def project_kernel(
    half_ref, t_ref, wq_ref, wk_ref, wv_ref, tok_out, q_out, k_out, v_out,
    tok_ref, q_ref, k_ref, v_ref, sem,
):
    half = half_ref[0]
    pairs = ((tok_ref, tok_out), (q_ref, q_out), (k_ref, k_out), (v_ref, v_out))
    copies = [pltpu.make_async_copy(a, b, sem.at[i]) for i, (a, b) in enumerate(pairs)]
    for core in range(2):
        for slot in range(2):
            at = pl.multiple_of((2 * lax.rem(half + slot, 2) + core) * WIDTH, E)
            tok_ref[pl.ds(at, WIDTH), :] = t_ref[core, slot]
    copies[0].start()
    tok = tok_ref[...]
    for i, (w_ref, out_ref) in enumerate(((wq_ref, q_ref), (wk_ref, k_ref), (wv_ref, v_ref))):
        out_ref[...] = dot(w_ref[...], tok, 1, 0).T.astype(BF16)
        copies[i + 1].start()
    for copy in copies:
        copy.wait()


def project(half, parts, wq, wk, wv):
    vmem = pl.BlockSpec(memory_space=pltpu.VMEM)
    return pl.pallas_call(
        project_kernel,
        out_shape=(pltpu.HBM((4 * WIDTH, P_SIZE), BF16),)
        + (pltpu.HBM((P_SIZE, WIDTH), BF16),) * 3,
        in_specs=[pl.BlockSpec(memory_space=pltpu.SMEM)] + [vmem] * 4,
        out_specs=[pl.BlockSpec(memory_space=pltpu.HBM)] * 4,
        scratch_shapes=[pltpu.VMEM((4 * WIDTH, P_SIZE), BF16)]
        + [pltpu.VMEM((P_SIZE, WIDTH), BF16)] * 3
        + [pltpu.SemaphoreType.DMA((4,))],
        compiler_params=pltpu.CompilerParams(vmem_limit_bytes=VMEM_BYTES),
    )(half.reshape(1), parts, wq, wk, wv)


def ref_kernel(half_ref, p_ref, wk_ref, wv_ref, out_ref, rows_ref):
    first = half_ref[0] == 0
    blocks = []
    for half in range(2):
        for core in range(2):
            own, other = p_ref[core, 0].astype(F32), p_ref[core, 1].astype(F32)
            blocks.append(jnp.where(first, own, other) if half == 0 else jnp.where(first, other, own))
    hidden = jnp.concatenate(blocks, axis=1).astype(BF16)
    pair = jnp.concatenate([dot(hidden, wk_ref[...], 1, 1), dot(hidden, wv_ref[...], 1, 1)], axis=1)
    rows_ref[...] = jnp.zeros_like(rows_ref)
    for row in range(REF_ROWS):
        for group in range(GROUPS):
            at = row * GROUPS + group
            rows_ref[at : at + 1, :] = pair[row : row + 1, LANES * group : LANES * (group + 1)]
    out_ref[...] = jnp.broadcast_to(rows_ref[...].astype(BF16)[None], out_ref.shape)


def ref_pair(half, parts, wk, wv):
    vmem = pl.BlockSpec(memory_space=pltpu.VMEM)
    return pl.pallas_call(
        ref_kernel,
        out_shape=jax.ShapeDtypeStruct((NYZ, 16, LANES), BF16),
        in_specs=[pl.BlockSpec(memory_space=pltpu.SMEM)] + [vmem] * 3,
        out_specs=vmem,
        scratch_shapes=[pltpu.VMEM((16, LANES), F32)],
        compiler_params=pltpu.CompilerParams(vmem_limit_bytes=12 * 1024 * 1024),
    )(half.reshape(1), parts, wk, wv)


def attention_kernel(
    q_in, k_in, v_in, pair_in, tok_in, gt_ref, ot_out, dq_out, dk_out, dv_out, pack_out,
    q_ref, k_ref, v_ref, pair_ref, tok_ref, wide_ref, r_ref, dqt_ref, dw_ref,
    ot_ref, dq_ref, dk_ref, dv_ref, pack_ref, in_sem, out_sem,
):
    n_frames = NX * NYZ
    pairs = (
        (pair_in, pair_ref), (k_in, k_ref), (q_in, q_ref), (v_in, v_ref), (tok_in, tok_ref)
    )
    loads = [pltpu.make_async_copy(a, b, in_sem.at[i]) for i, (a, b) in enumerate(pairs)]
    for load in loads:
        load.start()
    loads[0].wait()
    wide_ref[...] = pair_ref[...].astype(F32)
    for row in range(REF_ROWS):
        for group in range(GROUPS):
            r_ref[n_frames * row : n_frames * (row + 1), LANES * group : LANES * (group + 1)] = (
                wide_ref[pl.ds(row * GROUPS + group, n_frames, stride=16), :].astype(BF16)
            )
    g_all = gt_ref[...].astype(F32).T.astype(BF16)
    for load in loads[1:4]:
        load.wait()
    for head in range(HEADS):
        lo, hi = head * E, head * E + E
        q, g = q_ref[:, lo:hi], g_all[:, lo:hi]
        k = jnp.concatenate([k_ref[:, lo:hi], r_ref[:, lo:hi]], 0)
        v = jnp.concatenate([v_ref[:, lo:hi], r_ref[:, WIDTH + lo : WIDTH + hi]], 0)
        s = dot(k, q, 1, 1)
        s = jnp.exp2((s - jnp.max(s, axis=0, keepdims=True)) * (SCALE * math.log2(math.e)))
        p = s * (1.0 / jnp.sum(s, axis=0, keepdims=True))
        p_low = p.astype(BF16)
        ot_ref[lo:hi, :] = dot(v, p_low, 0, 0).astype(BF16)
        dp = dot(v, gt_ref[lo:hi, :], 1, 0)
        ds = (p * (dp - jnp.sum(p * dp, axis=0, keepdims=True))).astype(BF16)
        dqt_ref[lo:hi, :] = dot(k, ds, 0, 0) * SCALE
        dk = dot(ds, q, 1, 0) * SCALE
        dv = dot(p_low, g, 1, 0)
        dk_ref[:, lo:hi] = dk[:P_SIZE].astype(BF16)
        dv_ref[:, lo:hi] = dv[:P_SIZE].astype(BF16)
        for col, part in ((lo, dk), (WIDTH + lo, dv)):
            for x in range(NX):
                for row in range(REF_ROWS):
                    at = P_SIZE + n_frames * row + NYZ * x
                    pack_ref[x, NYZ * row : NYZ * (row + 1), col : col + E] = part[
                        at : at + NYZ
                    ].astype(BF16)
    dq = dqt_ref[...].T.astype(BF16)
    dq_ref[...] = dq
    loads[4].wait()
    pairs = ((ot_ref, ot_out), (dq_ref, dq_out), (dk_ref, dk_out), (dv_ref, dv_out))
    stores = [pltpu.make_async_copy(a, b, out_sem.at[NX + i]) for i, (a, b) in enumerate(pairs)]
    for store in stores:
        store.start()
    for x in range(NX):
        dw = dot(tok_ref[x * WIDTH : (x + 1) * WIDTH, :], dq, 1, 0)
        dw_ref[0], dw_ref[1] = dw[:, :LANES], dw[:, LANES : 2 * LANES]
        dw_ref[2, :, :E] = dw[:, 2 * LANES :]
        for row in range(HALF_ROWS):
            at = NYZ * (REF_ROWS + row)
            left, right = [
                [dw_ref[group, pl.ds(first, NYZ, stride=ROWS_OUT), :] for group in range(3)]
                for first in (row, row + HALF_ROWS)
            ]
            last = jnp.concatenate([left[2][:, :E], right[2][:, :E]], axis=1)
            for group, part in enumerate((left[0], left[1], right[0], right[1], last)):
                pack_ref[x, at : at + NYZ, LANES * group : LANES * (group + 1)] = part.astype(BF16)
        stores.append(pltpu.make_async_copy(pack_ref.at[x], pack_out.at[x], out_sem.at[x]))
        stores[-1].start()
    for store in stores:
        store.wait()


def attention(q, k, v, pair, gt, tok):
    hbm, vmem = [pl.BlockSpec(memory_space=space) for space in (pltpu.HBM, pltpu.VMEM)]
    rows = REF_ROWS + HALF_ROWS
    return pl.pallas_call(
        attention_kernel,
        out_shape=(pltpu.HBM((WIDTH, P_SIZE), BF16),)
        + (pltpu.HBM((P_SIZE, WIDTH), BF16),) * 3
        + (pltpu.HBM((NX, NYZ * rows, 2 * WIDTH), BF16),),
        in_specs=[hbm] * 5 + [vmem],
        out_specs=[hbm] * 5,
        scratch_shapes=[pltpu.VMEM((P_SIZE, WIDTH), BF16)] * 3
        + [
            pltpu.VMEM((NX * NYZ * 16, LANES), BF16),
            pltpu.VMEM((4 * WIDTH, P_SIZE), BF16),
            pltpu.VMEM((NX * NYZ * 16, LANES), F32),
            pltpu.VMEM((P_SIZE, 2 * WIDTH), BF16),
            pltpu.VMEM((WIDTH, P_SIZE), F32),
            pltpu.VMEM((3, WIDTH, LANES), F32),
            pltpu.VMEM((WIDTH, P_SIZE), BF16),
            pltpu.VMEM((P_SIZE, WIDTH), BF16),
            pltpu.VMEM((P_SIZE, WIDTH), BF16),
            pltpu.VMEM((P_SIZE, WIDTH), BF16),
            pltpu.VMEM((NX, NYZ * rows, 2 * WIDTH), BF16),
            pltpu.SemaphoreType.DMA((5,)),
            pltpu.SemaphoreType.DMA((NX + 4,)),
        ],
        compiler_params=pltpu.CompilerParams(vmem_limit_bytes=VMEM_BYTES),
    )(*[pltpu.with_memory_space_constraint(a, pltpu.HBM) for a in (q, k, v, pair, tok)], gt)


def token_kernel(core_ref, dq_ref, dk_ref, dv_ref, wq_ref, wk_ref, wv_ref, kept_ref, sent_ref):
    core = core_ref[0]
    total = dot(dq_ref[...], wq_ref[...], 1, 0)
    total = total + dot(dk_ref[...], wk_ref[...], 1, 0)
    total = total + dot(dv_ref[...], wv_ref[...], 1, 0)
    total = total.T.astype(BF16)
    for half in range(2):
        zero, one = [total[(2 * half + c) * WIDTH : (2 * half + c + 1) * WIDTH] for c in range(2)]
        kept_ref[half] = jnp.where(core == 0, zero, one)
        sent_ref[half] = jnp.where(core == 0, one, zero)


def token_parts(core, dq, dk, dv, wq, wk, wv):
    vmem = pl.BlockSpec(memory_space=pltpu.VMEM)
    return pl.pallas_call(
        token_kernel,
        out_shape=(jax.ShapeDtypeStruct((2, WIDTH, P_SIZE), BF16),) * 2,
        in_specs=[pl.BlockSpec(memory_space=pltpu.SMEM)] + [vmem] * 6,
        out_specs=[vmem] * 2,
        compiler_params=pltpu.CompilerParams(vmem_limit_bytes=VMEM_BYTES),
    )(core.reshape(1), dq, dk, dv, wq, wk, wv)


def regroup_kernel(in_ref, out_ref, held_ref):
    rows = REF_ROWS + HALF_ROWS
    for row in range(rows):
        at = NYZ * row
        part = in_ref[0, at : at + NYZ, :].astype(F32)
        for x in range(1, NX):
            part = part + in_ref[x, at : at + NYZ, :].astype(F32)
        for group in range(GROUPS):
            held_ref[group, pl.ds(row, NYZ, stride=rows), :] = part[
                :, LANES * group : LANES * (group + 1)
            ]
    for group in range(GROUPS):
        out_ref[:, LANES * group : LANES * (group + 1)] = held_ref[group].astype(BF16)


def regroup(parts):
    rows = REF_ROWS + HALF_ROWS
    return pl.pallas_call(
        regroup_kernel,
        out_shape=jax.ShapeDtypeStruct((NYZ * rows, 2 * WIDTH), BF16),
        scratch_shapes=[pltpu.VMEM((GROUPS, NYZ * rows, LANES), F32)],
        compiler_params=pltpu.CompilerParams(vmem_limit_bytes=8 * 1024 * 1024),
    )(parts)


def per_device(
    tokens, reference_image, query_weight, key_weight, value_weight, ref_weight, cotangent
):
    core, half = lax.axis_index("c"), lax.axis_index("h")
    swap = [(0, 1), (1, 0)]
    wq, wk, wv = query_weight.T, key_weight.T, value_weight.T
    start_col = (2 * half + core) * WIDTH
    source_cols = lax.dynamic_slice_in_dim(reference_image, start_col, WIDTH, 1)
    ref_cols = (source_cols.astype(F32) + dot(reference_image, ref_weight, 1, 0)).astype(BF16)
    ref_cols = jnp.pad(ref_cols, ((0, 16 - REF_ROWS), (0, 0)))
    ref_other = lax.ppermute(ref_cols, "h", swap)
    own, _ = lax.optimization_barrier((tokens.T, ref_cols))
    other = lax.ppermute(own, "h", swap)
    ref_parts = lax.all_gather(jnp.stack([ref_cols, ref_other]), "c", axis=0, tiled=False)
    pair = ref_pair(half, ref_parts, wk, wv)
    pair, other = lax.optimization_barrier((pair, other))
    pair = lax.all_to_all(pair, ("y", "z"), 0, 0, tiled=True).reshape(1, NYZ * 16, LANES)
    pair = lax.all_to_all(jnp.broadcast_to(pair, (NX, NYZ * 16, LANES)), "x", 0, 0, tiled=True)
    parts = lax.all_gather(jnp.stack([own, other]), "c", axis=0, tiled=False)
    tok, queries, keys, values = project(half, parts, wq, wk, wv)
    attended, query_grads, key_grads, value_grads, pack = attention(
        queries, keys, values, pair.reshape(NX * NYZ * 16, LANES), cotangent.T, tok
    )
    pack = lax.all_to_all(pack, "x", 0, 0, tiled=True)
    kept, sent = token_parts(core, query_grads, key_grads, value_grads, wq, wk, wv)
    pieces = []
    for low, high in ((0, CUT), (CUT, WIDTH)):
        got = lax.ppermute(sent[:, low:high], "c", swap)
        both = (kept[:, low:high].astype(F32) + got.astype(F32)).astype(BF16)
        mine = lax.dynamic_index_in_dim(both, half, 0, False)
        theirs = lax.dynamic_index_in_dim(both, 1 - half, 0, False)
        got = lax.ppermute(theirs, "h", swap)
        pieces.append((mine.astype(F32) + got.astype(F32)).astype(BF16))
        if low == 0:
            pack, _ = lax.optimization_barrier((pack, got))
    token_grads = jnp.concatenate(pieces, axis=0).T
    pack = regroup(pack)
    pack = pack.reshape(NYZ, REF_ROWS + HALF_ROWS, 2 * WIDTH)
    pack = lax.all_to_all(pack, ("y", "z"), 0, 0, tiled=True)
    sums = jnp.sum(pack.astype(F32), axis=0)
    low, tail = sums[REF_ROWS:, : 4 * LANES], sums[REF_ROWS:, 4 * LANES :]
    left = jnp.concatenate([low[:, : 2 * LANES], tail[:, :E]], axis=1)
    right = jnp.concatenate([low[:, 2 * LANES :], tail[:, E:]], axis=1)
    return (
        attended.T,
        token_grads,
        jnp.concatenate([left, right], axis=0),
        sums[:REF_ROWS, :WIDTH].astype(BF16),
        sums[:REF_ROWS, WIDTH:].astype(BF16),
    )


def solution(mesh):
    mesh = Mesh(mesh.devices.reshape(4, 8, 4, 2, 2), FRAMES + TENSOR)
    return jax.shard_map(
        per_device,
        mesh=mesh,
        in_specs=(
            P(FRAMES, TENSOR),
            P(FRAMES, None),
            P(None, TENSOR),
            P(None, TENSOR),
            P(None, TENSOR),
            P(None, TENSOR),
            P(FRAMES, TENSOR),
        ),
        out_specs=(P(FRAMES, TENSOR),) * 5,
        check_vma=False,
    )
```

```python
import math

import jax
import jax.numpy as jnp
from jax import lax
from jax.experimental import pallas as pl
from jax.experimental.pallas import tpu as pltpu
from jax.sharding import Mesh
from jax.sharding import PartitionSpec as P

E = 64
P_SIZE = 384
HEADS = 5
WIDTH = HEADS * E
FRAMES = ("x", "y", "z")
TENSOR = ("h", "c")
NX, NYZ = 4, 32
REF_ROWS = 3
ROWS_OUT = 10
HALF_ROWS = ROWS_OUT // 2
LANES = 128
REGROUP_COST = 10**10
VMEM_BYTES = 24 * 1024 * 1024
GROUPS = 2 * WIDTH // LANES
SCALE = 1.0 / math.sqrt(E)
F32 = jnp.float32
BF16 = jnp.bfloat16


def dot(a, b, a_dim, b_dim):
    return lax.dot_general(a, b, (((a_dim,), (b_dim,)), ((), ())), preferred_element_type=F32)


def project_kernel(
    g_ref, wq_ref, wk_ref, wv_ref, tok_out, q_out, k_out, v_out, tok_ref, q_ref, k_ref, v_ref, sem
):
    pairs = ((tok_ref, tok_out), (q_ref, q_out), (k_ref, k_out), (v_ref, v_out))
    copies = [pltpu.make_async_copy(a, b, sem.at[i]) for i, (a, b) in enumerate(pairs)]
    for t in range(4):
        tok_ref[t * WIDTH : (t + 1) * WIDTH, :] = g_ref[t, :WIDTH, :]
    copies[0].start()
    tok = tok_ref[...]
    for i, (w_ref, out_ref) in enumerate(((wq_ref, q_ref), (wk_ref, k_ref), (wv_ref, v_ref))):
        out_ref[...] = dot(w_ref[...], tok, 1, 0).T.astype(BF16)
        copies[i + 1].start()
    for copy in copies:
        copy.wait()


def project(gathered, wq, wk, wv):
    return pl.pallas_call(
        project_kernel,
        out_shape=(pltpu.HBM((4 * WIDTH, P_SIZE), BF16),)
        + (pltpu.HBM((P_SIZE, WIDTH), BF16),) * 3,
        out_specs=[pl.BlockSpec(memory_space=pltpu.HBM)] * 4,
        scratch_shapes=[pltpu.VMEM((4 * WIDTH, P_SIZE), BF16)]
        + [pltpu.VMEM((P_SIZE, WIDTH), BF16)] * 3
        + [pltpu.SemaphoreType.DMA((4,))],
        compiler_params=pltpu.CompilerParams(vmem_limit_bytes=VMEM_BYTES),
    )(gathered, wq, wk, wv)


def ref_kernel(g_ref, wk_ref, wv_ref, out_ref, rows_ref):
    hidden = [g_ref[t, WIDTH : WIDTH + 16, :WIDTH].astype(F32) for t in range(4)]
    hidden = jnp.concatenate(hidden, axis=1).astype(BF16)
    pair = jnp.concatenate([dot(hidden, wk_ref[...], 1, 1), dot(hidden, wv_ref[...], 1, 1)], axis=1)
    rows_ref[...] = jnp.zeros_like(rows_ref)
    for row in range(REF_ROWS):
        for group in range(GROUPS):
            at = row * GROUPS + group
            rows_ref[at : at + 1, :] = pair[row : row + 1, LANES * group : LANES * (group + 1)]
    out_ref[...] = jnp.broadcast_to(rows_ref[...].astype(BF16)[None], out_ref.shape)


def ref_pair(gathered, wk, wv):
    return pl.pallas_call(
        ref_kernel,
        out_shape=jax.ShapeDtypeStruct((NYZ, 16, LANES), BF16),
        scratch_shapes=[pltpu.VMEM((16, LANES), F32)],
        compiler_params=pltpu.CompilerParams(vmem_limit_bytes=12 * 1024 * 1024),
    )(gathered, wk, wv)


def attention_kernel(
    q_in, k_in, v_in, pair_in, tok_in, gt_ref, ot_out, dq_out, dk_out, dv_out, pack_out,
    q_ref, k_ref, v_ref, pair_ref, tok_ref, wide_ref, r_ref, dqt_ref, dw_ref,
    ot_ref, dq_ref, dk_ref, dv_ref, pack_ref, in_sem, out_sem,
):
    n_frames = NX * NYZ
    pairs = (
        (pair_in, pair_ref), (k_in, k_ref), (q_in, q_ref), (v_in, v_ref), (tok_in, tok_ref)
    )
    loads = [pltpu.make_async_copy(a, b, in_sem.at[i]) for i, (a, b) in enumerate(pairs)]
    for load in loads:
        load.start()
    loads[0].wait()
    wide_ref[...] = pair_ref[...].astype(F32)
    for row in range(REF_ROWS):
        for group in range(GROUPS):
            r_ref[n_frames * row : n_frames * (row + 1), LANES * group : LANES * (group + 1)] = (
                wide_ref[pl.ds(row * GROUPS + group, n_frames, stride=16), :].astype(BF16)
            )
    g_all = gt_ref[...].astype(F32).T.astype(BF16)
    for load in loads[1:4]:
        load.wait()
    for head in range(HEADS):
        lo, hi = head * E, head * E + E
        q, g = q_ref[:, lo:hi], g_all[:, lo:hi]
        k = jnp.concatenate([k_ref[:, lo:hi], r_ref[:, lo:hi]], 0)
        v = jnp.concatenate([v_ref[:, lo:hi], r_ref[:, WIDTH + lo : WIDTH + hi]], 0)
        s = dot(k, q, 1, 1)
        s = jnp.exp2((s - jnp.max(s, axis=0, keepdims=True)) * (SCALE * math.log2(math.e)))
        p = s * (1.0 / jnp.sum(s, axis=0, keepdims=True))
        p_low = p.astype(BF16)
        ot_ref[lo:hi, :] = dot(v, p_low, 0, 0).astype(BF16)
        dp = dot(v, gt_ref[lo:hi, :], 1, 0)
        ds = (p * (dp - jnp.sum(p * dp, axis=0, keepdims=True))).astype(BF16)
        dqt_ref[lo:hi, :] = dot(k, ds, 0, 0) * SCALE
        dk = dot(ds, q, 1, 0) * SCALE
        dv = dot(p_low, g, 1, 0)
        dk_ref[:, lo:hi] = dk[:P_SIZE].astype(BF16)
        dv_ref[:, lo:hi] = dv[:P_SIZE].astype(BF16)
        for col, part in ((lo, dk), (WIDTH + lo, dv)):
            for x in range(NX):
                for row in range(REF_ROWS):
                    at = P_SIZE + n_frames * row + NYZ * x
                    pack_ref[x, NYZ * row : NYZ * (row + 1), col : col + E] = part[
                        at : at + NYZ
                    ].astype(BF16)
    dq = dqt_ref[...].T.astype(BF16)
    dq_ref[...] = dq
    loads[4].wait()
    pairs = ((ot_ref, ot_out), (dq_ref, dq_out), (dk_ref, dk_out), (dv_ref, dv_out))
    stores = [pltpu.make_async_copy(a, b, out_sem.at[NX + i]) for i, (a, b) in enumerate(pairs)]
    for store in stores:
        store.start()
    for x in range(NX):
        dw = dot(tok_ref[x * WIDTH : (x + 1) * WIDTH, :], dq, 1, 0)
        dw_ref[0], dw_ref[1] = dw[:, :LANES], dw[:, LANES : 2 * LANES]
        dw_ref[2, :, :E] = dw[:, 2 * LANES :]
        for row in range(HALF_ROWS):
            at = NYZ * (REF_ROWS + row)
            left, right = [
                [dw_ref[group, pl.ds(first, NYZ, stride=ROWS_OUT), :] for group in range(3)]
                for first in (row, row + HALF_ROWS)
            ]
            last = jnp.concatenate([left[2][:, :E], right[2][:, :E]], axis=1)
            for group, part in enumerate((left[0], left[1], right[0], right[1], last)):
                pack_ref[x, at : at + NYZ, LANES * group : LANES * (group + 1)] = part.astype(BF16)
        stores.append(pltpu.make_async_copy(pack_ref.at[x], pack_out.at[x], out_sem.at[x]))
        stores[-1].start()
    for store in stores:
        store.wait()


def attention(q, k, v, pair, gt, tok):
    hbm, vmem = [pl.BlockSpec(memory_space=space) for space in (pltpu.HBM, pltpu.VMEM)]
    rows = REF_ROWS + HALF_ROWS
    return pl.pallas_call(
        attention_kernel,
        out_shape=(pltpu.HBM((WIDTH, P_SIZE), BF16),)
        + (pltpu.HBM((P_SIZE, WIDTH), BF16),) * 3
        + (pltpu.HBM((NX, NYZ * rows, 2 * WIDTH), BF16),),
        in_specs=[hbm] * 5 + [vmem],
        out_specs=[hbm] * 5,
        scratch_shapes=[pltpu.VMEM((P_SIZE, WIDTH), BF16)] * 3
        + [
            pltpu.VMEM((NX * NYZ * 16, LANES), BF16),
            pltpu.VMEM((4 * WIDTH, P_SIZE), BF16),
            pltpu.VMEM((NX * NYZ * 16, LANES), F32),
            pltpu.VMEM((P_SIZE, 2 * WIDTH), BF16),
            pltpu.VMEM((WIDTH, P_SIZE), F32),
            pltpu.VMEM((3, WIDTH, LANES), F32),
            pltpu.VMEM((WIDTH, P_SIZE), BF16),
            pltpu.VMEM((P_SIZE, WIDTH), BF16),
            pltpu.VMEM((P_SIZE, WIDTH), BF16),
            pltpu.VMEM((P_SIZE, WIDTH), BF16),
            pltpu.VMEM((NX, NYZ * rows, 2 * WIDTH), BF16),
            pltpu.SemaphoreType.DMA((5,)),
            pltpu.SemaphoreType.DMA((NX + 4,)),
        ],
        compiler_params=pltpu.CompilerParams(vmem_limit_bytes=VMEM_BYTES),
    )(*[pltpu.with_memory_space_constraint(a, pltpu.HBM) for a in (q, k, v, pair, tok)], gt)


def token_kernel(
    core_ref, dq_in, dk_in, dv_in, wq_ref, wk_ref, wv_ref, kept_out, sent_out,
    dq_ref, dk_ref, dv_ref, kept_ref, sent_ref, in_sem, out_sem,
):
    pairs = ((dq_in, dq_ref), (dk_in, dk_ref), (dv_in, dv_ref))
    loads = [pltpu.make_async_copy(a, b, in_sem.at[i]) for i, (a, b) in enumerate(pairs)]
    for load in loads:
        load.start()
    core = core_ref[0]
    total = None
    for load, (d_ref, w_ref) in zip(
        loads, ((dq_ref, wq_ref), (dk_ref, wk_ref), (dv_ref, wv_ref))
    ):
        load.wait()
        part = dot(d_ref[...], w_ref[...], 1, 0)
        total = part if total is None else total + part
    total = total.T.astype(BF16)
    stores = []
    for half in range(2):
        zero, one = [total[(2 * half + c) * WIDTH : (2 * half + c + 1) * WIDTH] for c in range(2)]
        sent_ref[half] = jnp.where(core == 0, one, zero)
        kept_ref[half] = jnp.where(core == 0, zero, one)
        for i, (a, b) in enumerate(((sent_ref, sent_out), (kept_ref, kept_out))):
            store = pltpu.make_async_copy(a.at[half], b.at[half], out_sem.at[2 * half + i])
            store.start()
            stores.append(store)
    for store in stores:
        store.wait()


def token_parts(core, dq, dk, dv, wq, wk, wv):
    hbm, vmem = [pl.BlockSpec(memory_space=space) for space in (pltpu.HBM, pltpu.VMEM)]
    return pl.pallas_call(
        token_kernel,
        out_shape=(pltpu.HBM((2, WIDTH, P_SIZE), BF16),) * 2,
        in_specs=[pl.BlockSpec(memory_space=pltpu.SMEM)] + [hbm] * 3 + [vmem] * 3,
        out_specs=[hbm] * 2,
        scratch_shapes=[pltpu.VMEM((P_SIZE, WIDTH), BF16)] * 3
        + [pltpu.VMEM((2, WIDTH, P_SIZE), BF16)] * 2
        + [pltpu.SemaphoreType.DMA((3,)), pltpu.SemaphoreType.DMA((4,))],
        cost_estimate=pl.CostEstimate(flops=1, bytes_accessed=1, transcendentals=0),
        compiler_params=pltpu.CompilerParams(vmem_limit_bytes=VMEM_BYTES),
    )(
        core.reshape(1),
        *[pltpu.with_memory_space_constraint(a, pltpu.HBM) for a in (dq, dk, dv)],
        wq, wk, wv,
    )


def regroup_kernel(in_ref, out_ref, held_ref):
    rows = REF_ROWS + HALF_ROWS
    for row in range(rows):
        at = NYZ * row
        part = in_ref[0, at : at + NYZ, :].astype(F32)
        for x in range(1, NX):
            part = part + in_ref[x, at : at + NYZ, :].astype(F32)
        for group in range(GROUPS):
            held_ref[group, pl.ds(row, NYZ, stride=rows), :] = part[
                :, LANES * group : LANES * (group + 1)
            ]
    for group in range(GROUPS):
        out_ref[:, LANES * group : LANES * (group + 1)] = held_ref[group].astype(BF16)


def regroup(parts):
    rows = REF_ROWS + HALF_ROWS
    return pl.pallas_call(
        regroup_kernel,
        out_shape=jax.ShapeDtypeStruct((NYZ * rows, 2 * WIDTH), BF16),
        scratch_shapes=[pltpu.VMEM((GROUPS, NYZ * rows, LANES), F32)],
        cost_estimate=pl.CostEstimate(
            flops=REGROUP_COST, bytes_accessed=REGROUP_COST, transcendentals=0
        ),
        compiler_params=pltpu.CompilerParams(vmem_limit_bytes=8 * 1024 * 1024),
    )(parts)


def finish_kernel(in_ref, grad_ref, key_ref, value_ref):
    total = in_ref[0].astype(F32)
    for j in range(1, NYZ):
        total = total + in_ref[j].astype(F32)
    key_ref[...] = total[:REF_ROWS, :WIDTH].astype(BF16)
    value_ref[...] = total[:REF_ROWS, WIDTH:].astype(BF16)
    low, tail = total[:, : 4 * LANES], total[:, 4 * LANES :]
    left = jnp.concatenate([low[:, : 2 * LANES], tail[:, :E]], axis=1)
    right = jnp.concatenate([low[:, 2 * LANES :], tail[:, E:]], axis=1)
    grad_ref[:HALF_ROWS, :] = left[REF_ROWS:]
    grad_ref[HALF_ROWS:, :] = right[REF_ROWS:]


def finish(parts):
    return pl.pallas_call(
        finish_kernel,
        out_shape=(
            jax.ShapeDtypeStruct((ROWS_OUT, WIDTH), F32),
            jax.ShapeDtypeStruct((REF_ROWS, WIDTH), BF16),
            jax.ShapeDtypeStruct((REF_ROWS, WIDTH), BF16),
        ),
        compiler_params=pltpu.CompilerParams(vmem_limit_bytes=8 * 1024 * 1024),
    )(parts)


def per_device(
    tokens, reference_image, query_weight, key_weight, value_weight, ref_weight, cotangent
):
    core, half = lax.axis_index("c"), lax.axis_index("h")
    swap = [(0, 1), (1, 0)]
    wq, wk, wv = query_weight.T, key_weight.T, value_weight.T
    start_col = (2 * half + core) * WIDTH
    source_cols = lax.dynamic_slice_in_dim(reference_image, start_col, WIDTH, 1)
    ref_cols = (source_cols.astype(F32) + dot(reference_image, ref_weight, 1, 0)).astype(BF16)
    ref_block = jnp.pad(ref_cols, ((0, 16 - REF_ROWS), (0, P_SIZE - WIDTH)))
    gathered = lax.all_gather(
        jnp.concatenate([tokens.T, ref_block], axis=0), TENSOR, axis=0, tiled=False
    )
    pair = ref_pair(gathered, wk, wv)
    pair = lax.all_to_all(pair, ("y", "z"), 0, 0, tiled=True).reshape(1, NYZ * 16, LANES)
    pair = lax.all_to_all(jnp.broadcast_to(pair, (NX, NYZ * 16, LANES)), "x", 0, 0, tiled=True)
    tok, queries, keys, values = project(gathered, wq, wk, wv)
    attended, query_grads, key_grads, value_grads, pack = attention(
        queries, keys, values, pair.reshape(NX * NYZ * 16, LANES), cotangent.T, tok
    )
    pack = lax.all_to_all(pack, "x", 0, 0, tiled=True)
    kept, sent = token_parts(core, query_grads, key_grads, value_grads, wq, wk, wv)
    got = lax.ppermute(sent, "c", swap)
    paired = (kept.astype(F32) + got.astype(F32)).astype(BF16)
    kept = lax.dynamic_index_in_dim(paired, half, 0, False)
    sent = lax.dynamic_index_in_dim(paired, 1 - half, 0, False)
    got = lax.ppermute(sent, "h", swap)
    token_grads = (kept.astype(F32) + got.astype(F32)).astype(BF16).T
    pack = regroup(pack)
    pack, _ = lax.optimization_barrier((pack, got))
    pack = pack.reshape(NYZ, REF_ROWS + HALF_ROWS, 2 * WIDTH)
    pack = lax.all_to_all(pack, ("y", "z"), 0, 0, tiled=True)
    query_weight_grad, ref_key_grads, ref_value_grads = finish(pack)
    return attended.T, token_grads, query_weight_grad, ref_key_grads, ref_value_grads


def solution(mesh):
    mesh = Mesh(mesh.devices.reshape(4, 8, 4, 2, 2), FRAMES + TENSOR)
    return jax.shard_map(
        per_device,
        mesh=mesh,
        in_specs=(
            P(FRAMES, TENSOR),
            P(FRAMES, None),
            P(None, TENSOR),
            P(None, TENSOR),
            P(None, TENSOR),
            P(None, TENSOR),
            P(FRAMES, TENSOR),
        ),
        out_specs=(P(FRAMES, TENSOR),) * 5,
        check_vma=False,
    )
```

```python
import math

import jax
import jax.numpy as jnp
from jax import lax
from jax.experimental import pallas as pl
from jax.experimental.pallas import tpu as pltpu
from jax.sharding import Mesh
from jax.sharding import PartitionSpec as P

E = 64
P_SIZE = 384
HEADS = 5
WIDTH = HEADS * E
FRAMES = ("x", "y", "z")
TENSOR = ("h", "c")
NX, NYZ = 4, 32
REF_ROWS = 3
ROWS_OUT = 10
HALF_ROWS = ROWS_OUT // 2
LANES = 128
LONG = pl.CostEstimate(flops=10**10, bytes_accessed=10**10, transcendentals=0)
VMEM_BYTES = 24 * 1024 * 1024
GROUPS = 2 * WIDTH // LANES
SCALE = 1.0 / math.sqrt(E)
F32 = jnp.float32
BF16 = jnp.bfloat16


def dot(a, b, a_dim, b_dim):
    return lax.dot_general(a, b, (((a_dim,), (b_dim,)), ((), ())), preferred_element_type=F32)


def project_kernel(
    half_ref, t_ref, wq_ref, wk_ref, wv_ref, tok_out, q_out, k_out, v_out,
    tok_ref, q_ref, k_ref, v_ref, sem,
):
    half = half_ref[0]
    pairs = ((tok_ref, tok_out), (q_ref, q_out), (k_ref, k_out), (v_ref, v_out))
    copies = [pltpu.make_async_copy(a, b, sem.at[i]) for i, (a, b) in enumerate(pairs)]
    for core in range(2):
        for slot in range(2):
            at = pl.multiple_of((2 * lax.rem(half + slot, 2) + core) * WIDTH, E)
            tok_ref[pl.ds(at, WIDTH), :] = t_ref[core, slot]
    copies[0].start()
    tok = tok_ref[...]
    for i, (w_ref, out_ref) in enumerate(((wq_ref, q_ref), (wk_ref, k_ref), (wv_ref, v_ref))):
        out_ref[...] = dot(w_ref[...], tok, 1, 0).T.astype(BF16)
        copies[i + 1].start()
    for copy in copies:
        copy.wait()


def project(half, parts, wq, wk, wv):
    vmem = pl.BlockSpec(memory_space=pltpu.VMEM)
    return pl.pallas_call(
        project_kernel,
        out_shape=(pltpu.HBM((4 * WIDTH, P_SIZE), BF16),)
        + (pltpu.HBM((P_SIZE, WIDTH), BF16),) * 3,
        in_specs=[pl.BlockSpec(memory_space=pltpu.SMEM)] + [vmem] * 4,
        out_specs=[pl.BlockSpec(memory_space=pltpu.HBM)] * 4,
        scratch_shapes=[pltpu.VMEM((4 * WIDTH, P_SIZE), BF16)]
        + [pltpu.VMEM((P_SIZE, WIDTH), BF16)] * 3
        + [pltpu.SemaphoreType.DMA((4,))],
        cost_estimate=LONG,
        compiler_params=pltpu.CompilerParams(vmem_limit_bytes=VMEM_BYTES),
    )(half.reshape(1), parts, wq, wk, wv)


def ref_kernel(g_ref, wk_ref, wv_ref, out_ref, rows_ref):
    hidden = [g_ref[t].astype(F32) for t in range(4)]
    hidden = jnp.concatenate(hidden, axis=1).astype(BF16)
    pair = jnp.concatenate([dot(hidden, wk_ref[...], 1, 1), dot(hidden, wv_ref[...], 1, 1)], axis=1)
    rows_ref[...] = jnp.zeros_like(rows_ref)
    for row in range(REF_ROWS):
        for group in range(GROUPS):
            at = row * GROUPS + group
            rows_ref[at : at + 1, :] = pair[row : row + 1, LANES * group : LANES * (group + 1)]
    out_ref[...] = jnp.broadcast_to(rows_ref[...].astype(BF16)[None], out_ref.shape)


def ref_pair(gathered, wk, wv):
    return pl.pallas_call(
        ref_kernel,
        out_shape=jax.ShapeDtypeStruct((NX * NYZ, 16, LANES), BF16),
        scratch_shapes=[pltpu.VMEM((16, LANES), F32)],
        cost_estimate=LONG,
        compiler_params=pltpu.CompilerParams(vmem_limit_bytes=12 * 1024 * 1024),
    )(gathered, wk, wv)


def attention_kernel(
    q_in, k_in, v_in, tok_in, pair_ref, gt_ref, ot_out, dq_out, dk_out, dv_out, pack_out,
    q_ref, k_ref, v_ref, tok_ref, wide_ref, r_ref, dqt_ref, dw_ref,
    ot_ref, dq_ref, dk_ref, dv_ref, pack_ref, in_sem, out_sem,
):
    n_frames = NX * NYZ
    pairs = ((k_in, k_ref), (q_in, q_ref), (v_in, v_ref), (tok_in, tok_ref))
    loads = [pltpu.make_async_copy(a, b, in_sem.at[i]) for i, (a, b) in enumerate(pairs)]
    for load in loads:
        load.start()
    wide_ref[...] = pair_ref[...].astype(F32)
    for row in range(REF_ROWS):
        for group in range(GROUPS):
            r_ref[n_frames * row : n_frames * (row + 1), LANES * group : LANES * (group + 1)] = (
                wide_ref[pl.ds(row * GROUPS + group, n_frames, stride=16), :].astype(BF16)
            )
    g_all = gt_ref[...].astype(F32).T.astype(BF16)
    for load in loads[:3]:
        load.wait()
    for head in range(HEADS):
        lo, hi = head * E, head * E + E
        q, g = q_ref[:, lo:hi], g_all[:, lo:hi]
        k = jnp.concatenate([k_ref[:, lo:hi], r_ref[:, lo:hi]], 0)
        v = jnp.concatenate([v_ref[:, lo:hi], r_ref[:, WIDTH + lo : WIDTH + hi]], 0)
        s = dot(k, q, 1, 1)
        s = jnp.exp2((s - jnp.max(s, axis=0, keepdims=True)) * (SCALE * math.log2(math.e)))
        p = s * (1.0 / jnp.sum(s, axis=0, keepdims=True))
        p_low = p.astype(BF16)
        ot_ref[lo:hi, :] = dot(v, p_low, 0, 0).astype(BF16)
        dp = dot(v, gt_ref[lo:hi, :], 1, 0)
        ds = (p * (dp - jnp.sum(p * dp, axis=0, keepdims=True))).astype(BF16)
        dqt_ref[lo:hi, :] = dot(k, ds, 0, 0) * SCALE
        dk = dot(ds, q, 1, 0) * SCALE
        dv = dot(p_low, g, 1, 0)
        dk_ref[:, lo:hi] = dk[:P_SIZE].astype(BF16)
        dv_ref[:, lo:hi] = dv[:P_SIZE].astype(BF16)
        for col, part in ((lo, dk), (WIDTH + lo, dv)):
            for x in range(NX):
                for row in range(REF_ROWS):
                    at = P_SIZE + n_frames * row + NYZ * x
                    pack_ref[x, NYZ * row : NYZ * (row + 1), col : col + E] = part[
                        at : at + NYZ
                    ].astype(BF16)
    dq = dqt_ref[...].T.astype(BF16)
    dq_ref[...] = dq
    loads[3].wait()
    pairs = ((ot_ref, ot_out), (dq_ref, dq_out), (dk_ref, dk_out), (dv_ref, dv_out))
    stores = [pltpu.make_async_copy(a, b, out_sem.at[NX + i]) for i, (a, b) in enumerate(pairs)]
    for store in stores:
        store.start()
    for x in range(NX):
        dw = dot(tok_ref[x * WIDTH : (x + 1) * WIDTH, :], dq, 1, 0)
        dw_ref[0], dw_ref[1] = dw[:, :LANES], dw[:, LANES : 2 * LANES]
        dw_ref[2, :, :E] = dw[:, 2 * LANES :]
        for row in range(HALF_ROWS):
            at = NYZ * (REF_ROWS + row)
            left, right = [
                [dw_ref[group, pl.ds(first, NYZ, stride=ROWS_OUT), :] for group in range(3)]
                for first in (row, row + HALF_ROWS)
            ]
            last = jnp.concatenate([left[2][:, :E], right[2][:, :E]], axis=1)
            for group, part in enumerate((left[0], left[1], right[0], right[1], last)):
                pack_ref[x, at : at + NYZ, LANES * group : LANES * (group + 1)] = part.astype(BF16)
        stores.append(pltpu.make_async_copy(pack_ref.at[x], pack_out.at[x], out_sem.at[x]))
        stores[-1].start()
    for store in stores:
        store.wait()


def attention(q, k, v, pair, gt, tok):
    hbm, vmem = [pl.BlockSpec(memory_space=space) for space in (pltpu.HBM, pltpu.VMEM)]
    rows = REF_ROWS + HALF_ROWS
    return pl.pallas_call(
        attention_kernel,
        out_shape=(pltpu.HBM((WIDTH, P_SIZE), BF16),)
        + (pltpu.HBM((P_SIZE, WIDTH), BF16),) * 3
        + (pltpu.HBM((NX, NYZ * rows, 2 * WIDTH), BF16),),
        in_specs=[hbm] * 4 + [vmem] * 2,
        out_specs=[hbm] * 5,
        scratch_shapes=[pltpu.VMEM((P_SIZE, WIDTH), BF16)] * 3
        + [
            pltpu.VMEM((4 * WIDTH, P_SIZE), BF16),
            pltpu.VMEM((NX * NYZ * 16, LANES), F32),
            pltpu.VMEM((P_SIZE, 2 * WIDTH), BF16),
            pltpu.VMEM((WIDTH, P_SIZE), F32),
            pltpu.VMEM((3, WIDTH, LANES), F32),
            pltpu.VMEM((WIDTH, P_SIZE), BF16),
            pltpu.VMEM((P_SIZE, WIDTH), BF16),
            pltpu.VMEM((P_SIZE, WIDTH), BF16),
            pltpu.VMEM((P_SIZE, WIDTH), BF16),
            pltpu.VMEM((NX, NYZ * rows, 2 * WIDTH), BF16),
            pltpu.SemaphoreType.DMA((4,)),
            pltpu.SemaphoreType.DMA((NX + 4,)),
        ],
        compiler_params=pltpu.CompilerParams(vmem_limit_bytes=VMEM_BYTES),
    )(*[pltpu.with_memory_space_constraint(a, pltpu.HBM) for a in (q, k, v, tok)], pair, gt)


def token_kernel(
    core_ref, dq_in, dk_in, dv_in, wq_ref, wk_ref, wv_ref, kept_out, sent_out,
    dq_ref, dk_ref, dv_ref, kept_ref, sent_ref, in_sem, out_sem,
):
    pairs = ((dq_in, dq_ref), (dk_in, dk_ref), (dv_in, dv_ref))
    loads = [pltpu.make_async_copy(a, b, in_sem.at[i]) for i, (a, b) in enumerate(pairs)]
    for load in loads:
        load.start()
    core = core_ref[0]
    total = None
    for load, (d_ref, w_ref) in zip(
        loads, ((dq_ref, wq_ref), (dk_ref, wk_ref), (dv_ref, wv_ref))
    ):
        load.wait()
        part = dot(d_ref[...], w_ref[...], 1, 0)
        total = part if total is None else total + part
    total = total.T.astype(BF16)
    stores = []
    for half in range(2):
        zero, one = [total[(2 * half + c) * WIDTH : (2 * half + c + 1) * WIDTH] for c in range(2)]
        sent_ref[half] = jnp.where(core == 0, one, zero)
        kept_ref[half] = jnp.where(core == 0, zero, one)
        for i, (a, b) in enumerate(((sent_ref, sent_out), (kept_ref, kept_out))):
            store = pltpu.make_async_copy(a.at[half], b.at[half], out_sem.at[2 * half + i])
            store.start()
            stores.append(store)
    for store in stores:
        store.wait()


def token_parts(core, dq, dk, dv, wq, wk, wv):
    hbm, vmem = [pl.BlockSpec(memory_space=space) for space in (pltpu.HBM, pltpu.VMEM)]
    return pl.pallas_call(
        token_kernel,
        out_shape=(pltpu.HBM((2, WIDTH, P_SIZE), BF16),) * 2,
        in_specs=[pl.BlockSpec(memory_space=pltpu.SMEM)] + [hbm] * 3 + [vmem] * 3,
        out_specs=[hbm] * 2,
        scratch_shapes=[pltpu.VMEM((P_SIZE, WIDTH), BF16)] * 3
        + [pltpu.VMEM((2, WIDTH, P_SIZE), BF16)] * 2
        + [pltpu.SemaphoreType.DMA((3,)), pltpu.SemaphoreType.DMA((4,))],
        cost_estimate=pl.CostEstimate(flops=1, bytes_accessed=1, transcendentals=0),
        compiler_params=pltpu.CompilerParams(vmem_limit_bytes=VMEM_BYTES),
    )(
        core.reshape(1),
        *[pltpu.with_memory_space_constraint(a, pltpu.HBM) for a in (dq, dk, dv)],
        wq, wk, wv,
    )


def combine_kernel(half_ref, pair_ref, got_ref, out_ref):
    mine = jnp.where(half_ref[0] == 0, pair_ref[0].astype(F32), pair_ref[1].astype(F32))
    out_ref[...] = (mine + got_ref[...].astype(F32)).astype(BF16)


def combine(half, paired, got):
    vmem = pl.BlockSpec(memory_space=pltpu.VMEM)
    return pl.pallas_call(
        combine_kernel,
        out_shape=jax.ShapeDtypeStruct((WIDTH, P_SIZE), BF16),
        in_specs=[pl.BlockSpec(memory_space=pltpu.SMEM)] + [vmem] * 2,
        out_specs=vmem,
        cost_estimate=LONG,
        compiler_params=pltpu.CompilerParams(vmem_limit_bytes=8 * 1024 * 1024),
    )(half.reshape(1), paired, got)


def regroup_kernel(in_ref, out_ref, held_ref):
    rows = REF_ROWS + HALF_ROWS
    for row in range(rows):
        at = NYZ * row
        part = in_ref[0, at : at + NYZ, :].astype(F32)
        for x in range(1, NX):
            part = part + in_ref[x, at : at + NYZ, :].astype(F32)
        for group in range(GROUPS):
            held_ref[group, pl.ds(row, NYZ, stride=rows), :] = part[
                :, LANES * group : LANES * (group + 1)
            ]
    for group in range(GROUPS):
        out_ref[:, LANES * group : LANES * (group + 1)] = held_ref[group].astype(BF16)


def regroup(parts):
    rows = REF_ROWS + HALF_ROWS
    return pl.pallas_call(
        regroup_kernel,
        out_shape=jax.ShapeDtypeStruct((NYZ * rows, 2 * WIDTH), BF16),
        scratch_shapes=[pltpu.VMEM((GROUPS, NYZ * rows, LANES), F32)],
        cost_estimate=LONG,
        compiler_params=pltpu.CompilerParams(vmem_limit_bytes=8 * 1024 * 1024),
    )(parts)


def finish_kernel(in_ref, grad_ref, key_ref, value_ref):
    total = in_ref[0].astype(F32)
    for j in range(1, NYZ):
        total = total + in_ref[j].astype(F32)
    key_ref[...] = total[:REF_ROWS, :WIDTH].astype(BF16)
    value_ref[...] = total[:REF_ROWS, WIDTH:].astype(BF16)
    low, tail = total[:, : 4 * LANES], total[:, 4 * LANES :]
    left = jnp.concatenate([low[:, : 2 * LANES], tail[:, :E]], axis=1)
    right = jnp.concatenate([low[:, 2 * LANES :], tail[:, E:]], axis=1)
    grad_ref[:HALF_ROWS, :] = left[REF_ROWS:]
    grad_ref[HALF_ROWS:, :] = right[REF_ROWS:]


def finish(parts):
    return pl.pallas_call(
        finish_kernel,
        out_shape=(
            jax.ShapeDtypeStruct((ROWS_OUT, WIDTH), F32),
            jax.ShapeDtypeStruct((REF_ROWS, WIDTH), BF16),
            jax.ShapeDtypeStruct((REF_ROWS, WIDTH), BF16),
        ),
        compiler_params=pltpu.CompilerParams(vmem_limit_bytes=8 * 1024 * 1024),
    )(parts)


def per_device(
    tokens, reference_image, query_weight, key_weight, value_weight, ref_weight, cotangent
):
    core, half = lax.axis_index("c"), lax.axis_index("h")
    swap = [(0, 1), (1, 0)]
    wq, wk, wv = query_weight.T, key_weight.T, value_weight.T
    start_col = (2 * half + core) * WIDTH
    source_cols = lax.dynamic_slice_in_dim(reference_image, start_col, WIDTH, 1)
    ref_cols = (source_cols.astype(F32) + dot(reference_image, ref_weight, 1, 0)).astype(BF16)
    ref_cols = jnp.pad(ref_cols, ((0, 16 - REF_ROWS), (0, 0)))
    ref_hidden = lax.all_gather(ref_cols, TENSOR, axis=0, tiled=False)
    ref_hidden, own = lax.optimization_barrier((ref_hidden, tokens.T))
    other = lax.ppermute(own, "h", swap)
    pair = ref_pair(ref_hidden, wk, wv)
    pair = lax.all_to_all(pair, FRAMES, 0, 0, tiled=True)
    parts = lax.all_gather(jnp.stack([own, other]), "c", axis=0, tiled=False)
    tok, queries, keys, values = project(half, parts, wq, wk, wv)
    attended, query_grads, key_grads, value_grads, pack = attention(
        queries, keys, values, pair.reshape(NX * NYZ * 16, LANES), cotangent.T, tok
    )
    pack = lax.all_to_all(pack, "x", 0, 0, tiled=True)
    kept, sent = token_parts(core, query_grads, key_grads, value_grads, wq, wk, wv)
    got = lax.ppermute(sent, "c", swap)
    paired = (kept.astype(F32) + got.astype(F32)).astype(BF16)
    sent = lax.dynamic_index_in_dim(paired, 1 - half, 0, False)
    got = lax.ppermute(sent, "h", swap)
    token_grads = combine(half, paired, got).T
    pack = regroup(pack)
    pack = pack.reshape(NYZ, REF_ROWS + HALF_ROWS, 2 * WIDTH)
    pack = lax.all_to_all(pack, ("y", "z"), 0, 0, tiled=True)
    query_weight_grad, ref_key_grads, ref_value_grads = finish(pack)
    return attended.T, token_grads, query_weight_grad, ref_key_grads, ref_value_grads


def solution(mesh):
    mesh = Mesh(mesh.devices.reshape(4, 8, 4, 2, 2), FRAMES + TENSOR)
    return jax.shard_map(
        per_device,
        mesh=mesh,
        in_specs=(
            P(FRAMES, TENSOR),
            P(FRAMES, None),
            P(None, TENSOR),
            P(None, TENSOR),
            P(None, TENSOR),
            P(None, TENSOR),
            P(FRAMES, TENSOR),
        ),
        out_specs=(P(FRAMES, TENSOR),) * 5,
        check_vma=False,
    )
```

```python
import math

import jax
import jax.numpy as jnp
from jax import lax
from jax.experimental import pallas as pl
from jax.experimental.pallas import tpu as pltpu
from jax.sharding import Mesh
from jax.sharding import PartitionSpec as P

E = 64
P_SIZE = 384
HEADS = 5
WIDTH = HEADS * E
FRAMES = ("x", "y", "z")
TENSOR = ("h", "c")
NX, NYZ = 4, 32
REF_ROWS = 3
ROWS_OUT = 10
HALF_ROWS = ROWS_OUT // 2
LANES = 128
LONG = pl.CostEstimate(flops=10**10, bytes_accessed=10**10, transcendentals=0)
VMEM_BYTES = 24 * 1024 * 1024
GROUPS = 2 * WIDTH // LANES
SCALE = 1.0 / math.sqrt(E)
F32 = jnp.float32
BF16 = jnp.bfloat16


def dot(a, b, a_dim, b_dim):
    return lax.dot_general(a, b, (((a_dim,), (b_dim,)), ((), ())), preferred_element_type=F32)


def project_kernel(
    half_ref, t_ref, wq_ref, wk_ref, wv_ref, tok_out, q_out, k_out, v_out,
    tok_ref, q_ref, k_ref, v_ref, sem,
):
    half = half_ref[0]
    pairs = ((tok_ref, tok_out), (q_ref, q_out), (k_ref, k_out), (v_ref, v_out))
    copies = [pltpu.make_async_copy(a, b, sem.at[i]) for i, (a, b) in enumerate(pairs)]
    for core in range(2):
        for slot in range(2):
            at = pl.multiple_of((2 * lax.rem(half + slot, 2) + core) * WIDTH, E)
            tok_ref[pl.ds(at, WIDTH), :] = t_ref[core, slot]
    copies[0].start()
    tok = tok_ref[...]
    for i, (w_ref, out_ref) in enumerate(((wq_ref, q_ref), (wk_ref, k_ref), (wv_ref, v_ref))):
        out_ref[...] = dot(w_ref[...], tok, 1, 0).T.astype(BF16)
        copies[i + 1].start()
    for copy in copies:
        copy.wait()


def project(half, parts, wq, wk, wv):
    vmem = pl.BlockSpec(memory_space=pltpu.VMEM)
    return pl.pallas_call(
        project_kernel,
        out_shape=(pltpu.HBM((4 * WIDTH, P_SIZE), BF16),)
        + (pltpu.HBM((P_SIZE, WIDTH), BF16),) * 3,
        in_specs=[pl.BlockSpec(memory_space=pltpu.SMEM)] + [vmem] * 4,
        out_specs=[pl.BlockSpec(memory_space=pltpu.HBM)] * 4,
        scratch_shapes=[pltpu.VMEM((4 * WIDTH, P_SIZE), BF16)]
        + [pltpu.VMEM((P_SIZE, WIDTH), BF16)] * 3
        + [pltpu.SemaphoreType.DMA((4,))],
        cost_estimate=LONG,
        compiler_params=pltpu.CompilerParams(vmem_limit_bytes=VMEM_BYTES),
    )(half.reshape(1), parts, wq, wk, wv)


def cols_kernel(at_ref, r_ref, w_in, out_ref, w_ref, sem):
    load = pltpu.make_async_copy(w_in, w_ref, sem.at[0])
    load.start()
    image = r_ref[...]
    mine = image[:, :WIDTH]
    for t in range(1, 4):
        mine = jnp.where(at_ref[0] == t, image[:, t * WIDTH : (t + 1) * WIDTH], mine)
    load.wait()
    cols = mine.astype(F32) + dot(image, w_ref[...], 1, 1)
    out_ref[...] = jnp.zeros_like(out_ref)
    out_ref[:REF_ROWS, :] = cols.astype(BF16)


def ref_cols(at, image, wr):
    vmem = pl.BlockSpec(memory_space=pltpu.VMEM)
    return pl.pallas_call(
        cols_kernel,
        out_shape=jax.ShapeDtypeStruct((16, WIDTH), BF16),
        in_specs=[
            pl.BlockSpec(memory_space=pltpu.SMEM), vmem, pl.BlockSpec(memory_space=pltpu.HBM)
        ],
        out_specs=vmem,
        scratch_shapes=[
            pltpu.VMEM((WIDTH, 4 * WIDTH), BF16),
            pltpu.SemaphoreType.DMA((1,)),
        ],
        compiler_params=pltpu.CompilerParams(vmem_limit_bytes=8 * 1024 * 1024),
    )(at.reshape(1), image, pltpu.with_memory_space_constraint(wr, pltpu.HBM))


def ref_kernel(g_ref, wk_in, wv_in, out_ref, rows_ref, wk_ref, wv_ref, sem):
    loads = [
        pltpu.make_async_copy(a, b, sem.at[i])
        for i, (a, b) in enumerate(((wk_in, wk_ref), (wv_in, wv_ref)))
    ]
    for load in loads:
        load.start()
    hidden = [g_ref[t].astype(F32) for t in range(4)]
    hidden = jnp.concatenate(hidden, axis=1).astype(BF16)
    rows_ref[...] = jnp.zeros_like(rows_ref)
    pair = []
    for load, w_ref in zip(loads, (wk_ref, wv_ref)):
        load.wait()
        pair.append(dot(hidden, w_ref[...], 1, 1))
    pair = jnp.concatenate(pair, axis=1)
    for row in range(REF_ROWS):
        for group in range(GROUPS):
            at = row * GROUPS + group
            rows_ref[at : at + 1, :] = pair[row : row + 1, LANES * group : LANES * (group + 1)]
    out_ref[...] = jnp.broadcast_to(rows_ref[...].astype(BF16)[None], out_ref.shape)


def ref_pair(gathered, wk, wv):
    hbm, vmem = [pl.BlockSpec(memory_space=space) for space in (pltpu.HBM, pltpu.VMEM)]
    return pl.pallas_call(
        ref_kernel,
        out_shape=jax.ShapeDtypeStruct((NX * NYZ, 16, LANES), BF16),
        in_specs=[vmem, hbm, hbm],
        out_specs=vmem,
        scratch_shapes=[pltpu.VMEM((16, LANES), F32)]
        + [pltpu.VMEM((WIDTH, 4 * WIDTH), BF16)] * 2
        + [pltpu.SemaphoreType.DMA((2,))],
        cost_estimate=LONG,
        compiler_params=pltpu.CompilerParams(vmem_limit_bytes=12 * 1024 * 1024),
    )(gathered, *[pltpu.with_memory_space_constraint(a, pltpu.HBM) for a in (wk, wv)])


def attention_kernel(
    q_in, k_in, v_in, tok_in, pair_ref, gt_ref, ot_out, dq_out, dk_out, dv_out, pack_out,
    q_ref, k_ref, v_ref, tok_ref, wide_ref, r_ref, dqt_ref, dw_ref,
    ot_ref, dq_ref, dk_ref, dv_ref, pack_ref, in_sem, out_sem,
):
    n_frames = NX * NYZ
    pairs = ((k_in, k_ref), (q_in, q_ref), (v_in, v_ref), (tok_in, tok_ref))
    loads = [pltpu.make_async_copy(a, b, in_sem.at[i]) for i, (a, b) in enumerate(pairs)]
    for load in loads:
        load.start()
    wide_ref[...] = pair_ref[...].astype(F32)
    for row in range(REF_ROWS):
        for group in range(GROUPS):
            r_ref[n_frames * row : n_frames * (row + 1), LANES * group : LANES * (group + 1)] = (
                wide_ref[pl.ds(row * GROUPS + group, n_frames, stride=16), :].astype(BF16)
            )
    g_all = gt_ref[...].astype(F32).T.astype(BF16)
    for load in loads[:3]:
        load.wait()
    def scores(head):
        lo, hi = head * E, head * E + E
        q = q_ref[:, lo:hi]
        k = jnp.concatenate([k_ref[:, lo:hi], r_ref[:, lo:hi]], 0)
        v = jnp.concatenate([v_ref[:, lo:hi], r_ref[:, WIDTH + lo : WIDTH + hi]], 0)
        return k, v, q, dot(k, q, 1, 1), dot(v, gt_ref[lo:hi, :], 1, 0)

    def soften(k, v, q, s, dp):
        e = jnp.exp2((s - jnp.max(s, axis=0, keepdims=True)) * (SCALE * math.log2(math.e)))
        inv = 1.0 / jnp.sum(e, axis=0, keepdims=True)
        mean = jnp.sum(e * dp, axis=0, keepdims=True) * inv
        p = e * inv
        return k, v, q, p.astype(BF16), (p * (dp - mean)).astype(BF16)

    def write(head, k, v, q, p_low, ds):
        lo, hi = head * E, head * E + E
        ot_ref[lo:hi, :] = dot(v, p_low, 0, 0).astype(BF16)
        dqt_ref[lo:hi, :] = dot(k, ds, 0, 0) * SCALE
        dk = dot(ds, q, 1, 0) * SCALE
        dv = dot(p_low, g_all[:, lo:hi], 1, 0)
        dk_ref[:, lo:hi] = dk[:P_SIZE].astype(BF16)
        dv_ref[:, lo:hi] = dv[:P_SIZE].astype(BF16)
        for col, part in ((lo, dk), (WIDTH + lo, dv)):
            for x in range(NX):
                for row in range(REF_ROWS):
                    at = P_SIZE + n_frames * row + NYZ * x
                    pack_ref[x, NYZ * row : NYZ * (row + 1), col : col + E] = part[
                        at : at + NYZ
                    ].astype(BF16)

    ahead = scores(0)
    for head in range(HEADS):
        now = ahead
        if head + 1 < HEADS:
            ahead = scores(head + 1)
        write(head, *soften(*now))
    dq = dqt_ref[...].T.astype(BF16)
    dq_ref[...] = dq
    loads[3].wait()
    pairs = ((ot_ref, ot_out), (dq_ref, dq_out), (dk_ref, dk_out), (dv_ref, dv_out))
    stores = [pltpu.make_async_copy(a, b, out_sem.at[NX + i]) for i, (a, b) in enumerate(pairs)]
    for store in stores:
        store.start()
    for x in range(NX):
        dw = dot(tok_ref[x * WIDTH : (x + 1) * WIDTH, :], dq, 1, 0)
        dw_ref[0], dw_ref[1] = dw[:, :LANES], dw[:, LANES : 2 * LANES]
        dw_ref[2, :, :E] = dw[:, 2 * LANES :]
        for row in range(HALF_ROWS):
            at = NYZ * (REF_ROWS + row)
            left, right = [
                [dw_ref[group, pl.ds(first, NYZ, stride=ROWS_OUT), :] for group in range(3)]
                for first in (row, row + HALF_ROWS)
            ]
            last = jnp.concatenate([left[2][:, :E], right[2][:, :E]], axis=1)
            for group, part in enumerate((left[0], left[1], right[0], right[1], last)):
                pack_ref[x, at : at + NYZ, LANES * group : LANES * (group + 1)] = part.astype(BF16)
        stores.append(pltpu.make_async_copy(pack_ref.at[x], pack_out.at[x], out_sem.at[x]))
        stores[-1].start()
    for store in stores:
        store.wait()


def attention(q, k, v, pair, gt, tok):
    hbm, vmem = [pl.BlockSpec(memory_space=space) for space in (pltpu.HBM, pltpu.VMEM)]
    rows = REF_ROWS + HALF_ROWS
    return pl.pallas_call(
        attention_kernel,
        out_shape=(pltpu.HBM((WIDTH, P_SIZE), BF16),)
        + (pltpu.HBM((P_SIZE, WIDTH), BF16),) * 3
        + (pltpu.HBM((NX, NYZ * rows, 2 * WIDTH), BF16),),
        in_specs=[hbm] * 4 + [vmem] * 2,
        out_specs=[hbm] * 5,
        scratch_shapes=[pltpu.VMEM((P_SIZE, WIDTH), BF16)] * 3
        + [
            pltpu.VMEM((4 * WIDTH, P_SIZE), BF16),
            pltpu.VMEM((NX * NYZ * 16, LANES), F32),
            pltpu.VMEM((P_SIZE, 2 * WIDTH), BF16),
            pltpu.VMEM((WIDTH, P_SIZE), F32),
            pltpu.VMEM((3, WIDTH, LANES), F32),
            pltpu.VMEM((WIDTH, P_SIZE), BF16),
            pltpu.VMEM((P_SIZE, WIDTH), BF16),
            pltpu.VMEM((P_SIZE, WIDTH), BF16),
            pltpu.VMEM((P_SIZE, WIDTH), BF16),
            pltpu.VMEM((NX, NYZ * rows, 2 * WIDTH), BF16),
            pltpu.SemaphoreType.DMA((4,)),
            pltpu.SemaphoreType.DMA((NX + 4,)),
        ],
        compiler_params=pltpu.CompilerParams(vmem_limit_bytes=VMEM_BYTES),
    )(*[pltpu.with_memory_space_constraint(a, pltpu.HBM) for a in (q, k, v, tok)], pair, gt)


def token_kernel(
    core_ref, dq_in, dk_in, dv_in, wq_in, wk_in, wv_in, kept_out, sent_out,
    dq_ref, dk_ref, dv_ref, wq_ref, wk_ref, wv_ref, kept_ref, sent_ref, in_sem, out_sem,
):
    pairs = (
        (wq_in, wq_ref), (dq_in, dq_ref), (wk_in, wk_ref),
        (dk_in, dk_ref), (wv_in, wv_ref), (dv_in, dv_ref),
    )
    loads = [pltpu.make_async_copy(a, b, in_sem.at[i]) for i, (a, b) in enumerate(pairs)]
    for load in loads:
        load.start()
    core = core_ref[0]
    total = None
    for i, (d_ref, w_ref) in enumerate(((dq_ref, wq_ref), (dk_ref, wk_ref), (dv_ref, wv_ref))):
        loads[2 * i].wait()
        loads[2 * i + 1].wait()
        part = dot(d_ref[...], w_ref[...], 1, 0)
        total = part if total is None else total + part
    total = total.T.astype(BF16)
    stores = []
    for half in range(2):
        zero, one = [total[(2 * half + c) * WIDTH : (2 * half + c + 1) * WIDTH] for c in range(2)]
        sent_ref[half] = jnp.where(core == 0, one, zero)
        kept_ref[half] = jnp.where(core == 0, zero, one)
        for i, (a, b) in enumerate(((sent_ref, sent_out), (kept_ref, kept_out))):
            store = pltpu.make_async_copy(a.at[half], b.at[half], out_sem.at[2 * half + i])
            store.start()
            stores.append(store)
    for store in stores:
        store.wait()


def token_parts(core, dq, dk, dv, wq, wk, wv):
    hbm = pl.BlockSpec(memory_space=pltpu.HBM)
    return pl.pallas_call(
        token_kernel,
        out_shape=(pltpu.HBM((2, WIDTH, P_SIZE), BF16),) * 2,
        in_specs=[pl.BlockSpec(memory_space=pltpu.SMEM)] + [hbm] * 6,
        out_specs=[hbm] * 2,
        scratch_shapes=[pltpu.VMEM((P_SIZE, WIDTH), BF16)] * 3
        + [pltpu.VMEM((WIDTH, 4 * WIDTH), BF16)] * 3
        + [pltpu.VMEM((2, WIDTH, P_SIZE), BF16)] * 2
        + [pltpu.SemaphoreType.DMA((6,)), pltpu.SemaphoreType.DMA((4,))],
        cost_estimate=pl.CostEstimate(flops=1, bytes_accessed=1, transcendentals=0),
        compiler_params=pltpu.CompilerParams(vmem_limit_bytes=VMEM_BYTES),
    )(
        core.reshape(1),
        *[pltpu.with_memory_space_constraint(a, pltpu.HBM) for a in (dq, dk, dv, wq, wk, wv)],
    )


def combine_kernel(half_ref, pair_ref, got_ref, out_ref):
    mine = jnp.where(half_ref[0] == 0, pair_ref[0].astype(F32), pair_ref[1].astype(F32))
    out_ref[...] = (mine + got_ref[...].astype(F32)).astype(BF16)


def combine(half, paired, got):
    vmem = pl.BlockSpec(memory_space=pltpu.VMEM)
    return pl.pallas_call(
        combine_kernel,
        out_shape=jax.ShapeDtypeStruct((WIDTH, P_SIZE), BF16),
        in_specs=[pl.BlockSpec(memory_space=pltpu.SMEM)] + [vmem] * 2,
        out_specs=vmem,
        cost_estimate=LONG,
        compiler_params=pltpu.CompilerParams(vmem_limit_bytes=8 * 1024 * 1024),
    )(half.reshape(1), paired, got)


def regroup_kernel(in_ref, out_ref, held_ref):
    rows = REF_ROWS + HALF_ROWS
    for row in range(rows):
        at = NYZ * row
        part = in_ref[0, at : at + NYZ, :].astype(F32)
        for x in range(1, NX):
            part = part + in_ref[x, at : at + NYZ, :].astype(F32)
        for group in range(GROUPS):
            held_ref[group, pl.ds(row, NYZ, stride=rows), :] = part[
                :, LANES * group : LANES * (group + 1)
            ]
    for group in range(GROUPS):
        out_ref[:, LANES * group : LANES * (group + 1)] = held_ref[group].astype(BF16)


def regroup(parts):
    rows = REF_ROWS + HALF_ROWS
    return pl.pallas_call(
        regroup_kernel,
        out_shape=jax.ShapeDtypeStruct((NYZ * rows, 2 * WIDTH), BF16),
        scratch_shapes=[pltpu.VMEM((GROUPS, NYZ * rows, LANES), F32)],
        cost_estimate=LONG,
        compiler_params=pltpu.CompilerParams(vmem_limit_bytes=8 * 1024 * 1024),
    )(parts)


def finish_kernel(in_ref, grad_ref, key_ref, value_ref):
    total = in_ref[0].astype(F32)
    for j in range(1, NYZ):
        total = total + in_ref[j].astype(F32)
    key_ref[...] = total[:REF_ROWS, :WIDTH].astype(BF16)
    value_ref[...] = total[:REF_ROWS, WIDTH:].astype(BF16)
    low, tail = total[:, : 4 * LANES], total[:, 4 * LANES :]
    left = jnp.concatenate([low[:, : 2 * LANES], tail[:, :E]], axis=1)
    right = jnp.concatenate([low[:, 2 * LANES :], tail[:, E:]], axis=1)
    grad_ref[:HALF_ROWS, :] = left[REF_ROWS:]
    grad_ref[HALF_ROWS:, :] = right[REF_ROWS:]


def finish(parts):
    return pl.pallas_call(
        finish_kernel,
        out_shape=(
            jax.ShapeDtypeStruct((ROWS_OUT, WIDTH), F32),
            jax.ShapeDtypeStruct((REF_ROWS, WIDTH), BF16),
            jax.ShapeDtypeStruct((REF_ROWS, WIDTH), BF16),
        ),
        compiler_params=pltpu.CompilerParams(vmem_limit_bytes=8 * 1024 * 1024),
    )(parts)


def per_device(
    tokens, reference_image, query_weight, key_weight, value_weight, ref_weight, cotangent
):
    core, half = lax.axis_index("c"), lax.axis_index("h")
    swap = [(0, 1), (1, 0)]
    wq, wk, wv = query_weight.T, key_weight.T, value_weight.T
    cols = ref_cols(2 * half + core, reference_image, ref_weight.T)
    ref_hidden = lax.all_gather(cols, TENSOR, axis=0, tiled=False)
    ref_hidden, own = lax.optimization_barrier((ref_hidden, tokens.T))
    other = lax.ppermute(own, "h", swap)
    pair = ref_pair(ref_hidden, wk, wv)
    pair = lax.all_to_all(pair, FRAMES, 0, 0, tiled=True)
    parts = lax.all_gather(jnp.stack([own, other]), "c", axis=0, tiled=False)
    tok, queries, keys, values = project(half, parts, wq, wk, wv)
    attended, query_grads, key_grads, value_grads, pack = attention(
        queries, keys, values, pair.reshape(NX * NYZ * 16, LANES), cotangent.T, tok
    )
    pack = lax.all_to_all(pack, "x", 0, 0, tiled=True)
    kept, sent = token_parts(core, query_grads, key_grads, value_grads, wq, wk, wv)
    got = lax.ppermute(sent, "c", swap)
    paired = (kept.astype(F32) + got.astype(F32)).astype(BF16)
    sent = lax.dynamic_index_in_dim(paired, 1 - half, 0, False)
    got = lax.ppermute(sent, "h", swap)
    token_grads = combine(half, paired, got).T
    pack = regroup(pack)
    pack = pack.reshape(NYZ, REF_ROWS + HALF_ROWS, 2 * WIDTH)
    pack = lax.all_to_all(pack, ("y", "z"), 0, 0, tiled=True)
    query_weight_grad, ref_key_grads, ref_value_grads = finish(pack)
    return attended.T, token_grads, query_weight_grad, ref_key_grads, ref_value_grads


def solution(mesh):
    mesh = Mesh(mesh.devices.reshape(4, 8, 4, 2, 2), FRAMES + TENSOR)
    return jax.shard_map(
        per_device,
        mesh=mesh,
        in_specs=(
            P(FRAMES, TENSOR),
            P(FRAMES, None),
            P(None, TENSOR),
            P(None, TENSOR),
            P(None, TENSOR),
            P(None, TENSOR),
            P(FRAMES, TENSOR),
        ),
        out_specs=(P(FRAMES, TENSOR),) * 5,
        check_vma=False,
    )
```

```python
import math

import jax
import jax.numpy as jnp
from jax import lax
from jax.experimental import pallas as pl
from jax.experimental.pallas import tpu as pltpu
from jax.sharding import Mesh
from jax.sharding import PartitionSpec as P

E = 64
P_SIZE = 384
HEADS = 5
WIDTH = HEADS * E
FRAMES = ("x", "yh", "yl", "z")
FIRST = ("x", "yl")
SECOND = ("yh", "z")
TENSOR = ("h", "c")
N_FIRST, N_SECOND = 8, 16
N_FRAMES = N_FIRST * N_SECOND
REF_ROWS = 3
ROWS_OUT = 10
HALF_ROWS = ROWS_OUT // 2
LANES = 128
LONG = pl.CostEstimate(flops=10**10, bytes_accessed=10**10, transcendentals=0)
VMEM_BYTES = 24 * 1024 * 1024
GROUPS = 2 * WIDTH // LANES
SCALE = 1.0 / math.sqrt(E)
F32 = jnp.float32
BF16 = jnp.bfloat16


def pick(rows, low):
    return jnp.concatenate([rows[8 * i + 4 * low : 8 * i + 4 * low + 4] for i in range(4)], axis=0)


def dot(a, b, a_dim, b_dim):
    return lax.dot_general(a, b, (((a_dim,), (b_dim,)), ((), ())), preferred_element_type=F32)


def project_kernel(
    half_ref, t_ref, wq_ref, wk_ref, wv_ref, tok_out, q_out, k_out, v_out,
    tok_ref, q_ref, k_ref, v_ref, sem,
):
    half = half_ref[0]
    pairs = ((tok_ref, tok_out), (q_ref, q_out), (k_ref, k_out), (v_ref, v_out))
    copies = [pltpu.make_async_copy(a, b, sem.at[i]) for i, (a, b) in enumerate(pairs)]
    for core in range(2):
        for slot in range(2):
            at = pl.multiple_of((2 * lax.rem(half + slot, 2) + core) * WIDTH, E)
            tok_ref[pl.ds(at, WIDTH), :] = t_ref[core, slot]
    copies[0].start()
    tok = tok_ref[...]
    for i, (w_ref, out_ref) in enumerate(((wq_ref, q_ref), (wk_ref, k_ref), (wv_ref, v_ref))):
        out_ref[...] = dot(w_ref[...], tok, 1, 0).T.astype(BF16)
        copies[i + 1].start()
    for copy in copies:
        copy.wait()


def project(half, parts, wq, wk, wv):
    vmem = pl.BlockSpec(memory_space=pltpu.VMEM)
    return pl.pallas_call(
        project_kernel,
        out_shape=(pltpu.HBM((4 * WIDTH, P_SIZE), BF16),)
        + (pltpu.HBM((P_SIZE, WIDTH), BF16),) * 3,
        in_specs=[pl.BlockSpec(memory_space=pltpu.SMEM)] + [vmem] * 4,
        out_specs=[pl.BlockSpec(memory_space=pltpu.HBM)] * 4,
        scratch_shapes=[pltpu.VMEM((4 * WIDTH, P_SIZE), BF16)]
        + [pltpu.VMEM((P_SIZE, WIDTH), BF16)] * 3
        + [pltpu.SemaphoreType.DMA((4,))],
        cost_estimate=LONG,
        compiler_params=pltpu.CompilerParams(vmem_limit_bytes=VMEM_BYTES),
    )(half.reshape(1), parts, wq, wk, wv)


def cols_kernel(at_ref, r_ref, w_in, out_ref, w_ref, sem):
    load = pltpu.make_async_copy(w_in, w_ref, sem.at[0])
    load.start()
    image = r_ref[...]
    mine = image[:, :WIDTH]
    for t in range(1, 4):
        mine = jnp.where(at_ref[0] == t, image[:, t * WIDTH : (t + 1) * WIDTH], mine)
    load.wait()
    cols = mine.astype(F32) + dot(image, w_ref[...], 1, 1)
    out_ref[...] = jnp.zeros_like(out_ref)
    out_ref[:REF_ROWS, :] = cols.astype(BF16)


def ref_cols(at, image, wr):
    vmem = pl.BlockSpec(memory_space=pltpu.VMEM)
    return pl.pallas_call(
        cols_kernel,
        out_shape=jax.ShapeDtypeStruct((16, WIDTH), BF16),
        in_specs=[
            pl.BlockSpec(memory_space=pltpu.SMEM), vmem, pl.BlockSpec(memory_space=pltpu.HBM)
        ],
        out_specs=vmem,
        scratch_shapes=[
            pltpu.VMEM((WIDTH, 4 * WIDTH), BF16),
            pltpu.SemaphoreType.DMA((1,)),
        ],
        compiler_params=pltpu.CompilerParams(vmem_limit_bytes=8 * 1024 * 1024),
    )(at.reshape(1), image, pltpu.with_memory_space_constraint(wr, pltpu.HBM))


def ref_kernel(g_ref, wk_in, wv_in, out_ref, rows_ref, wk_ref, wv_ref, sem):
    loads = [
        pltpu.make_async_copy(a, b, sem.at[i])
        for i, (a, b) in enumerate(((wk_in, wk_ref), (wv_in, wv_ref)))
    ]
    for load in loads:
        load.start()
    hidden = [g_ref[t].astype(F32) for t in range(4)]
    hidden = jnp.concatenate(hidden, axis=1).astype(BF16)
    rows_ref[...] = jnp.zeros_like(rows_ref)
    pair = []
    for load, w_ref in zip(loads, (wk_ref, wv_ref)):
        load.wait()
        pair.append(dot(hidden, w_ref[...], 1, 1))
    pair = jnp.concatenate(pair, axis=1)
    for row in range(REF_ROWS):
        for group in range(GROUPS):
            at = row * GROUPS + group
            rows_ref[at : at + 1, :] = pair[row : row + 1, LANES * group : LANES * (group + 1)]
    out_ref[...] = jnp.broadcast_to(rows_ref[...].astype(BF16)[None], out_ref.shape)


def ref_pair(gathered, wk, wv):
    hbm, vmem = [pl.BlockSpec(memory_space=space) for space in (pltpu.HBM, pltpu.VMEM)]
    return pl.pallas_call(
        ref_kernel,
        out_shape=jax.ShapeDtypeStruct((N_FRAMES, 16, LANES), BF16),
        in_specs=[vmem, hbm, hbm],
        out_specs=vmem,
        scratch_shapes=[pltpu.VMEM((16, LANES), F32)]
        + [pltpu.VMEM((WIDTH, 4 * WIDTH), BF16)] * 2
        + [pltpu.SemaphoreType.DMA((2,))],
        cost_estimate=LONG,
        compiler_params=pltpu.CompilerParams(vmem_limit_bytes=12 * 1024 * 1024),
    )(gathered, *[pltpu.with_memory_space_constraint(a, pltpu.HBM) for a in (wk, wv)])


def attention_kernel(
    q_in, k_in, v_in, tok_in, pair_ref, gt_ref, ot_out, dq_out, dk_out, dv_out, pack_out,
    q_ref, k_ref, v_ref, tok_ref, wide_ref, r_ref, dqt_ref, dw_ref,
    ot_ref, dq_ref, dk_ref, dv_ref, pack_ref, in_sem, out_sem,
):
    pairs = ((k_in, k_ref), (q_in, q_ref), (v_in, v_ref), (tok_in, tok_ref))
    loads = [pltpu.make_async_copy(a, b, in_sem.at[i]) for i, (a, b) in enumerate(pairs)]
    for load in loads:
        load.start()
    wide_ref[...] = pair_ref[...].astype(F32)
    for row in range(REF_ROWS):
        for group in range(GROUPS):
            r_ref[N_FRAMES * row : N_FRAMES * (row + 1), LANES * group : LANES * (group + 1)] = (
                wide_ref[pl.ds(row * GROUPS + group, N_FRAMES, stride=16), :].astype(BF16)
            )
    g_all = gt_ref[...].astype(F32).T.astype(BF16)
    for load in loads[:3]:
        load.wait()
    def scores(head):
        lo, hi = head * E, head * E + E
        q = q_ref[:, lo:hi]
        k = jnp.concatenate([k_ref[:, lo:hi], r_ref[:, lo:hi]], 0)
        v = jnp.concatenate([v_ref[:, lo:hi], r_ref[:, WIDTH + lo : WIDTH + hi]], 0)
        return k, v, q, dot(k, q, 1, 1), dot(v, gt_ref[lo:hi, :], 1, 0)

    def soften(k, v, q, s, dp):
        e = jnp.exp2((s - jnp.max(s, axis=0, keepdims=True)) * (SCALE * math.log2(math.e)))
        inv = 1.0 / jnp.sum(e, axis=0, keepdims=True)
        mean = jnp.sum(e * dp, axis=0, keepdims=True) * inv
        p = e * inv
        return k, v, q, p.astype(BF16), (p * (dp - mean)).astype(BF16)

    def write(head, k, v, q, p_low, ds):
        lo, hi = head * E, head * E + E
        ot_ref[lo:hi, :] = dot(v, p_low, 0, 0).astype(BF16)
        dqt_ref[lo:hi, :] = dot(k, ds, 0, 0) * SCALE
        dk = dot(ds, q, 1, 0) * SCALE
        dv = dot(p_low, g_all[:, lo:hi], 1, 0)
        dk_ref[:, lo:hi] = dk[:P_SIZE].astype(BF16)
        dv_ref[:, lo:hi] = dv[:P_SIZE].astype(BF16)
        for col, part in ((lo, dk), (WIDTH + lo, dv)):
            for chunk in range(N_FIRST):
                for row in range(REF_ROWS):
                    at = P_SIZE + N_FRAMES * row + N_SECOND * chunk
                    to = N_SECOND * row
                    pack_ref[chunk, to : to + N_SECOND, col : col + E] = part[
                        at : at + N_SECOND
                    ].astype(BF16)

    ahead = scores(0)
    for head in range(HEADS):
        now = ahead
        if head + 1 < HEADS:
            ahead = scores(head + 1)
        write(head, *soften(*now))
    dq = dqt_ref[...].T.astype(BF16)
    dq_ref[...] = dq
    loads[3].wait()
    pairs = ((ot_ref, ot_out), (dq_ref, dq_out), (dk_ref, dk_out), (dv_ref, dv_out))
    stores = [pltpu.make_async_copy(a, b, out_sem.at[N_FIRST + i]) for i, (a, b) in enumerate(pairs)]
    for store in stores:
        store.start()
    for x in range(4):
        dw = dot(tok_ref[x * WIDTH : (x + 1) * WIDTH, :], dq, 1, 0)
        dw_ref[0], dw_ref[1] = dw[:, :LANES], dw[:, LANES : 2 * LANES]
        dw_ref[2, :, :E] = dw[:, 2 * LANES :]
        for row in range(HALF_ROWS):
            left, right = [
                [dw_ref[group, pl.ds(first, 32, stride=ROWS_OUT), :] for group in range(3)]
                for first in (row, row + HALF_ROWS)
            ]
            last = jnp.concatenate([left[2][:, :E], right[2][:, :E]], axis=1)
            at = N_SECOND * (REF_ROWS + row)
            for group, part in enumerate((left[0], left[1], right[0], right[1], last)):
                for low in range(2):
                    pack_ref[
                        2 * x + low, at : at + N_SECOND, LANES * group : LANES * (group + 1)
                    ] = pick(part, low).astype(BF16)
        for chunk in (2 * x, 2 * x + 1):
            stores.append(
                pltpu.make_async_copy(pack_ref.at[chunk], pack_out.at[chunk], out_sem.at[chunk])
            )
            stores[-1].start()
    for store in stores:
        store.wait()


def attention(q, k, v, pair, gt, tok):
    hbm, vmem = [pl.BlockSpec(memory_space=space) for space in (pltpu.HBM, pltpu.VMEM)]
    rows = REF_ROWS + HALF_ROWS
    return pl.pallas_call(
        attention_kernel,
        out_shape=(pltpu.HBM((WIDTH, P_SIZE), BF16),)
        + (pltpu.HBM((P_SIZE, WIDTH), BF16),) * 3
        + (pltpu.HBM((N_FIRST, N_SECOND * rows, 2 * WIDTH), BF16),),
        in_specs=[hbm] * 4 + [vmem] * 2,
        out_specs=[hbm] * 5,
        scratch_shapes=[pltpu.VMEM((P_SIZE, WIDTH), BF16)] * 3
        + [
            pltpu.VMEM((4 * WIDTH, P_SIZE), BF16),
            pltpu.VMEM((N_FRAMES * 16, LANES), F32),
            pltpu.VMEM((P_SIZE, 2 * WIDTH), BF16),
            pltpu.VMEM((WIDTH, P_SIZE), F32),
            pltpu.VMEM((3, WIDTH, LANES), F32),
            pltpu.VMEM((WIDTH, P_SIZE), BF16),
            pltpu.VMEM((P_SIZE, WIDTH), BF16),
            pltpu.VMEM((P_SIZE, WIDTH), BF16),
            pltpu.VMEM((P_SIZE, WIDTH), BF16),
            pltpu.VMEM((N_FIRST, N_SECOND * rows, 2 * WIDTH), BF16),
            pltpu.SemaphoreType.DMA((4,)),
            pltpu.SemaphoreType.DMA((N_FIRST + 4,)),
        ],
        compiler_params=pltpu.CompilerParams(vmem_limit_bytes=VMEM_BYTES),
    )(*[pltpu.with_memory_space_constraint(a, pltpu.HBM) for a in (q, k, v, tok)], pair, gt)


def token_kernel(
    core_ref, dq_in, dk_in, dv_in, wq_in, wk_in, wv_in, kept_out, sent_out,
    dq_ref, dk_ref, dv_ref, wq_ref, wk_ref, wv_ref, kept_ref, sent_ref, in_sem, out_sem,
):
    pairs = (
        (wq_in, wq_ref), (dq_in, dq_ref), (wk_in, wk_ref),
        (dk_in, dk_ref), (wv_in, wv_ref), (dv_in, dv_ref),
    )
    loads = [pltpu.make_async_copy(a, b, in_sem.at[i]) for i, (a, b) in enumerate(pairs)]
    for load in loads:
        load.start()
    core = core_ref[0]
    total = None
    for i, (d_ref, w_ref) in enumerate(((dq_ref, wq_ref), (dk_ref, wk_ref), (dv_ref, wv_ref))):
        loads[2 * i].wait()
        loads[2 * i + 1].wait()
        part = dot(d_ref[...], w_ref[...], 1, 0)
        total = part if total is None else total + part
    total = total.T.astype(BF16)
    stores = []
    for half in range(2):
        zero, one = [total[(2 * half + c) * WIDTH : (2 * half + c + 1) * WIDTH] for c in range(2)]
        sent_ref[half] = jnp.where(core == 0, one, zero)
        kept_ref[half] = jnp.where(core == 0, zero, one)
        for i, (a, b) in enumerate(((sent_ref, sent_out), (kept_ref, kept_out))):
            store = pltpu.make_async_copy(a.at[half], b.at[half], out_sem.at[2 * half + i])
            store.start()
            stores.append(store)
    for store in stores:
        store.wait()


def token_parts(core, dq, dk, dv, wq, wk, wv):
    hbm = pl.BlockSpec(memory_space=pltpu.HBM)
    return pl.pallas_call(
        token_kernel,
        out_shape=(pltpu.HBM((2, WIDTH, P_SIZE), BF16),) * 2,
        in_specs=[pl.BlockSpec(memory_space=pltpu.SMEM)] + [hbm] * 6,
        out_specs=[hbm] * 2,
        scratch_shapes=[pltpu.VMEM((P_SIZE, WIDTH), BF16)] * 3
        + [pltpu.VMEM((WIDTH, 4 * WIDTH), BF16)] * 3
        + [pltpu.VMEM((2, WIDTH, P_SIZE), BF16)] * 2
        + [pltpu.SemaphoreType.DMA((6,)), pltpu.SemaphoreType.DMA((4,))],
        cost_estimate=pl.CostEstimate(flops=1, bytes_accessed=1, transcendentals=0),
        compiler_params=pltpu.CompilerParams(vmem_limit_bytes=VMEM_BYTES),
    )(
        core.reshape(1),
        *[pltpu.with_memory_space_constraint(a, pltpu.HBM) for a in (dq, dk, dv, wq, wk, wv)],
    )


def combine_kernel(half_ref, pair_ref, got_ref, out_ref):
    mine = jnp.where(half_ref[0] == 0, pair_ref[0].astype(F32), pair_ref[1].astype(F32))
    out_ref[...] = (mine + got_ref[...].astype(F32)).astype(BF16)


def combine(half, paired, got):
    vmem = pl.BlockSpec(memory_space=pltpu.VMEM)
    return pl.pallas_call(
        combine_kernel,
        out_shape=jax.ShapeDtypeStruct((WIDTH, P_SIZE), BF16),
        in_specs=[pl.BlockSpec(memory_space=pltpu.SMEM)] + [vmem] * 2,
        out_specs=vmem,
        cost_estimate=LONG,
        compiler_params=pltpu.CompilerParams(vmem_limit_bytes=8 * 1024 * 1024),
    )(half.reshape(1), paired, got)


def regroup_kernel(in_ref, out_ref, held_ref):
    rows = REF_ROWS + HALF_ROWS
    for row in range(rows):
        at = N_SECOND * row
        part = in_ref[0, at : at + N_SECOND, :].astype(F32)
        for x in range(1, N_FIRST):
            part = part + in_ref[x, at : at + N_SECOND, :].astype(F32)
        for group in range(GROUPS):
            held_ref[group, pl.ds(row, N_SECOND, stride=rows), :] = part[
                :, LANES * group : LANES * (group + 1)
            ]
    for group in range(GROUPS):
        out_ref[:, LANES * group : LANES * (group + 1)] = held_ref[group].astype(BF16)


def regroup(parts):
    rows = REF_ROWS + HALF_ROWS
    return pl.pallas_call(
        regroup_kernel,
        out_shape=jax.ShapeDtypeStruct((N_SECOND * rows, 2 * WIDTH), BF16),
        scratch_shapes=[pltpu.VMEM((GROUPS, N_SECOND * rows, LANES), F32)],
        cost_estimate=LONG,
        compiler_params=pltpu.CompilerParams(vmem_limit_bytes=8 * 1024 * 1024),
    )(parts)


def finish_kernel(in_ref, grad_ref, key_ref, value_ref):
    total = in_ref[0].astype(F32)
    for j in range(1, N_SECOND):
        total = total + in_ref[j].astype(F32)
    key_ref[...] = total[:REF_ROWS, :WIDTH].astype(BF16)
    value_ref[...] = total[:REF_ROWS, WIDTH:].astype(BF16)
    low, tail = total[:, : 4 * LANES], total[:, 4 * LANES :]
    left = jnp.concatenate([low[:, : 2 * LANES], tail[:, :E]], axis=1)
    right = jnp.concatenate([low[:, 2 * LANES :], tail[:, E:]], axis=1)
    grad_ref[:HALF_ROWS, :] = left[REF_ROWS:]
    grad_ref[HALF_ROWS:, :] = right[REF_ROWS:]


def finish(parts):
    return pl.pallas_call(
        finish_kernel,
        out_shape=(
            jax.ShapeDtypeStruct((ROWS_OUT, WIDTH), F32),
            jax.ShapeDtypeStruct((REF_ROWS, WIDTH), BF16),
            jax.ShapeDtypeStruct((REF_ROWS, WIDTH), BF16),
        ),
        compiler_params=pltpu.CompilerParams(vmem_limit_bytes=8 * 1024 * 1024),
    )(parts)


def per_device(
    tokens, reference_image, query_weight, key_weight, value_weight, ref_weight, cotangent
):
    core, half = lax.axis_index("c"), lax.axis_index("h")
    swap = [(0, 1), (1, 0)]
    wq, wk, wv = query_weight.T, key_weight.T, value_weight.T
    cols = ref_cols(2 * half + core, reference_image, ref_weight.T)
    ref_hidden = lax.all_gather(cols, TENSOR, axis=0, tiled=False)
    ref_hidden, own = lax.optimization_barrier((ref_hidden, tokens.T))
    other = lax.ppermute(own, "h", swap)
    pair = ref_pair(ref_hidden, wk, wv)
    pair = lax.all_to_all(pair, FIRST + SECOND, 0, 0, tiled=True)
    parts = lax.all_gather(jnp.stack([own, other]), "c", axis=0, tiled=False)
    tok, queries, keys, values = project(half, parts, wq, wk, wv)
    attended, query_grads, key_grads, value_grads, pack = attention(
        queries, keys, values, pair.reshape(N_FRAMES * 16, LANES), cotangent.T, tok
    )
    pack = lax.all_to_all(pack, FIRST, 0, 0, tiled=True)
    kept, sent = token_parts(core, query_grads, key_grads, value_grads, wq, wk, wv)
    got = lax.ppermute(sent, "c", swap)
    paired = (kept.astype(F32) + got.astype(F32)).astype(BF16)
    sent = lax.dynamic_index_in_dim(paired, 1 - half, 0, False)
    got = lax.ppermute(sent, "h", swap)
    token_grads = combine(half, paired, got).T
    pack = regroup(pack)
    pack = pack.reshape(N_SECOND, REF_ROWS + HALF_ROWS, 2 * WIDTH)
    pack = lax.all_to_all(pack, SECOND, 0, 0, tiled=True)
    query_weight_grad, ref_key_grads, ref_value_grads = finish(pack)
    return attended.T, token_grads, query_weight_grad, ref_key_grads, ref_value_grads


def solution(mesh):
    mesh = Mesh(mesh.devices.reshape(4, 4, 2, 4, 2, 2), FRAMES + TENSOR)
    return jax.shard_map(
        per_device,
        mesh=mesh,
        in_specs=(
            P(FRAMES, TENSOR),
            P(FRAMES, None),
            P(None, TENSOR),
            P(None, TENSOR),
            P(None, TENSOR),
            P(None, TENSOR),
            P(FRAMES, TENSOR),
        ),
        out_specs=(P(FRAMES, TENSOR),) * 5,
        check_vma=False,
    )
```

```python
import math

import jax
import jax.numpy as jnp
from jax import lax
from jax.experimental import pallas as pl
from jax.experimental.pallas import tpu as pltpu
from jax.sharding import Mesh
from jax.sharding import PartitionSpec as P

E = 64
P_SIZE = 384
HEADS = 5
WIDTH = HEADS * E
FRAMES = ("x", "yh", "yl", "z")
FIRST = ("x", "yl")
SECOND = ("yh", "z")
TENSOR = ("h", "c")
N_FIRST, N_SECOND = 8, 16
N_FRAMES = N_FIRST * N_SECOND
REF_ROWS = 3
ROWS_OUT = 10
HALF_ROWS = ROWS_OUT // 2
LANES = 128
LONG = pl.CostEstimate(flops=10**10, bytes_accessed=10**10, transcendentals=0)
VMEM_BYTES = 24 * 1024 * 1024
GROUPS = 2 * WIDTH // LANES
SCALE = 1.0 / math.sqrt(E)
F32 = jnp.float32
BF16 = jnp.bfloat16


def pick(rows, low):
    return jnp.concatenate([rows[8 * i + 4 * low : 8 * i + 4 * low + 4] for i in range(4)], axis=0)


def dot(a, b, a_dim, b_dim):
    return lax.dot_general(a, b, (((a_dim,), (b_dim,)), ((), ())), preferred_element_type=F32)


def stack_kernel(own_ref, other_ref, out_ref):
    out_ref[0] = own_ref[...]
    out_ref[1] = other_ref[...]


def stack(own, other):
    return pl.pallas_call(
        stack_kernel,
        out_shape=jax.ShapeDtypeStruct((2, WIDTH, P_SIZE), BF16),
        cost_estimate=LONG,
        compiler_params=pltpu.CompilerParams(vmem_limit_bytes=8 * 1024 * 1024),
    )(own, other)


def project_kernel(
    half_ref, t_ref, wq_ref, wk_ref, wv_ref, tok_out, q_out, k_out, v_out,
    tok_ref, q_ref, k_ref, v_ref, sem,
):
    half = half_ref[0]
    pairs = ((tok_ref, tok_out), (q_ref, q_out), (k_ref, k_out), (v_ref, v_out))
    copies = [pltpu.make_async_copy(a, b, sem.at[i]) for i, (a, b) in enumerate(pairs)]
    for core in range(2):
        for slot in range(2):
            at = pl.multiple_of((2 * lax.rem(half + slot, 2) + core) * WIDTH, E)
            tok_ref[pl.ds(at, WIDTH), :] = t_ref[core, slot]
    copies[0].start()
    tok = tok_ref[...]
    for i, (w_ref, out_ref) in enumerate(((wq_ref, q_ref), (wk_ref, k_ref), (wv_ref, v_ref))):
        out_ref[...] = dot(w_ref[...], tok, 1, 0).T.astype(BF16)
        copies[i + 1].start()
    for copy in copies:
        copy.wait()


def project(half, parts, wq, wk, wv):
    vmem = pl.BlockSpec(memory_space=pltpu.VMEM)
    return pl.pallas_call(
        project_kernel,
        out_shape=(pltpu.HBM((4 * WIDTH, P_SIZE), BF16),)
        + (pltpu.HBM((P_SIZE, WIDTH), BF16),) * 3,
        in_specs=[pl.BlockSpec(memory_space=pltpu.SMEM)] + [vmem] * 4,
        out_specs=[pl.BlockSpec(memory_space=pltpu.HBM)] * 4,
        scratch_shapes=[pltpu.VMEM((4 * WIDTH, P_SIZE), BF16)]
        + [pltpu.VMEM((P_SIZE, WIDTH), BF16)] * 3
        + [pltpu.SemaphoreType.DMA((4,))],
        compiler_params=pltpu.CompilerParams(vmem_limit_bytes=VMEM_BYTES),
    )(half.reshape(1), parts, wq, wk, wv)


def cols_kernel(at_ref, r_ref, w_in, out_ref, w_ref, sem):
    load = pltpu.make_async_copy(w_in, w_ref, sem.at[0])
    load.start()
    image = r_ref[...]
    mine = image[:, :WIDTH]
    for t in range(1, 4):
        mine = jnp.where(at_ref[0] == t, image[:, t * WIDTH : (t + 1) * WIDTH], mine)
    load.wait()
    cols = mine.astype(F32) + dot(image, w_ref[...], 1, 1)
    out_ref[...] = jnp.zeros_like(out_ref)
    out_ref[:REF_ROWS, :] = cols.astype(BF16)


def ref_cols(at, image, wr):
    vmem = pl.BlockSpec(memory_space=pltpu.VMEM)
    return pl.pallas_call(
        cols_kernel,
        out_shape=jax.ShapeDtypeStruct((16, WIDTH), BF16),
        in_specs=[
            pl.BlockSpec(memory_space=pltpu.SMEM), vmem, pl.BlockSpec(memory_space=pltpu.HBM)
        ],
        out_specs=vmem,
        scratch_shapes=[
            pltpu.VMEM((WIDTH, 4 * WIDTH), BF16),
            pltpu.SemaphoreType.DMA((1,)),
        ],
        compiler_params=pltpu.CompilerParams(vmem_limit_bytes=8 * 1024 * 1024),
    )(at.reshape(1), image, pltpu.with_memory_space_constraint(wr, pltpu.HBM))


def ref_kernel(g_ref, wk_in, wv_in, out_ref, rows_ref, wk_ref, wv_ref, sem):
    loads = [
        pltpu.make_async_copy(a, b, sem.at[i])
        for i, (a, b) in enumerate(((wk_in, wk_ref), (wv_in, wv_ref)))
    ]
    for load in loads:
        load.start()
    hidden = [g_ref[t].astype(F32) for t in range(4)]
    hidden = jnp.concatenate(hidden, axis=1).astype(BF16)
    rows_ref[...] = jnp.zeros_like(rows_ref)
    pair = []
    for load, w_ref in zip(loads, (wk_ref, wv_ref)):
        load.wait()
        pair.append(dot(hidden, w_ref[...], 1, 1))
    pair = jnp.concatenate(pair, axis=1)
    for row in range(REF_ROWS):
        for group in range(GROUPS):
            at = row * GROUPS + group
            rows_ref[at : at + 1, :] = pair[row : row + 1, LANES * group : LANES * (group + 1)]
    out_ref[...] = jnp.broadcast_to(rows_ref[...].astype(BF16)[None], out_ref.shape)


def ref_pair(gathered, wk, wv):
    hbm, vmem = [pl.BlockSpec(memory_space=space) for space in (pltpu.HBM, pltpu.VMEM)]
    return pl.pallas_call(
        ref_kernel,
        out_shape=jax.ShapeDtypeStruct((N_SECOND, 16, LANES), BF16),
        in_specs=[vmem, hbm, hbm],
        out_specs=vmem,
        scratch_shapes=[pltpu.VMEM((16, LANES), F32)]
        + [pltpu.VMEM((WIDTH, 4 * WIDTH), BF16)] * 2
        + [pltpu.SemaphoreType.DMA((2,))],
        cost_estimate=LONG,
        compiler_params=pltpu.CompilerParams(vmem_limit_bytes=12 * 1024 * 1024),
    )(gathered, *[pltpu.with_memory_space_constraint(a, pltpu.HBM) for a in (wk, wv)])


def attention_kernel(
    q_in, k_in, v_in, tok_in, pair_ref, gt_ref, ot_out, dq_out, dk_out, dv_out, pack_out,
    q_ref, k_ref, v_ref, tok_ref, wide_ref, r_ref, dqt_ref, dw_ref,
    ot_ref, dq_ref, dk_ref, dv_ref, pack_ref, in_sem, out_sem,
):
    pairs = ((k_in, k_ref), (q_in, q_ref), (v_in, v_ref), (tok_in, tok_ref))
    loads = [pltpu.make_async_copy(a, b, in_sem.at[i]) for i, (a, b) in enumerate(pairs)]
    for load in loads:
        load.start()
    wide_ref[...] = pair_ref[...].astype(F32)
    for row in range(REF_ROWS):
        for group in range(GROUPS):
            r_ref[N_FRAMES * row : N_FRAMES * (row + 1), LANES * group : LANES * (group + 1)] = (
                wide_ref[pl.ds(row * GROUPS + group, N_FRAMES, stride=16), :].astype(BF16)
            )
    g_all = gt_ref[...].astype(F32).T.astype(BF16)
    for load in loads[:3]:
        load.wait()
    def scores(head):
        lo, hi = head * E, head * E + E
        q = q_ref[:, lo:hi]
        k = jnp.concatenate([k_ref[:, lo:hi], r_ref[:, lo:hi]], 0)
        v = jnp.concatenate([v_ref[:, lo:hi], r_ref[:, WIDTH + lo : WIDTH + hi]], 0)
        return k, v, q, dot(k, q, 1, 1), dot(v, gt_ref[lo:hi, :], 1, 0)

    def soften(k, v, q, s, dp):
        e = jnp.exp2((s - jnp.max(s, axis=0, keepdims=True)) * (SCALE * math.log2(math.e)))
        inv = 1.0 / jnp.sum(e, axis=0, keepdims=True)
        mean = jnp.sum(e * dp, axis=0, keepdims=True) * inv
        p = e * inv
        return k, v, q, p.astype(BF16), (p * (dp - mean)).astype(BF16)

    def write(head, k, v, q, p_low, ds):
        lo, hi = head * E, head * E + E
        ot_ref[lo:hi, :] = dot(v, p_low, 0, 0).astype(BF16)
        dqt_ref[lo:hi, :] = dot(k, ds, 0, 0) * SCALE
        dk = dot(ds, q, 1, 0) * SCALE
        dv = dot(p_low, g_all[:, lo:hi], 1, 0)
        dk_ref[:, lo:hi] = dk[:P_SIZE].astype(BF16)
        dv_ref[:, lo:hi] = dv[:P_SIZE].astype(BF16)
        for col, part in ((lo, dk), (WIDTH + lo, dv)):
            for chunk in range(N_FIRST):
                for row in range(REF_ROWS):
                    at = P_SIZE + N_FRAMES * row + N_SECOND * chunk
                    to = N_SECOND * row
                    pack_ref[chunk, to : to + N_SECOND, col : col + E] = part[
                        at : at + N_SECOND
                    ].astype(BF16)

    ahead = scores(0)
    for head in range(HEADS):
        now = ahead
        if head + 1 < HEADS:
            ahead = scores(head + 1)
        write(head, *soften(*now))
    dq = dqt_ref[...].T.astype(BF16)
    dq_ref[...] = dq
    loads[3].wait()
    pairs = ((ot_ref, ot_out), (dq_ref, dq_out), (dk_ref, dk_out), (dv_ref, dv_out))
    stores = [pltpu.make_async_copy(a, b, out_sem.at[N_FIRST + i]) for i, (a, b) in enumerate(pairs)]
    for store in stores:
        store.start()
    for x in range(4):
        dw = dot(tok_ref[x * WIDTH : (x + 1) * WIDTH, :], dq, 1, 0)
        dw_ref[0], dw_ref[1] = dw[:, :LANES], dw[:, LANES : 2 * LANES]
        dw_ref[2, :, :E] = dw[:, 2 * LANES :]
        for row in range(HALF_ROWS):
            left, right = [
                [dw_ref[group, pl.ds(first, 32, stride=ROWS_OUT), :] for group in range(3)]
                for first in (row, row + HALF_ROWS)
            ]
            last = jnp.concatenate([left[2][:, :E], right[2][:, :E]], axis=1)
            at = N_SECOND * (REF_ROWS + row)
            for group, part in enumerate((left[0], left[1], right[0], right[1], last)):
                for low in range(2):
                    pack_ref[
                        2 * x + low, at : at + N_SECOND, LANES * group : LANES * (group + 1)
                    ] = pick(part, low).astype(BF16)
        for chunk in (2 * x, 2 * x + 1):
            stores.append(
                pltpu.make_async_copy(pack_ref.at[chunk], pack_out.at[chunk], out_sem.at[chunk])
            )
            stores[-1].start()
    for store in stores:
        store.wait()


def attention(q, k, v, pair, gt, tok):
    hbm, vmem = [pl.BlockSpec(memory_space=space) for space in (pltpu.HBM, pltpu.VMEM)]
    rows = REF_ROWS + HALF_ROWS
    return pl.pallas_call(
        attention_kernel,
        out_shape=(pltpu.HBM((WIDTH, P_SIZE), BF16),)
        + (pltpu.HBM((P_SIZE, WIDTH), BF16),) * 3
        + (pltpu.HBM((N_FIRST, N_SECOND * rows, 2 * WIDTH), BF16),),
        in_specs=[hbm] * 4 + [vmem] * 2,
        out_specs=[hbm] * 5,
        scratch_shapes=[pltpu.VMEM((P_SIZE, WIDTH), BF16)] * 3
        + [
            pltpu.VMEM((4 * WIDTH, P_SIZE), BF16),
            pltpu.VMEM((N_FRAMES * 16, LANES), F32),
            pltpu.VMEM((P_SIZE, 2 * WIDTH), BF16),
            pltpu.VMEM((WIDTH, P_SIZE), F32),
            pltpu.VMEM((3, WIDTH, LANES), F32),
            pltpu.VMEM((WIDTH, P_SIZE), BF16),
            pltpu.VMEM((P_SIZE, WIDTH), BF16),
            pltpu.VMEM((P_SIZE, WIDTH), BF16),
            pltpu.VMEM((P_SIZE, WIDTH), BF16),
            pltpu.VMEM((N_FIRST, N_SECOND * rows, 2 * WIDTH), BF16),
            pltpu.SemaphoreType.DMA((4,)),
            pltpu.SemaphoreType.DMA((N_FIRST + 4,)),
        ],
        compiler_params=pltpu.CompilerParams(vmem_limit_bytes=VMEM_BYTES),
    )(*[pltpu.with_memory_space_constraint(a, pltpu.HBM) for a in (q, k, v, tok)], pair, gt)


def token_kernel(
    core_ref, dq_in, dk_in, dv_in, wq_in, wk_in, wv_in, kept_out, sent_out,
    dq_ref, dk_ref, dv_ref, wq_ref, wk_ref, wv_ref, kept_ref, sent_ref, in_sem, out_sem,
):
    pairs = (
        (wq_in, wq_ref), (dq_in, dq_ref), (wk_in, wk_ref),
        (dk_in, dk_ref), (wv_in, wv_ref), (dv_in, dv_ref),
    )
    loads = [pltpu.make_async_copy(a, b, in_sem.at[i]) for i, (a, b) in enumerate(pairs)]
    for load in loads:
        load.start()
    core = core_ref[0]
    total = None
    for i, (d_ref, w_ref) in enumerate(((dq_ref, wq_ref), (dk_ref, wk_ref), (dv_ref, wv_ref))):
        loads[2 * i].wait()
        loads[2 * i + 1].wait()
        part = dot(d_ref[...], w_ref[...], 1, 0)
        total = part if total is None else total + part
    total = total.T.astype(BF16)
    stores = []
    for half in range(2):
        zero, one = [total[(2 * half + c) * WIDTH : (2 * half + c + 1) * WIDTH] for c in range(2)]
        sent_ref[half] = jnp.where(core == 0, one, zero)
        kept_ref[half] = jnp.where(core == 0, zero, one)
        for i, (a, b) in enumerate(((sent_ref, sent_out), (kept_ref, kept_out))):
            store = pltpu.make_async_copy(a.at[half], b.at[half], out_sem.at[2 * half + i])
            store.start()
            stores.append(store)
    for store in stores:
        store.wait()


def token_parts(core, dq, dk, dv, wq, wk, wv):
    hbm = pl.BlockSpec(memory_space=pltpu.HBM)
    return pl.pallas_call(
        token_kernel,
        out_shape=(pltpu.HBM((2, WIDTH, P_SIZE), BF16),) * 2,
        in_specs=[pl.BlockSpec(memory_space=pltpu.SMEM)] + [hbm] * 6,
        out_specs=[hbm] * 2,
        scratch_shapes=[pltpu.VMEM((P_SIZE, WIDTH), BF16)] * 3
        + [pltpu.VMEM((WIDTH, 4 * WIDTH), BF16)] * 3
        + [pltpu.VMEM((2, WIDTH, P_SIZE), BF16)] * 2
        + [pltpu.SemaphoreType.DMA((6,)), pltpu.SemaphoreType.DMA((4,))],
        cost_estimate=pl.CostEstimate(flops=1, bytes_accessed=1, transcendentals=0),
        compiler_params=pltpu.CompilerParams(vmem_limit_bytes=VMEM_BYTES),
    )(
        core.reshape(1),
        *[pltpu.with_memory_space_constraint(a, pltpu.HBM) for a in (dq, dk, dv, wq, wk, wv)],
    )


def combine_kernel(half_ref, pair_ref, got_ref, out_ref):
    mine = jnp.where(half_ref[0] == 0, pair_ref[0].astype(F32), pair_ref[1].astype(F32))
    out_ref[...] = (mine + got_ref[...].astype(F32)).astype(BF16)


def combine(half, paired, got):
    vmem = pl.BlockSpec(memory_space=pltpu.VMEM)
    return pl.pallas_call(
        combine_kernel,
        out_shape=jax.ShapeDtypeStruct((WIDTH, P_SIZE), BF16),
        in_specs=[pl.BlockSpec(memory_space=pltpu.SMEM)] + [vmem] * 2,
        out_specs=vmem,
        cost_estimate=LONG,
        compiler_params=pltpu.CompilerParams(vmem_limit_bytes=8 * 1024 * 1024),
    )(half.reshape(1), paired, got)


def regroup_kernel(in_ref, out_ref, held_ref):
    rows = REF_ROWS + HALF_ROWS
    for row in range(rows):
        at = N_SECOND * row
        part = in_ref[0, at : at + N_SECOND, :].astype(F32)
        for x in range(1, N_FIRST):
            part = part + in_ref[x, at : at + N_SECOND, :].astype(F32)
        for group in range(GROUPS):
            held_ref[group, pl.ds(row, N_SECOND, stride=rows), :] = part[
                :, LANES * group : LANES * (group + 1)
            ]
    for group in range(GROUPS):
        out_ref[:, LANES * group : LANES * (group + 1)] = held_ref[group].astype(BF16)


def regroup(parts):
    rows = REF_ROWS + HALF_ROWS
    return pl.pallas_call(
        regroup_kernel,
        out_shape=jax.ShapeDtypeStruct((N_SECOND * rows, 2 * WIDTH), BF16),
        scratch_shapes=[pltpu.VMEM((GROUPS, N_SECOND * rows, LANES), F32)],
        cost_estimate=LONG,
        compiler_params=pltpu.CompilerParams(vmem_limit_bytes=8 * 1024 * 1024),
    )(parts)


def finish_kernel(in_ref, grad_ref, key_ref, value_ref):
    total = in_ref[0].astype(F32)
    for j in range(1, N_SECOND):
        total = total + in_ref[j].astype(F32)
    key_ref[...] = total[:REF_ROWS, :WIDTH].astype(BF16)
    value_ref[...] = total[:REF_ROWS, WIDTH:].astype(BF16)
    low, tail = total[:, : 4 * LANES], total[:, 4 * LANES :]
    left = jnp.concatenate([low[:, : 2 * LANES], tail[:, :E]], axis=1)
    right = jnp.concatenate([low[:, 2 * LANES :], tail[:, E:]], axis=1)
    grad_ref[:HALF_ROWS, :] = left[REF_ROWS:]
    grad_ref[HALF_ROWS:, :] = right[REF_ROWS:]


def finish(parts):
    return pl.pallas_call(
        finish_kernel,
        out_shape=(
            jax.ShapeDtypeStruct((ROWS_OUT, WIDTH), F32),
            jax.ShapeDtypeStruct((REF_ROWS, WIDTH), BF16),
            jax.ShapeDtypeStruct((REF_ROWS, WIDTH), BF16),
        ),
        compiler_params=pltpu.CompilerParams(vmem_limit_bytes=8 * 1024 * 1024),
    )(parts)


def per_device(
    tokens, reference_image, query_weight, key_weight, value_weight, ref_weight, cotangent
):
    core, half = lax.axis_index("c"), lax.axis_index("h")
    swap = [(0, 1), (1, 0)]
    wq, wk, wv = query_weight.T, key_weight.T, value_weight.T
    cols = ref_cols(2 * half + core, reference_image, ref_weight.T)
    ref_hidden = lax.all_gather(cols, TENSOR, axis=0, tiled=False)
    ref_hidden, own = lax.optimization_barrier((ref_hidden, tokens.T))
    other = lax.ppermute(own, "h", swap)
    pair = ref_pair(ref_hidden, wk, wv)
    pair = lax.all_to_all(pair, SECOND, 0, 0, tiled=True).reshape(1, N_SECOND * 16, LANES)
    pair, blocks = lax.optimization_barrier((pair, stack(own, other)))
    pair = jnp.broadcast_to(pair, (N_FIRST, N_SECOND * 16, LANES))
    pair = lax.all_to_all(pair, FIRST, 0, 0, tiled=True)
    parts = lax.all_gather(blocks, "c", axis=0, tiled=False)
    tok, queries, keys, values = project(half, parts, wq, wk, wv)
    attended, query_grads, key_grads, value_grads, pack = attention(
        queries, keys, values, pair.reshape(N_FRAMES * 16, LANES), cotangent.T, tok
    )
    pack = lax.all_to_all(pack, FIRST, 0, 0, tiled=True)
    kept, sent = token_parts(core, query_grads, key_grads, value_grads, wq, wk, wv)
    got = lax.ppermute(sent, "c", swap)
    paired = (kept.astype(F32) + got.astype(F32)).astype(BF16)
    sent = lax.dynamic_index_in_dim(paired, 1 - half, 0, False)
    got = lax.ppermute(sent, "h", swap)
    token_grads = combine(half, paired, got).T
    pack = regroup(pack)
    pack = pack.reshape(N_SECOND, REF_ROWS + HALF_ROWS, 2 * WIDTH)
    pack = lax.all_to_all(pack, SECOND, 0, 0, tiled=True)
    query_weight_grad, ref_key_grads, ref_value_grads = finish(pack)
    return attended.T, token_grads, query_weight_grad, ref_key_grads, ref_value_grads


def solution(mesh):
    mesh = Mesh(mesh.devices.reshape(4, 4, 2, 4, 2, 2), FRAMES + TENSOR)
    return jax.shard_map(
        per_device,
        mesh=mesh,
        in_specs=(
            P(FRAMES, TENSOR),
            P(FRAMES, None),
            P(None, TENSOR),
            P(None, TENSOR),
            P(None, TENSOR),
            P(None, TENSOR),
            P(FRAMES, TENSOR),
        ),
        out_specs=(P(FRAMES, TENSOR),) * 5,
        check_vma=False,
    )
```

```python
import math

import jax
import jax.numpy as jnp
from jax import lax
from jax.experimental import pallas as pl
from jax.experimental.pallas import tpu as pltpu
from jax.sharding import Mesh
from jax.sharding import PartitionSpec as P

E = 64
P_SIZE = 384
HEADS = 5
WIDTH = HEADS * E
FRAMES = ("x", "yh", "yl", "z")
FIRST = ("x", "yl")
SECOND = ("yh", "z")
TENSOR = ("h", "c")
N_FIRST, N_SECOND = 8, 16
N_FRAMES = N_FIRST * N_SECOND
REF_ROWS = 3
ROWS_OUT = 10
HALF_ROWS = ROWS_OUT // 2
LANES = 128
LONG = pl.CostEstimate(flops=10**10, bytes_accessed=10**10, transcendentals=0)
VMEM_BYTES = 24 * 1024 * 1024
GROUPS = 2 * WIDTH // LANES
SCALE = 1.0 / math.sqrt(E)
F32 = jnp.float32
BF16 = jnp.bfloat16


def pick(rows, low):
    return jnp.concatenate([rows[8 * i + 4 * low : 8 * i + 4 * low + 4] for i in range(4)], axis=0)


def dot(a, b, a_dim, b_dim):
    return lax.dot_general(a, b, (((a_dim,), (b_dim,)), ((), ())), preferred_element_type=F32)


def spread_kernel(in_ref, out_ref, sem):
    copies = [pltpu.make_async_copy(in_ref, out_ref.at[i], sem.at[i]) for i in range(N_FIRST)]
    for copy in copies:
        copy.start()
    for copy in copies:
        copy.wait()


def spread(pair):
    return pl.pallas_call(
        spread_kernel,
        out_shape=pltpu.HBM((N_FIRST,) + pair.shape, BF16),
        out_specs=pl.BlockSpec(memory_space=pltpu.HBM),
        scratch_shapes=[pltpu.SemaphoreType.DMA((N_FIRST,))],
        cost_estimate=LONG,
        compiler_params=pltpu.CompilerParams(vmem_limit_bytes=8 * 1024 * 1024),
    )(pair)


def stack_kernel(own_ref, other_ref, out_ref):
    out_ref[0] = own_ref[...]
    out_ref[1] = other_ref[...]


def stack(own, other):
    return pl.pallas_call(
        stack_kernel,
        out_shape=jax.ShapeDtypeStruct((2, WIDTH, P_SIZE), BF16),
        cost_estimate=LONG,
        compiler_params=pltpu.CompilerParams(vmem_limit_bytes=8 * 1024 * 1024),
    )(own, other)


def project_kernel(
    half_ref, t_ref, wq_ref, wk_ref, wv_ref, tok_out, q_out, k_out, v_out,
    tok_ref, q_ref, k_ref, v_ref, sem,
):
    half = half_ref[0]
    pairs = ((tok_ref, tok_out), (q_ref, q_out), (k_ref, k_out), (v_ref, v_out))
    copies = [pltpu.make_async_copy(a, b, sem.at[i]) for i, (a, b) in enumerate(pairs)]
    for core in range(2):
        for slot in range(2):
            at = pl.multiple_of((2 * lax.rem(half + slot, 2) + core) * WIDTH, E)
            tok_ref[pl.ds(at, WIDTH), :] = t_ref[core, slot]
    copies[0].start()
    tok = tok_ref[...]
    for i, (w_ref, out_ref) in enumerate(((wq_ref, q_ref), (wk_ref, k_ref), (wv_ref, v_ref))):
        out_ref[...] = dot(w_ref[...], tok, 1, 0).T.astype(BF16)
        copies[i + 1].start()
    for copy in copies:
        copy.wait()


def project(half, parts, wq, wk, wv):
    vmem = pl.BlockSpec(memory_space=pltpu.VMEM)
    return pl.pallas_call(
        project_kernel,
        out_shape=(pltpu.HBM((4 * WIDTH, P_SIZE), BF16),)
        + (pltpu.HBM((P_SIZE, WIDTH), BF16),) * 3,
        in_specs=[pl.BlockSpec(memory_space=pltpu.SMEM)] + [vmem] * 4,
        out_specs=[pl.BlockSpec(memory_space=pltpu.HBM)] * 4,
        scratch_shapes=[pltpu.VMEM((4 * WIDTH, P_SIZE), BF16)]
        + [pltpu.VMEM((P_SIZE, WIDTH), BF16)] * 3
        + [pltpu.SemaphoreType.DMA((4,))],
        compiler_params=pltpu.CompilerParams(vmem_limit_bytes=VMEM_BYTES),
    )(half.reshape(1), parts, wq, wk, wv)


def cols_kernel(at_ref, r_ref, w_in, out_ref, w_ref, sem):
    load = pltpu.make_async_copy(w_in, w_ref, sem.at[0])
    load.start()
    image = r_ref[...]
    mine = image[:, :WIDTH]
    for t in range(1, 4):
        mine = jnp.where(at_ref[0] == t, image[:, t * WIDTH : (t + 1) * WIDTH], mine)
    load.wait()
    cols = mine.astype(F32) + dot(image, w_ref[...], 1, 1)
    out_ref[...] = jnp.zeros_like(out_ref)
    out_ref[:REF_ROWS, :] = cols.astype(BF16)


def ref_cols(at, image, wr):
    vmem = pl.BlockSpec(memory_space=pltpu.VMEM)
    return pl.pallas_call(
        cols_kernel,
        out_shape=jax.ShapeDtypeStruct((16, WIDTH), BF16),
        in_specs=[
            pl.BlockSpec(memory_space=pltpu.SMEM), vmem, pl.BlockSpec(memory_space=pltpu.HBM)
        ],
        out_specs=vmem,
        scratch_shapes=[
            pltpu.VMEM((WIDTH, 4 * WIDTH), BF16),
            pltpu.SemaphoreType.DMA((1,)),
        ],
        compiler_params=pltpu.CompilerParams(vmem_limit_bytes=8 * 1024 * 1024),
    )(at.reshape(1), image, pltpu.with_memory_space_constraint(wr, pltpu.HBM))


def ref_kernel(g_ref, wk_in, wv_in, out_ref, rows_ref, wk_ref, wv_ref, sem):
    loads = [
        pltpu.make_async_copy(a, b, sem.at[i])
        for i, (a, b) in enumerate(((wk_in, wk_ref), (wv_in, wv_ref)))
    ]
    for load in loads:
        load.start()
    hidden = [g_ref[t].astype(F32) for t in range(4)]
    hidden = jnp.concatenate(hidden, axis=1).astype(BF16)
    rows_ref[...] = jnp.zeros_like(rows_ref)
    pair = []
    for load, w_ref in zip(loads, (wk_ref, wv_ref)):
        load.wait()
        pair.append(dot(hidden, w_ref[...], 1, 1))
    pair = jnp.concatenate(pair, axis=1)
    for row in range(REF_ROWS):
        for group in range(GROUPS):
            at = row * GROUPS + group
            rows_ref[at : at + 1, :] = pair[row : row + 1, LANES * group : LANES * (group + 1)]
    out_ref[...] = jnp.broadcast_to(rows_ref[...].astype(BF16)[None], out_ref.shape)


def ref_pair(gathered, wk, wv):
    hbm, vmem = [pl.BlockSpec(memory_space=space) for space in (pltpu.HBM, pltpu.VMEM)]
    return pl.pallas_call(
        ref_kernel,
        out_shape=jax.ShapeDtypeStruct((N_SECOND, 16, LANES), BF16),
        in_specs=[vmem, hbm, hbm],
        out_specs=vmem,
        scratch_shapes=[pltpu.VMEM((16, LANES), F32)]
        + [pltpu.VMEM((WIDTH, 4 * WIDTH), BF16)] * 2
        + [pltpu.SemaphoreType.DMA((2,))],
        compiler_params=pltpu.CompilerParams(vmem_limit_bytes=12 * 1024 * 1024),
    )(gathered, *[pltpu.with_memory_space_constraint(a, pltpu.HBM) for a in (wk, wv)])


def attention_kernel(
    q_in, k_in, v_in, tok_in, pair_ref, gt_ref, ot_out, dq_out, dk_out, dv_out, pack_out,
    q_ref, k_ref, v_ref, tok_ref, wide_ref, r_ref, dqt_ref, dw_ref,
    ot_ref, dq_ref, dk_ref, dv_ref, pack_ref, in_sem, out_sem,
):
    pairs = ((k_in, k_ref), (q_in, q_ref), (v_in, v_ref), (tok_in, tok_ref))
    loads = [pltpu.make_async_copy(a, b, in_sem.at[i]) for i, (a, b) in enumerate(pairs)]
    for load in loads:
        load.start()
    wide_ref[...] = pair_ref[...].astype(F32)
    for row in range(REF_ROWS):
        for group in range(GROUPS):
            r_ref[N_FRAMES * row : N_FRAMES * (row + 1), LANES * group : LANES * (group + 1)] = (
                wide_ref[pl.ds(row * GROUPS + group, N_FRAMES, stride=16), :].astype(BF16)
            )
    g_all = gt_ref[...].astype(F32).T.astype(BF16)
    for load in loads[:3]:
        load.wait()
    def scores(head):
        lo, hi = head * E, head * E + E
        q = q_ref[:, lo:hi]
        k = jnp.concatenate([k_ref[:, lo:hi], r_ref[:, lo:hi]], 0)
        v = jnp.concatenate([v_ref[:, lo:hi], r_ref[:, WIDTH + lo : WIDTH + hi]], 0)
        return k, v, q, dot(k, q, 1, 1), dot(v, gt_ref[lo:hi, :], 1, 0)

    def soften(k, v, q, s, dp):
        e = jnp.exp2((s - jnp.max(s, axis=0, keepdims=True)) * (SCALE * math.log2(math.e)))
        inv = 1.0 / jnp.sum(e, axis=0, keepdims=True)
        mean = jnp.sum(e * dp, axis=0, keepdims=True) * inv
        p = e * inv
        return k, v, q, p.astype(BF16), (p * (dp - mean)).astype(BF16)

    def write(head, k, v, q, p_low, ds):
        lo, hi = head * E, head * E + E
        ot_ref[lo:hi, :] = dot(v, p_low, 0, 0).astype(BF16)
        dqt_ref[lo:hi, :] = dot(k, ds, 0, 0) * SCALE
        dk = dot(ds, q, 1, 0) * SCALE
        dv = dot(p_low, g_all[:, lo:hi], 1, 0)
        dk_ref[:, lo:hi] = dk[:P_SIZE].astype(BF16)
        dv_ref[:, lo:hi] = dv[:P_SIZE].astype(BF16)
        for col, part in ((lo, dk), (WIDTH + lo, dv)):
            for chunk in range(N_FIRST):
                for row in range(REF_ROWS):
                    at = P_SIZE + N_FRAMES * row + N_SECOND * chunk
                    to = N_SECOND * row
                    pack_ref[chunk, to : to + N_SECOND, col : col + E] = part[
                        at : at + N_SECOND
                    ].astype(BF16)

    ahead = scores(0)
    for head in range(HEADS):
        now = ahead
        if head + 1 < HEADS:
            ahead = scores(head + 1)
        write(head, *soften(*now))
    dq = dqt_ref[...].T.astype(BF16)
    dq_ref[...] = dq
    loads[3].wait()
    pairs = ((ot_ref, ot_out), (dq_ref, dq_out), (dk_ref, dk_out), (dv_ref, dv_out))
    stores = [pltpu.make_async_copy(a, b, out_sem.at[N_FIRST + i]) for i, (a, b) in enumerate(pairs)]
    for store in stores:
        store.start()
    for x in range(4):
        dw = dot(tok_ref[x * WIDTH : (x + 1) * WIDTH, :], dq, 1, 0)
        dw_ref[0], dw_ref[1] = dw[:, :LANES], dw[:, LANES : 2 * LANES]
        dw_ref[2, :, :E] = dw[:, 2 * LANES :]
        for row in range(HALF_ROWS):
            left, right = [
                [dw_ref[group, pl.ds(first, 32, stride=ROWS_OUT), :] for group in range(3)]
                for first in (row, row + HALF_ROWS)
            ]
            last = jnp.concatenate([left[2][:, :E], right[2][:, :E]], axis=1)
            at = N_SECOND * (REF_ROWS + row)
            for group, part in enumerate((left[0], left[1], right[0], right[1], last)):
                for low in range(2):
                    pack_ref[
                        2 * x + low, at : at + N_SECOND, LANES * group : LANES * (group + 1)
                    ] = pick(part, low).astype(BF16)
        for chunk in (2 * x, 2 * x + 1):
            stores.append(
                pltpu.make_async_copy(pack_ref.at[chunk], pack_out.at[chunk], out_sem.at[chunk])
            )
            stores[-1].start()
    for store in stores:
        store.wait()


def attention(q, k, v, pair, gt, tok):
    hbm, vmem = [pl.BlockSpec(memory_space=space) for space in (pltpu.HBM, pltpu.VMEM)]
    rows = REF_ROWS + HALF_ROWS
    return pl.pallas_call(
        attention_kernel,
        out_shape=(pltpu.HBM((WIDTH, P_SIZE), BF16),)
        + (pltpu.HBM((P_SIZE, WIDTH), BF16),) * 3
        + (pltpu.HBM((N_FIRST, N_SECOND * rows, 2 * WIDTH), BF16),),
        in_specs=[hbm] * 4 + [vmem] * 2,
        out_specs=[hbm] * 5,
        scratch_shapes=[pltpu.VMEM((P_SIZE, WIDTH), BF16)] * 3
        + [
            pltpu.VMEM((4 * WIDTH, P_SIZE), BF16),
            pltpu.VMEM((N_FRAMES * 16, LANES), F32),
            pltpu.VMEM((P_SIZE, 2 * WIDTH), BF16),
            pltpu.VMEM((WIDTH, P_SIZE), F32),
            pltpu.VMEM((3, WIDTH, LANES), F32),
            pltpu.VMEM((WIDTH, P_SIZE), BF16),
            pltpu.VMEM((P_SIZE, WIDTH), BF16),
            pltpu.VMEM((P_SIZE, WIDTH), BF16),
            pltpu.VMEM((P_SIZE, WIDTH), BF16),
            pltpu.VMEM((N_FIRST, N_SECOND * rows, 2 * WIDTH), BF16),
            pltpu.SemaphoreType.DMA((4,)),
            pltpu.SemaphoreType.DMA((N_FIRST + 4,)),
        ],
        compiler_params=pltpu.CompilerParams(vmem_limit_bytes=VMEM_BYTES),
    )(*[pltpu.with_memory_space_constraint(a, pltpu.HBM) for a in (q, k, v, tok)], pair, gt)


def token_kernel(
    core_ref, dq_in, dk_in, dv_in, wq_in, wk_in, wv_in, kept_out, sent_out,
    dq_ref, dk_ref, dv_ref, wq_ref, wk_ref, wv_ref, kept_ref, sent_ref, in_sem, out_sem,
):
    pairs = (
        (wq_in, wq_ref), (dq_in, dq_ref), (wk_in, wk_ref),
        (dk_in, dk_ref), (wv_in, wv_ref), (dv_in, dv_ref),
    )
    loads = [pltpu.make_async_copy(a, b, in_sem.at[i]) for i, (a, b) in enumerate(pairs)]
    for load in loads:
        load.start()
    core = core_ref[0]
    total = None
    for i, (d_ref, w_ref) in enumerate(((dq_ref, wq_ref), (dk_ref, wk_ref), (dv_ref, wv_ref))):
        loads[2 * i].wait()
        loads[2 * i + 1].wait()
        part = dot(d_ref[...], w_ref[...], 1, 0)
        total = part if total is None else total + part
    total = total.T.astype(BF16)
    stores = []
    for half in range(2):
        zero, one = [total[(2 * half + c) * WIDTH : (2 * half + c + 1) * WIDTH] for c in range(2)]
        sent_ref[half] = jnp.where(core == 0, one, zero)
        kept_ref[half] = jnp.where(core == 0, zero, one)
        for i, (a, b) in enumerate(((sent_ref, sent_out), (kept_ref, kept_out))):
            store = pltpu.make_async_copy(a.at[half], b.at[half], out_sem.at[2 * half + i])
            store.start()
            stores.append(store)
    for store in stores:
        store.wait()


def token_parts(core, dq, dk, dv, wq, wk, wv):
    hbm = pl.BlockSpec(memory_space=pltpu.HBM)
    return pl.pallas_call(
        token_kernel,
        out_shape=(pltpu.HBM((2, WIDTH, P_SIZE), BF16),) * 2,
        in_specs=[pl.BlockSpec(memory_space=pltpu.SMEM)] + [hbm] * 6,
        out_specs=[hbm] * 2,
        scratch_shapes=[pltpu.VMEM((P_SIZE, WIDTH), BF16)] * 3
        + [pltpu.VMEM((WIDTH, 4 * WIDTH), BF16)] * 3
        + [pltpu.VMEM((2, WIDTH, P_SIZE), BF16)] * 2
        + [pltpu.SemaphoreType.DMA((6,)), pltpu.SemaphoreType.DMA((4,))],
        cost_estimate=pl.CostEstimate(flops=1, bytes_accessed=1, transcendentals=0),
        compiler_params=pltpu.CompilerParams(vmem_limit_bytes=VMEM_BYTES),
    )(
        core.reshape(1),
        *[pltpu.with_memory_space_constraint(a, pltpu.HBM) for a in (dq, dk, dv, wq, wk, wv)],
    )


def combine_kernel(half_ref, pair_ref, got_ref, out_ref):
    mine = jnp.where(half_ref[0] == 0, pair_ref[0].astype(F32), pair_ref[1].astype(F32))
    out_ref[...] = (mine + got_ref[...].astype(F32)).astype(BF16)


def combine(half, paired, got):
    vmem = pl.BlockSpec(memory_space=pltpu.VMEM)
    return pl.pallas_call(
        combine_kernel,
        out_shape=jax.ShapeDtypeStruct((WIDTH, P_SIZE), BF16),
        in_specs=[pl.BlockSpec(memory_space=pltpu.SMEM)] + [vmem] * 2,
        out_specs=vmem,
        cost_estimate=LONG,
        compiler_params=pltpu.CompilerParams(vmem_limit_bytes=8 * 1024 * 1024),
    )(half.reshape(1), paired, got)


def regroup_kernel(in_ref, out_ref, held_ref):
    rows = REF_ROWS + HALF_ROWS
    for row in range(rows):
        at = N_SECOND * row
        part = in_ref[0, at : at + N_SECOND, :].astype(F32)
        for x in range(1, N_FIRST):
            part = part + in_ref[x, at : at + N_SECOND, :].astype(F32)
        for group in range(GROUPS):
            held_ref[group, pl.ds(row, N_SECOND, stride=rows), :] = part[
                :, LANES * group : LANES * (group + 1)
            ]
    for group in range(GROUPS):
        out_ref[:, LANES * group : LANES * (group + 1)] = held_ref[group].astype(BF16)


def regroup(parts):
    rows = REF_ROWS + HALF_ROWS
    return pl.pallas_call(
        regroup_kernel,
        out_shape=jax.ShapeDtypeStruct((N_SECOND * rows, 2 * WIDTH), BF16),
        scratch_shapes=[pltpu.VMEM((GROUPS, N_SECOND * rows, LANES), F32)],
        cost_estimate=LONG,
        compiler_params=pltpu.CompilerParams(vmem_limit_bytes=8 * 1024 * 1024),
    )(parts)


def finish_kernel(in_ref, grad_ref, key_ref, value_ref):
    total = in_ref[0].astype(F32)
    for j in range(1, N_SECOND):
        total = total + in_ref[j].astype(F32)
    key_ref[...] = total[:REF_ROWS, :WIDTH].astype(BF16)
    value_ref[...] = total[:REF_ROWS, WIDTH:].astype(BF16)
    low, tail = total[:, : 4 * LANES], total[:, 4 * LANES :]
    left = jnp.concatenate([low[:, : 2 * LANES], tail[:, :E]], axis=1)
    right = jnp.concatenate([low[:, 2 * LANES :], tail[:, E:]], axis=1)
    grad_ref[:HALF_ROWS, :] = left[REF_ROWS:]
    grad_ref[HALF_ROWS:, :] = right[REF_ROWS:]


def finish(parts):
    return pl.pallas_call(
        finish_kernel,
        out_shape=(
            jax.ShapeDtypeStruct((ROWS_OUT, WIDTH), F32),
            jax.ShapeDtypeStruct((REF_ROWS, WIDTH), BF16),
            jax.ShapeDtypeStruct((REF_ROWS, WIDTH), BF16),
        ),
        compiler_params=pltpu.CompilerParams(vmem_limit_bytes=8 * 1024 * 1024),
    )(parts)


def per_device(
    tokens, reference_image, query_weight, key_weight, value_weight, ref_weight, cotangent
):
    core, half = lax.axis_index("c"), lax.axis_index("h")
    swap = [(0, 1), (1, 0)]
    wq, wk, wv = query_weight.T, key_weight.T, value_weight.T
    cols = ref_cols(2 * half + core, reference_image, ref_weight.T)
    ref_hidden = lax.all_gather(cols, TENSOR, axis=0, tiled=False)
    ref_hidden, own = lax.optimization_barrier((ref_hidden, tokens.T))
    other = lax.ppermute(own, "h", swap)
    pair = ref_pair(ref_hidden, wk, wv)
    pair = lax.all_to_all(pair, SECOND, 0, 0, tiled=True).reshape(N_SECOND * 16, LANES)
    blocks = stack(own, other)
    pair = lax.all_to_all(spread(pair), FIRST, 0, 0, tiled=True)
    parts = lax.all_gather(blocks, "c", axis=0, tiled=False)
    tok, queries, keys, values = project(half, parts, wq, wk, wv)
    attended, query_grads, key_grads, value_grads, pack = attention(
        queries, keys, values, pair.reshape(N_FRAMES * 16, LANES), cotangent.T, tok
    )
    pack = lax.all_to_all(pack, FIRST, 0, 0, tiled=True)
    kept, sent = token_parts(core, query_grads, key_grads, value_grads, wq, wk, wv)
    got = lax.ppermute(sent, "c", swap)
    paired = (kept.astype(F32) + got.astype(F32)).astype(BF16)
    sent = lax.dynamic_index_in_dim(paired, 1 - half, 0, False)
    got = lax.ppermute(sent, "h", swap)
    token_grads = combine(half, paired, got).T
    pack = regroup(pack)
    pack = pack.reshape(N_SECOND, REF_ROWS + HALF_ROWS, 2 * WIDTH)
    pack = lax.all_to_all(pack, SECOND, 0, 0, tiled=True)
    query_weight_grad, ref_key_grads, ref_value_grads = finish(pack)
    return attended.T, token_grads, query_weight_grad, ref_key_grads, ref_value_grads


def solution(mesh):
    mesh = Mesh(mesh.devices.reshape(4, 4, 2, 4, 2, 2), FRAMES + TENSOR)
    return jax.shard_map(
        per_device,
        mesh=mesh,
        in_specs=(
            P(FRAMES, TENSOR),
            P(FRAMES, None),
            P(None, TENSOR),
            P(None, TENSOR),
            P(None, TENSOR),
            P(None, TENSOR),
            P(FRAMES, TENSOR),
        ),
        out_specs=(P(FRAMES, TENSOR),) * 5,
        check_vma=False,
    )
```

```python
import math

import jax
import jax.numpy as jnp
from jax import lax
from jax.experimental import pallas as pl
from jax.experimental.pallas import tpu as pltpu
from jax.sharding import Mesh
from jax.sharding import PartitionSpec as P

E = 64
P_SIZE = 384
HEADS = 5
WIDTH = HEADS * E
FRAMES = ("x", "yh", "yl", "z")
FIRST = ("x", "yl")
SECOND = ("yh", "z")
TENSOR = ("h", "c")
N_FIRST, N_SECOND = 8, 16
N_FRAMES = N_FIRST * N_SECOND
REF_ROWS = 3
ROWS_OUT = 10
HALF_ROWS = ROWS_OUT // 2
LANES = 128
LONG = pl.CostEstimate(flops=10**10, bytes_accessed=10**10, transcendentals=0)
VMEM_BYTES = 24 * 1024 * 1024
GROUPS = 2 * WIDTH // LANES
SCALE = 1.0 / math.sqrt(E)
F32 = jnp.float32
BF16 = jnp.bfloat16


def pick(rows, low):
    return jnp.concatenate([rows[8 * i + 4 * low : 8 * i + 4 * low + 4] for i in range(4)], axis=0)


def dot(a, b, a_dim, b_dim):
    return lax.dot_general(a, b, (((a_dim,), (b_dim,)), ((), ())), preferred_element_type=F32)


def spread_kernel(in_ref, out_ref, sem):
    copies = [pltpu.make_async_copy(in_ref, out_ref.at[i], sem.at[i]) for i in range(N_FIRST)]
    for copy in copies:
        copy.start()
    for copy in copies:
        copy.wait()


def spread(pair):
    return pl.pallas_call(
        spread_kernel,
        out_shape=pltpu.HBM((N_FIRST,) + pair.shape, BF16),
        out_specs=pl.BlockSpec(memory_space=pltpu.HBM),
        scratch_shapes=[pltpu.SemaphoreType.DMA((N_FIRST,))],
        cost_estimate=LONG,
        compiler_params=pltpu.CompilerParams(vmem_limit_bytes=8 * 1024 * 1024),
    )(pair)


def stack_kernel(own_ref, other_ref, out_ref):
    out_ref[0] = own_ref[...]
    out_ref[1] = other_ref[...]


def stack(own, other):
    return pl.pallas_call(
        stack_kernel,
        out_shape=jax.ShapeDtypeStruct((2, WIDTH, P_SIZE), BF16),
        cost_estimate=LONG,
        compiler_params=pltpu.CompilerParams(vmem_limit_bytes=8 * 1024 * 1024),
    )(own, other)


def project_kernel(
    half_ref, t_ref, wq_ref, wk_ref, wv_ref, tok_out, q_out, k_out, v_out,
    tok_ref, q_ref, k_ref, v_ref, sem,
):
    half = half_ref[0]
    pairs = ((tok_ref, tok_out), (q_ref, q_out), (k_ref, k_out), (v_ref, v_out))
    copies = [pltpu.make_async_copy(a, b, sem.at[i]) for i, (a, b) in enumerate(pairs)]
    for core in range(2):
        for slot in range(2):
            at = pl.multiple_of((2 * lax.rem(half + slot, 2) + core) * WIDTH, E)
            tok_ref[pl.ds(at, WIDTH), :] = t_ref[core, slot]
    copies[0].start()
    tok = tok_ref[...]
    for i, (w_ref, out_ref) in enumerate(((wq_ref, q_ref), (wk_ref, k_ref), (wv_ref, v_ref))):
        out_ref[...] = dot(w_ref[...], tok, 1, 0).T.astype(BF16)
        copies[i + 1].start()
    for copy in copies:
        copy.wait()


def project(half, parts, wq, wk, wv):
    vmem = pl.BlockSpec(memory_space=pltpu.VMEM)
    return pl.pallas_call(
        project_kernel,
        out_shape=(pltpu.HBM((4 * WIDTH, P_SIZE), BF16),)
        + (pltpu.HBM((P_SIZE, WIDTH), BF16),) * 3,
        in_specs=[pl.BlockSpec(memory_space=pltpu.SMEM)] + [vmem] * 4,
        out_specs=[pl.BlockSpec(memory_space=pltpu.HBM)] * 4,
        scratch_shapes=[pltpu.VMEM((4 * WIDTH, P_SIZE), BF16)]
        + [pltpu.VMEM((P_SIZE, WIDTH), BF16)] * 3
        + [pltpu.SemaphoreType.DMA((4,))],
        compiler_params=pltpu.CompilerParams(vmem_limit_bytes=VMEM_BYTES),
    )(half.reshape(1), parts, wq, wk, wv)


def cols_kernel(at_ref, r_ref, w_in, out_ref, w_ref, sem):
    load = pltpu.make_async_copy(w_in, w_ref, sem.at[0])
    load.start()
    image = r_ref[...]
    mine = image[:, :WIDTH]
    for t in range(1, 4):
        mine = jnp.where(at_ref[0] == t, image[:, t * WIDTH : (t + 1) * WIDTH], mine)
    load.wait()
    cols = mine.astype(F32) + dot(image, w_ref[...], 1, 1)
    out_ref[...] = jnp.zeros_like(out_ref)
    out_ref[:REF_ROWS, :] = cols.astype(BF16)


def ref_cols(at, image, wr):
    vmem = pl.BlockSpec(memory_space=pltpu.VMEM)
    return pl.pallas_call(
        cols_kernel,
        out_shape=jax.ShapeDtypeStruct((16, WIDTH), BF16),
        in_specs=[
            pl.BlockSpec(memory_space=pltpu.SMEM), vmem, pl.BlockSpec(memory_space=pltpu.HBM)
        ],
        out_specs=vmem,
        scratch_shapes=[
            pltpu.VMEM((WIDTH, 4 * WIDTH), BF16),
            pltpu.SemaphoreType.DMA((1,)),
        ],
        compiler_params=pltpu.CompilerParams(vmem_limit_bytes=8 * 1024 * 1024),
    )(at.reshape(1), image, pltpu.with_memory_space_constraint(wr, pltpu.HBM))


def ref_kernel(g_ref, wk_in, wv_in, out_ref, rows_ref, wk_ref, wv_ref, sem):
    loads = [
        pltpu.make_async_copy(a, b, sem.at[i])
        for i, (a, b) in enumerate(((wk_in, wk_ref), (wv_in, wv_ref)))
    ]
    for load in loads:
        load.start()
    hidden = [g_ref[t].astype(F32) for t in range(4)]
    hidden = jnp.concatenate(hidden, axis=1).astype(BF16)
    rows_ref[...] = jnp.zeros_like(rows_ref)
    pair = []
    for load, w_ref in zip(loads, (wk_ref, wv_ref)):
        load.wait()
        pair.append(dot(hidden, w_ref[...], 1, 1))
    pair = jnp.concatenate(pair, axis=1)
    for row in range(REF_ROWS):
        for group in range(GROUPS):
            at = row * GROUPS + group
            rows_ref[at : at + 1, :] = pair[row : row + 1, LANES * group : LANES * (group + 1)]
    out_ref[...] = jnp.broadcast_to(rows_ref[...].astype(BF16)[None], out_ref.shape)


def ref_pair(gathered, wk, wv):
    hbm, vmem = [pl.BlockSpec(memory_space=space) for space in (pltpu.HBM, pltpu.VMEM)]
    return pl.pallas_call(
        ref_kernel,
        out_shape=jax.ShapeDtypeStruct((N_SECOND, 16, LANES), BF16),
        in_specs=[vmem, hbm, hbm],
        out_specs=vmem,
        scratch_shapes=[pltpu.VMEM((16, LANES), F32)]
        + [pltpu.VMEM((WIDTH, 4 * WIDTH), BF16)] * 2
        + [pltpu.SemaphoreType.DMA((2,))],
        compiler_params=pltpu.CompilerParams(vmem_limit_bytes=12 * 1024 * 1024),
    )(gathered, *[pltpu.with_memory_space_constraint(a, pltpu.HBM) for a in (wk, wv)])


def attention_kernel(
    q_in, k_in, v_in, tok_in, pair_ref, gt_ref, ot_out, grads_out, pack_out,
    q_ref, k_ref, v_ref, tok_ref, wide_ref, r_ref, dqt_ref, dw_ref,
    ot_ref, grads_ref, pack_ref, in_sem, out_sem,
):
    pairs = ((k_in, k_ref), (q_in, q_ref), (v_in, v_ref), (tok_in, tok_ref))
    loads = [pltpu.make_async_copy(a, b, in_sem.at[i]) for i, (a, b) in enumerate(pairs)]
    for load in loads:
        load.start()
    wide_ref[...] = pair_ref[...].astype(F32)
    for row in range(REF_ROWS):
        for group in range(GROUPS):
            r_ref[N_FRAMES * row : N_FRAMES * (row + 1), LANES * group : LANES * (group + 1)] = (
                wide_ref[pl.ds(row * GROUPS + group, N_FRAMES, stride=16), :].astype(BF16)
            )
    g_all = gt_ref[...].astype(F32).T.astype(BF16)
    for load in loads[:3]:
        load.wait()
    def scores(head):
        lo, hi = head * E, head * E + E
        q = q_ref[:, lo:hi]
        k = jnp.concatenate([k_ref[:, lo:hi], r_ref[:, lo:hi]], 0)
        v = jnp.concatenate([v_ref[:, lo:hi], r_ref[:, WIDTH + lo : WIDTH + hi]], 0)
        return k, v, q, dot(k, q, 1, 1), dot(v, gt_ref[lo:hi, :], 1, 0)

    def soften(k, v, q, s, dp):
        e = jnp.exp2((s - jnp.max(s, axis=0, keepdims=True)) * (SCALE * math.log2(math.e)))
        inv = 1.0 / jnp.sum(e, axis=0, keepdims=True)
        mean = jnp.sum(e * dp, axis=0, keepdims=True) * inv
        p = e * inv
        return k, v, q, p.astype(BF16), (p * (dp - mean)).astype(BF16)

    def write(head, k, v, q, p_low, ds):
        lo, hi = head * E, head * E + E
        ot_ref[lo:hi, :] = dot(v, p_low, 0, 0).astype(BF16)
        dqt_ref[lo:hi, :] = dot(k, ds, 0, 0) * SCALE
        dk = dot(ds, q, 1, 0) * SCALE
        dv = dot(p_low, g_all[:, lo:hi], 1, 0)
        grads_ref[:, WIDTH + lo : WIDTH + hi] = dk[:P_SIZE].astype(BF16)
        grads_ref[:, 2 * WIDTH + lo : 2 * WIDTH + hi] = dv[:P_SIZE].astype(BF16)
        for col, part in ((lo, dk), (WIDTH + lo, dv)):
            for chunk in range(N_FIRST):
                for row in range(REF_ROWS):
                    at = P_SIZE + N_FRAMES * row + N_SECOND * chunk
                    to = N_SECOND * row
                    pack_ref[chunk, to : to + N_SECOND, col : col + E] = part[
                        at : at + N_SECOND
                    ].astype(BF16)

    ahead = scores(0)
    for head in range(HEADS):
        now = ahead
        if head + 1 < HEADS:
            ahead = scores(head + 1)
        write(head, *soften(*now))
    dq = dqt_ref[...].T.astype(BF16)
    grads_ref[:, :WIDTH] = dq
    loads[3].wait()
    pairs = ((ot_ref, ot_out), (grads_ref, grads_out))
    stores = [pltpu.make_async_copy(a, b, out_sem.at[N_FIRST + i]) for i, (a, b) in enumerate(pairs)]
    for store in stores:
        store.start()
    for x in range(4):
        dw = dot(tok_ref[x * WIDTH : (x + 1) * WIDTH, :], dq, 1, 0)
        dw_ref[0], dw_ref[1] = dw[:, :LANES], dw[:, LANES : 2 * LANES]
        dw_ref[2, :, :E] = dw[:, 2 * LANES :]
        for row in range(HALF_ROWS):
            left, right = [
                [dw_ref[group, pl.ds(first, 32, stride=ROWS_OUT), :] for group in range(3)]
                for first in (row, row + HALF_ROWS)
            ]
            last = jnp.concatenate([left[2][:, :E], right[2][:, :E]], axis=1)
            at = N_SECOND * (REF_ROWS + row)
            for group, part in enumerate((left[0], left[1], right[0], right[1], last)):
                for low in range(2):
                    pack_ref[
                        2 * x + low, at : at + N_SECOND, LANES * group : LANES * (group + 1)
                    ] = pick(part, low).astype(BF16)
        for chunk in (2 * x, 2 * x + 1):
            stores.append(
                pltpu.make_async_copy(pack_ref.at[chunk], pack_out.at[chunk], out_sem.at[chunk])
            )
            stores[-1].start()
    for store in stores:
        store.wait()


def attention(q, k, v, pair, gt, tok):
    hbm, vmem = [pl.BlockSpec(memory_space=space) for space in (pltpu.HBM, pltpu.VMEM)]
    rows = REF_ROWS + HALF_ROWS
    return pl.pallas_call(
        attention_kernel,
        out_shape=(pltpu.HBM((WIDTH, P_SIZE), BF16),)
        + (pltpu.HBM((P_SIZE, 3 * WIDTH), BF16),)
        + (pltpu.HBM((N_FIRST, N_SECOND * rows, 2 * WIDTH), BF16),),
        in_specs=[hbm] * 4 + [vmem] * 2,
        out_specs=[hbm] * 3,
        scratch_shapes=[pltpu.VMEM((P_SIZE, WIDTH), BF16)] * 3
        + [
            pltpu.VMEM((4 * WIDTH, P_SIZE), BF16),
            pltpu.VMEM((N_FRAMES * 16, LANES), F32),
            pltpu.VMEM((P_SIZE, 2 * WIDTH), BF16),
            pltpu.VMEM((WIDTH, P_SIZE), F32),
            pltpu.VMEM((3, WIDTH, LANES), F32),
            pltpu.VMEM((WIDTH, P_SIZE), BF16),
            pltpu.VMEM((P_SIZE, 3 * WIDTH), BF16),
            pltpu.VMEM((N_FIRST, N_SECOND * rows, 2 * WIDTH), BF16),
            pltpu.SemaphoreType.DMA((4,)),
            pltpu.SemaphoreType.DMA((N_FIRST + 2,)),
        ],
        compiler_params=pltpu.CompilerParams(vmem_limit_bytes=VMEM_BYTES),
    )(*[pltpu.with_memory_space_constraint(a, pltpu.HBM) for a in (q, k, v, tok)], pair, gt)


def token_kernel(
    core_ref, grads_in, wq_in, wk_in, wv_in, kept_out, sent_out,
    grads_ref, w_ref, kept_ref, sent_ref, in_sem, out_sem,
):
    pairs = [(grads_in, grads_ref)]
    for i, w_in in enumerate((wq_in, wk_in, wv_in)):
        pairs.append((w_in, w_ref.at[pl.ds(i * WIDTH, WIDTH)]))
    loads = [pltpu.make_async_copy(a, b, in_sem.at[i]) for i, (a, b) in enumerate(pairs)]
    for load in loads:
        load.start()
    core = core_ref[0]
    for load in loads:
        load.wait()
    total = dot(grads_ref[...], w_ref[...], 1, 0)
    total = total.T.astype(BF16)
    stores = []
    for half in range(2):
        zero, one = [total[(2 * half + c) * WIDTH : (2 * half + c + 1) * WIDTH] for c in range(2)]
        sent_ref[half] = jnp.where(core == 0, one, zero)
        kept_ref[half] = jnp.where(core == 0, zero, one)
        for i, (a, b) in enumerate(((sent_ref, sent_out), (kept_ref, kept_out))):
            store = pltpu.make_async_copy(a.at[half], b.at[half], out_sem.at[2 * half + i])
            store.start()
            stores.append(store)
    for store in stores:
        store.wait()


def token_parts(core, grads, wq, wk, wv):
    hbm = pl.BlockSpec(memory_space=pltpu.HBM)
    return pl.pallas_call(
        token_kernel,
        out_shape=(pltpu.HBM((2, WIDTH, P_SIZE), BF16),) * 2,
        in_specs=[pl.BlockSpec(memory_space=pltpu.SMEM)] + [hbm] * 4,
        out_specs=[hbm] * 2,
        scratch_shapes=[
            pltpu.VMEM((P_SIZE, 3 * WIDTH), BF16),
            pltpu.VMEM((3 * WIDTH, 4 * WIDTH), BF16),
        ]
        + [pltpu.VMEM((2, WIDTH, P_SIZE), BF16)] * 2
        + [pltpu.SemaphoreType.DMA((4,)), pltpu.SemaphoreType.DMA((4,))],
        cost_estimate=pl.CostEstimate(flops=1, bytes_accessed=1, transcendentals=0),
        compiler_params=pltpu.CompilerParams(vmem_limit_bytes=VMEM_BYTES),
    )(
        core.reshape(1),
        *[pltpu.with_memory_space_constraint(a, pltpu.HBM) for a in (grads, wq, wk, wv)],
    )


def combine_kernel(half_ref, pair_ref, got_ref, out_ref):
    mine = jnp.where(half_ref[0] == 0, pair_ref[0].astype(F32), pair_ref[1].astype(F32))
    out_ref[...] = (mine + got_ref[...].astype(F32)).astype(BF16)


def combine(half, paired, got):
    vmem = pl.BlockSpec(memory_space=pltpu.VMEM)
    return pl.pallas_call(
        combine_kernel,
        out_shape=jax.ShapeDtypeStruct((WIDTH, P_SIZE), BF16),
        in_specs=[pl.BlockSpec(memory_space=pltpu.SMEM)] + [vmem] * 2,
        out_specs=vmem,
        cost_estimate=LONG,
        compiler_params=pltpu.CompilerParams(vmem_limit_bytes=8 * 1024 * 1024),
    )(half.reshape(1), paired, got)


def regroup_kernel(in_ref, out_ref, held_ref):
    rows = REF_ROWS + HALF_ROWS
    for row in range(rows):
        at = N_SECOND * row
        part = in_ref[0, at : at + N_SECOND, :].astype(F32)
        for x in range(1, N_FIRST):
            part = part + in_ref[x, at : at + N_SECOND, :].astype(F32)
        for group in range(GROUPS):
            held_ref[group, pl.ds(row, N_SECOND, stride=rows), :] = part[
                :, LANES * group : LANES * (group + 1)
            ]
    for group in range(GROUPS):
        out_ref[:, LANES * group : LANES * (group + 1)] = held_ref[group].astype(BF16)


def regroup(parts):
    rows = REF_ROWS + HALF_ROWS
    return pl.pallas_call(
        regroup_kernel,
        out_shape=jax.ShapeDtypeStruct((N_SECOND * rows, 2 * WIDTH), BF16),
        scratch_shapes=[pltpu.VMEM((GROUPS, N_SECOND * rows, LANES), F32)],
        cost_estimate=LONG,
        compiler_params=pltpu.CompilerParams(vmem_limit_bytes=8 * 1024 * 1024),
    )(parts)


def finish_kernel(in_ref, grad_ref, key_ref, value_ref):
    total = in_ref[0].astype(F32)
    for j in range(1, N_SECOND):
        total = total + in_ref[j].astype(F32)
    key_ref[...] = total[:REF_ROWS, :WIDTH].astype(BF16)
    value_ref[...] = total[:REF_ROWS, WIDTH:].astype(BF16)
    low, tail = total[:, : 4 * LANES], total[:, 4 * LANES :]
    left = jnp.concatenate([low[:, : 2 * LANES], tail[:, :E]], axis=1)
    right = jnp.concatenate([low[:, 2 * LANES :], tail[:, E:]], axis=1)
    grad_ref[:HALF_ROWS, :] = left[REF_ROWS:]
    grad_ref[HALF_ROWS:, :] = right[REF_ROWS:]


def finish(parts):
    return pl.pallas_call(
        finish_kernel,
        out_shape=(
            jax.ShapeDtypeStruct((ROWS_OUT, WIDTH), F32),
            jax.ShapeDtypeStruct((REF_ROWS, WIDTH), BF16),
            jax.ShapeDtypeStruct((REF_ROWS, WIDTH), BF16),
        ),
        compiler_params=pltpu.CompilerParams(vmem_limit_bytes=8 * 1024 * 1024),
    )(parts)


def per_device(
    tokens, reference_image, query_weight, key_weight, value_weight, ref_weight, cotangent
):
    core, half = lax.axis_index("c"), lax.axis_index("h")
    swap = [(0, 1), (1, 0)]
    wq, wk, wv = query_weight.T, key_weight.T, value_weight.T
    cols = ref_cols(2 * half + core, reference_image, ref_weight.T)
    ref_hidden = lax.all_gather(cols, TENSOR, axis=0, tiled=False)
    ref_hidden, own = lax.optimization_barrier((ref_hidden, tokens.T))
    other = lax.ppermute(own, "h", swap)
    pair = ref_pair(ref_hidden, wk, wv)
    pair = lax.all_to_all(pair, SECOND, 0, 0, tiled=True).reshape(N_SECOND * 16, LANES)
    blocks = stack(own, other)
    pair = lax.all_to_all(spread(pair), FIRST, 0, 0, tiled=True)
    parts = lax.all_gather(blocks, "c", axis=0, tiled=False)
    tok, queries, keys, values = project(half, parts, wq, wk, wv)
    attended, grads, pack = attention(
        queries, keys, values, pair.reshape(N_FRAMES * 16, LANES), cotangent.T, tok
    )
    pack = lax.all_to_all(pack, FIRST, 0, 0, tiled=True)
    kept, sent = token_parts(core, grads, wq, wk, wv)
    got = lax.ppermute(sent, "c", swap)
    paired = (kept.astype(F32) + got.astype(F32)).astype(BF16)
    sent = lax.dynamic_index_in_dim(paired, 1 - half, 0, False)
    got = lax.ppermute(sent, "h", swap)
    token_grads = combine(half, paired, got).T
    pack = regroup(pack)
    pack = pack.reshape(N_SECOND, REF_ROWS + HALF_ROWS, 2 * WIDTH)
    pack = lax.all_to_all(pack, SECOND, 0, 0, tiled=True)
    query_weight_grad, ref_key_grads, ref_value_grads = finish(pack)
    return attended.T, token_grads, query_weight_grad, ref_key_grads, ref_value_grads


def solution(mesh):
    mesh = Mesh(mesh.devices.reshape(4, 4, 2, 4, 2, 2), FRAMES + TENSOR)
    return jax.shard_map(
        per_device,
        mesh=mesh,
        in_specs=(
            P(FRAMES, TENSOR),
            P(FRAMES, None),
            P(None, TENSOR),
            P(None, TENSOR),
            P(None, TENSOR),
            P(None, TENSOR),
            P(FRAMES, TENSOR),
        ),
        out_specs=(P(FRAMES, TENSOR),) * 5,
        check_vma=False,
    )
```

```python
import math

import jax
import jax.numpy as jnp
from jax import lax
from jax.experimental import pallas as pl
from jax.experimental.pallas import tpu as pltpu
from jax.sharding import Mesh
from jax.sharding import PartitionSpec as P

E = 64
P_SIZE = 384
HEADS = 5
WIDTH = HEADS * E
FRAMES = ("x", "yh", "yl", "z")
FIRST = ("x", "yl")
SECOND = ("yh", "z")
TENSOR = ("h", "c")
N_FIRST, N_SECOND = 8, 16
N_FRAMES = N_FIRST * N_SECOND
REF_ROWS = 3
ROWS_OUT = 10
HALF_ROWS = ROWS_OUT // 2
LANES = 128
LONG = pl.CostEstimate(flops=10**10, bytes_accessed=10**10, transcendentals=0)
VMEM_BYTES = 24 * 1024 * 1024
GROUPS = 2 * WIDTH // LANES
SCALE = 1.0 / math.sqrt(E)
F32 = jnp.float32
BF16 = jnp.bfloat16


def pick(rows, low):
    return jnp.concatenate([rows[8 * i + 4 * low : 8 * i + 4 * low + 4] for i in range(4)], axis=0)


def dot(a, b, a_dim, b_dim):
    return lax.dot_general(a, b, (((a_dim,), (b_dim,)), ((), ())), preferred_element_type=F32)


def spread_kernel(in_ref, out_ref, sem):
    copies = [pltpu.make_async_copy(in_ref, out_ref.at[i], sem.at[i]) for i in range(N_FIRST)]
    for copy in copies:
        copy.start()
    for copy in copies:
        copy.wait()


def spread(pair):
    return pl.pallas_call(
        spread_kernel,
        out_shape=pltpu.HBM((N_FIRST,) + pair.shape, BF16),
        out_specs=pl.BlockSpec(memory_space=pltpu.HBM),
        scratch_shapes=[pltpu.SemaphoreType.DMA((N_FIRST,))],
        cost_estimate=LONG,
        compiler_params=pltpu.CompilerParams(vmem_limit_bytes=8 * 1024 * 1024),
    )(pair)


def stack_kernel(own_ref, other_ref, out_ref):
    out_ref[0] = own_ref[...]
    out_ref[1] = other_ref[...]


def stack(own, other):
    return pl.pallas_call(
        stack_kernel,
        out_shape=jax.ShapeDtypeStruct((2, WIDTH, P_SIZE), BF16),
        cost_estimate=LONG,
        compiler_params=pltpu.CompilerParams(vmem_limit_bytes=8 * 1024 * 1024),
    )(own, other)


def project_kernel(
    half_ref, t_ref, wq_ref, wk_ref, wv_ref, tok_out, q_out, k_out, v_out,
    tok_ref, q_ref, k_ref, v_ref, sem,
):
    half = half_ref[0]
    pairs = ((tok_ref, tok_out), (q_ref, q_out), (k_ref, k_out), (v_ref, v_out))
    copies = [pltpu.make_async_copy(a, b, sem.at[i]) for i, (a, b) in enumerate(pairs)]
    for core in range(2):
        for slot in range(2):
            at = pl.multiple_of((2 * lax.rem(half + slot, 2) + core) * WIDTH, E)
            tok_ref[pl.ds(at, WIDTH), :] = t_ref[core, slot]
    copies[0].start()
    tok = tok_ref[...]
    for i, (w_ref, out_ref) in enumerate(((wq_ref, q_ref), (wk_ref, k_ref), (wv_ref, v_ref))):
        out_ref[...] = dot(w_ref[...], tok, 1, 0).T.astype(BF16)
        copies[i + 1].start()
    for copy in copies:
        copy.wait()


def project(half, parts, wq, wk, wv):
    vmem = pl.BlockSpec(memory_space=pltpu.VMEM)
    return pl.pallas_call(
        project_kernel,
        out_shape=(pltpu.HBM((4 * WIDTH, P_SIZE), BF16),)
        + (pltpu.HBM((P_SIZE, WIDTH), BF16),) * 3,
        in_specs=[pl.BlockSpec(memory_space=pltpu.SMEM)] + [vmem] * 4,
        out_specs=[pl.BlockSpec(memory_space=pltpu.HBM)] * 4,
        scratch_shapes=[pltpu.VMEM((4 * WIDTH, P_SIZE), BF16)]
        + [pltpu.VMEM((P_SIZE, WIDTH), BF16)] * 3
        + [pltpu.SemaphoreType.DMA((4,))],
        compiler_params=pltpu.CompilerParams(vmem_limit_bytes=VMEM_BYTES),
    )(half.reshape(1), parts, wq, wk, wv)


def cols_kernel(at_ref, r_ref, w_in, out_ref, w_ref, sem):
    load = pltpu.make_async_copy(w_in, w_ref, sem.at[0])
    load.start()
    image = r_ref[...]
    mine = image[:, :WIDTH]
    for t in range(1, 4):
        mine = jnp.where(at_ref[0] == t, image[:, t * WIDTH : (t + 1) * WIDTH], mine)
    load.wait()
    cols = mine.astype(F32) + dot(image, w_ref[...], 1, 1)
    out_ref[...] = jnp.zeros_like(out_ref)
    out_ref[:REF_ROWS, :] = cols.astype(BF16)


def ref_cols(at, image, wr):
    vmem = pl.BlockSpec(memory_space=pltpu.VMEM)
    return pl.pallas_call(
        cols_kernel,
        out_shape=jax.ShapeDtypeStruct((16, WIDTH), BF16),
        in_specs=[
            pl.BlockSpec(memory_space=pltpu.SMEM), vmem, pl.BlockSpec(memory_space=pltpu.HBM)
        ],
        out_specs=vmem,
        scratch_shapes=[
            pltpu.VMEM((WIDTH, 4 * WIDTH), BF16),
            pltpu.SemaphoreType.DMA((1,)),
        ],
        compiler_params=pltpu.CompilerParams(vmem_limit_bytes=8 * 1024 * 1024),
    )(at.reshape(1), image, pltpu.with_memory_space_constraint(wr, pltpu.HBM))


def ref_kernel(half_ref, g_ref, wk_in, wv_in, out_ref, rows_ref, wk_ref, wv_ref, sem):
    loads = [
        pltpu.make_async_copy(a, b, sem.at[i])
        for i, (a, b) in enumerate(((wk_in, wk_ref), (wv_in, wv_ref)))
    ]
    for load in loads:
        load.start()
    first = half_ref[0] == 0
    hidden = []
    for low in range(2):
        for c in range(2):
            own, other = g_ref[c, low].astype(F32), g_ref[c, 1 - low].astype(F32)
            hidden.append(jnp.where(first, own, other))
    hidden = jnp.concatenate(hidden, axis=1).astype(BF16)
    rows_ref[...] = jnp.zeros_like(rows_ref)
    pair = []
    for load, w_ref in zip(loads, (wk_ref, wv_ref)):
        load.wait()
        pair.append(dot(hidden, w_ref[...], 1, 1))
    pair = jnp.concatenate(pair, axis=1)
    for row in range(REF_ROWS):
        for group in range(GROUPS):
            at = row * GROUPS + group
            rows_ref[at : at + 1, :] = pair[row : row + 1, LANES * group : LANES * (group + 1)]
    out_ref[...] = jnp.broadcast_to(rows_ref[...].astype(BF16)[None], out_ref.shape)


def ref_pair(half, gathered, wk, wv):
    hbm, vmem = [pl.BlockSpec(memory_space=space) for space in (pltpu.HBM, pltpu.VMEM)]
    return pl.pallas_call(
        ref_kernel,
        out_shape=jax.ShapeDtypeStruct((N_SECOND, 16, LANES), BF16),
        in_specs=[pl.BlockSpec(memory_space=pltpu.SMEM), vmem, hbm, hbm],
        out_specs=vmem,
        scratch_shapes=[pltpu.VMEM((16, LANES), F32)]
        + [pltpu.VMEM((WIDTH, 4 * WIDTH), BF16)] * 2
        + [pltpu.SemaphoreType.DMA((2,))],
        compiler_params=pltpu.CompilerParams(vmem_limit_bytes=12 * 1024 * 1024),
    )(half.reshape(1), gathered, *[pltpu.with_memory_space_constraint(a, pltpu.HBM) for a in (wk, wv)])


def attention_kernel(
    q_in, k_in, v_in, tok_in, pair_ref, gt_ref, ot_out, grads_out, pack_out,
    q_ref, k_ref, v_ref, tok_ref, wide_ref, r_ref, dqt_ref, dw_ref,
    ot_ref, grads_ref, pack_ref, in_sem, out_sem,
):
    pairs = ((k_in, k_ref), (q_in, q_ref), (v_in, v_ref), (tok_in, tok_ref))
    loads = [pltpu.make_async_copy(a, b, in_sem.at[i]) for i, (a, b) in enumerate(pairs)]
    for load in loads:
        load.start()
    wide_ref[...] = pair_ref[...].astype(F32)
    for row in range(REF_ROWS):
        for group in range(GROUPS):
            r_ref[N_FRAMES * row : N_FRAMES * (row + 1), LANES * group : LANES * (group + 1)] = (
                wide_ref[pl.ds(row * GROUPS + group, N_FRAMES, stride=16), :].astype(BF16)
            )
    g_all = gt_ref[...].astype(F32).T.astype(BF16)
    for load in loads[:3]:
        load.wait()
    def scores(head):
        lo, hi = head * E, head * E + E
        q = q_ref[:, lo:hi]
        k = jnp.concatenate([k_ref[:, lo:hi], r_ref[:, lo:hi]], 0)
        v = jnp.concatenate([v_ref[:, lo:hi], r_ref[:, WIDTH + lo : WIDTH + hi]], 0)
        return k, v, q, dot(k, q, 1, 1), dot(v, gt_ref[lo:hi, :], 1, 0)

    def soften(k, v, q, s, dp):
        e = jnp.exp2((s - jnp.max(s, axis=0, keepdims=True)) * (SCALE * math.log2(math.e)))
        inv = 1.0 / jnp.sum(e, axis=0, keepdims=True)
        mean = jnp.sum(e * dp, axis=0, keepdims=True) * inv
        p = e * inv
        return k, v, q, p.astype(BF16), (p * (dp - mean)).astype(BF16)

    def write(head, k, v, q, p_low, ds):
        lo, hi = head * E, head * E + E
        ot_ref[lo:hi, :] = dot(v, p_low, 0, 0).astype(BF16)
        dqt_ref[lo:hi, :] = dot(k, ds, 0, 0) * SCALE
        dk = dot(ds, q, 1, 0) * SCALE
        dv = dot(p_low, g_all[:, lo:hi], 1, 0)
        grads_ref[:, WIDTH + lo : WIDTH + hi] = dk[:P_SIZE].astype(BF16)
        grads_ref[:, 2 * WIDTH + lo : 2 * WIDTH + hi] = dv[:P_SIZE].astype(BF16)
        for col, part in ((lo, dk), (WIDTH + lo, dv)):
            for chunk in range(N_FIRST):
                for row in range(REF_ROWS):
                    at = P_SIZE + N_FRAMES * row + N_SECOND * chunk
                    to = N_SECOND * row
                    pack_ref[chunk, to : to + N_SECOND, col : col + E] = part[
                        at : at + N_SECOND
                    ].astype(BF16)

    ahead = scores(0)
    for head in range(HEADS):
        now = ahead
        if head + 1 < HEADS:
            ahead = scores(head + 1)
        write(head, *soften(*now))
    dq = dqt_ref[...].T.astype(BF16)
    grads_ref[:, :WIDTH] = dq
    loads[3].wait()
    pairs = ((ot_ref, ot_out), (grads_ref, grads_out))
    stores = [pltpu.make_async_copy(a, b, out_sem.at[N_FIRST + i]) for i, (a, b) in enumerate(pairs)]
    for store in stores:
        store.start()
    for x in range(4):
        dw = dot(tok_ref[x * WIDTH : (x + 1) * WIDTH, :], dq, 1, 0)
        dw_ref[0], dw_ref[1] = dw[:, :LANES], dw[:, LANES : 2 * LANES]
        dw_ref[2, :, :E] = dw[:, 2 * LANES :]
        for row in range(HALF_ROWS):
            left, right = [
                [dw_ref[group, pl.ds(first, 32, stride=ROWS_OUT), :] for group in range(3)]
                for first in (row, row + HALF_ROWS)
            ]
            last = jnp.concatenate([left[2][:, :E], right[2][:, :E]], axis=1)
            at = N_SECOND * (REF_ROWS + row)
            for group, part in enumerate((left[0], left[1], right[0], right[1], last)):
                for low in range(2):
                    pack_ref[
                        2 * x + low, at : at + N_SECOND, LANES * group : LANES * (group + 1)
                    ] = pick(part, low).astype(BF16)
        for chunk in (2 * x, 2 * x + 1):
            stores.append(
                pltpu.make_async_copy(pack_ref.at[chunk], pack_out.at[chunk], out_sem.at[chunk])
            )
            stores[-1].start()
    for store in stores:
        store.wait()


def attention(q, k, v, pair, gt, tok):
    hbm, vmem = [pl.BlockSpec(memory_space=space) for space in (pltpu.HBM, pltpu.VMEM)]
    rows = REF_ROWS + HALF_ROWS
    return pl.pallas_call(
        attention_kernel,
        out_shape=(pltpu.HBM((WIDTH, P_SIZE), BF16),)
        + (pltpu.HBM((P_SIZE, 3 * WIDTH), BF16),)
        + (pltpu.HBM((N_FIRST, N_SECOND * rows, 2 * WIDTH), BF16),),
        in_specs=[hbm] * 4 + [vmem] * 2,
        out_specs=[hbm] * 3,
        scratch_shapes=[pltpu.VMEM((P_SIZE, WIDTH), BF16)] * 3
        + [
            pltpu.VMEM((4 * WIDTH, P_SIZE), BF16),
            pltpu.VMEM((N_FRAMES * 16, LANES), F32),
            pltpu.VMEM((P_SIZE, 2 * WIDTH), BF16),
            pltpu.VMEM((WIDTH, P_SIZE), F32),
            pltpu.VMEM((3, WIDTH, LANES), F32),
            pltpu.VMEM((WIDTH, P_SIZE), BF16),
            pltpu.VMEM((P_SIZE, 3 * WIDTH), BF16),
            pltpu.VMEM((N_FIRST, N_SECOND * rows, 2 * WIDTH), BF16),
            pltpu.SemaphoreType.DMA((4,)),
            pltpu.SemaphoreType.DMA((N_FIRST + 2,)),
        ],
        compiler_params=pltpu.CompilerParams(vmem_limit_bytes=VMEM_BYTES),
    )(*[pltpu.with_memory_space_constraint(a, pltpu.HBM) for a in (q, k, v, tok)], pair, gt)


def token_kernel(
    core_ref, grads_in, wq_in, wk_in, wv_in, kept_out, sent_out,
    grads_ref, w_ref, kept_ref, sent_ref, in_sem, out_sem,
):
    pairs = [(grads_in, grads_ref)]
    for i, w_in in enumerate((wq_in, wk_in, wv_in)):
        pairs.append((w_in, w_ref.at[pl.ds(i * WIDTH, WIDTH)]))
    loads = [pltpu.make_async_copy(a, b, in_sem.at[i]) for i, (a, b) in enumerate(pairs)]
    for load in loads:
        load.start()
    core = core_ref[0]
    for load in loads:
        load.wait()
    total = dot(grads_ref[...], w_ref[...], 1, 0)
    total = total.T.astype(BF16)
    stores = []
    for half in range(2):
        zero, one = [total[(2 * half + c) * WIDTH : (2 * half + c + 1) * WIDTH] for c in range(2)]
        sent_ref[half] = jnp.where(core == 0, one, zero)
        kept_ref[half] = jnp.where(core == 0, zero, one)
        for i, (a, b) in enumerate(((sent_ref, sent_out), (kept_ref, kept_out))):
            store = pltpu.make_async_copy(a.at[half], b.at[half], out_sem.at[2 * half + i])
            store.start()
            stores.append(store)
    for store in stores:
        store.wait()


def token_parts(core, grads, wq, wk, wv):
    hbm = pl.BlockSpec(memory_space=pltpu.HBM)
    return pl.pallas_call(
        token_kernel,
        out_shape=(pltpu.HBM((2, WIDTH, P_SIZE), BF16),) * 2,
        in_specs=[pl.BlockSpec(memory_space=pltpu.SMEM)] + [hbm] * 4,
        out_specs=[hbm] * 2,
        scratch_shapes=[
            pltpu.VMEM((P_SIZE, 3 * WIDTH), BF16),
            pltpu.VMEM((3 * WIDTH, 4 * WIDTH), BF16),
        ]
        + [pltpu.VMEM((2, WIDTH, P_SIZE), BF16)] * 2
        + [pltpu.SemaphoreType.DMA((4,)), pltpu.SemaphoreType.DMA((4,))],
        cost_estimate=pl.CostEstimate(flops=1, bytes_accessed=1, transcendentals=0),
        compiler_params=pltpu.CompilerParams(vmem_limit_bytes=VMEM_BYTES),
    )(
        core.reshape(1),
        *[pltpu.with_memory_space_constraint(a, pltpu.HBM) for a in (grads, wq, wk, wv)],
    )


def combine_kernel(half_ref, pair_ref, got_ref, out_ref):
    mine = jnp.where(half_ref[0] == 0, pair_ref[0].astype(F32), pair_ref[1].astype(F32))
    out_ref[...] = (mine + got_ref[...].astype(F32)).astype(BF16)


def combine(half, paired, got):
    vmem = pl.BlockSpec(memory_space=pltpu.VMEM)
    return pl.pallas_call(
        combine_kernel,
        out_shape=jax.ShapeDtypeStruct((WIDTH, P_SIZE), BF16),
        in_specs=[pl.BlockSpec(memory_space=pltpu.SMEM)] + [vmem] * 2,
        out_specs=vmem,
        cost_estimate=LONG,
        compiler_params=pltpu.CompilerParams(vmem_limit_bytes=8 * 1024 * 1024),
    )(half.reshape(1), paired, got)


def regroup_kernel(in_ref, out_ref, held_ref):
    rows = REF_ROWS + HALF_ROWS
    for row in range(rows):
        at = N_SECOND * row
        part = in_ref[0, at : at + N_SECOND, :].astype(F32)
        for x in range(1, N_FIRST):
            part = part + in_ref[x, at : at + N_SECOND, :].astype(F32)
        for group in range(GROUPS):
            held_ref[group, pl.ds(row, N_SECOND, stride=rows), :] = part[
                :, LANES * group : LANES * (group + 1)
            ]
    for group in range(GROUPS):
        out_ref[:, LANES * group : LANES * (group + 1)] = held_ref[group].astype(BF16)


def regroup(parts):
    rows = REF_ROWS + HALF_ROWS
    return pl.pallas_call(
        regroup_kernel,
        out_shape=jax.ShapeDtypeStruct((N_SECOND * rows, 2 * WIDTH), BF16),
        scratch_shapes=[pltpu.VMEM((GROUPS, N_SECOND * rows, LANES), F32)],
        cost_estimate=LONG,
        compiler_params=pltpu.CompilerParams(vmem_limit_bytes=8 * 1024 * 1024),
    )(parts)


def finish_kernel(in_ref, grad_ref, key_ref, value_ref):
    total = in_ref[0].astype(F32)
    for j in range(1, N_SECOND):
        total = total + in_ref[j].astype(F32)
    key_ref[...] = total[:REF_ROWS, :WIDTH].astype(BF16)
    value_ref[...] = total[:REF_ROWS, WIDTH:].astype(BF16)
    low, tail = total[:, : 4 * LANES], total[:, 4 * LANES :]
    left = jnp.concatenate([low[:, : 2 * LANES], tail[:, :E]], axis=1)
    right = jnp.concatenate([low[:, 2 * LANES :], tail[:, E:]], axis=1)
    grad_ref[:HALF_ROWS, :] = left[REF_ROWS:]
    grad_ref[HALF_ROWS:, :] = right[REF_ROWS:]


def finish(parts):
    return pl.pallas_call(
        finish_kernel,
        out_shape=(
            jax.ShapeDtypeStruct((ROWS_OUT, WIDTH), F32),
            jax.ShapeDtypeStruct((REF_ROWS, WIDTH), BF16),
            jax.ShapeDtypeStruct((REF_ROWS, WIDTH), BF16),
        ),
        compiler_params=pltpu.CompilerParams(vmem_limit_bytes=8 * 1024 * 1024),
    )(parts)


def per_device(
    tokens, reference_image, query_weight, key_weight, value_weight, ref_weight, cotangent
):
    core, half = lax.axis_index("c"), lax.axis_index("h")
    swap = [(0, 1), (1, 0)]
    wq, wk, wv = query_weight.T, key_weight.T, value_weight.T
    cols = ref_cols(2 * half + core, reference_image, ref_weight.T)
    cols = jnp.stack([cols, lax.ppermute(cols, "h", swap)])
    ref_hidden = lax.all_gather(cols, "c", axis=0, tiled=False)
    ref_hidden, own = lax.optimization_barrier((ref_hidden, tokens.T))
    other = lax.ppermute(own, "h", swap)
    pair = ref_pair(half, ref_hidden, wk, wv)
    pair = lax.all_to_all(pair, SECOND, 0, 0, tiled=True).reshape(N_SECOND * 16, LANES)
    blocks = stack(own, other)
    pair = lax.all_to_all(spread(pair), FIRST, 0, 0, tiled=True)
    parts = lax.all_gather(blocks, "c", axis=0, tiled=False)
    tok, queries, keys, values = project(half, parts, wq, wk, wv)
    attended, grads, pack = attention(
        queries, keys, values, pair.reshape(N_FRAMES * 16, LANES), cotangent.T, tok
    )
    pack = lax.all_to_all(pack, FIRST, 0, 0, tiled=True)
    kept, sent = token_parts(core, grads, wq, wk, wv)
    got = lax.ppermute(sent, "c", swap)
    paired = (kept.astype(F32) + got.astype(F32)).astype(BF16)
    sent = lax.dynamic_index_in_dim(paired, 1 - half, 0, False)
    got = lax.ppermute(sent, "h", swap)
    token_grads = combine(half, paired, got).T
    pack = regroup(pack)
    pack = pack.reshape(N_SECOND, REF_ROWS + HALF_ROWS, 2 * WIDTH)
    pack = lax.all_to_all(pack, SECOND, 0, 0, tiled=True)
    query_weight_grad, ref_key_grads, ref_value_grads = finish(pack)
    return attended.T, token_grads, query_weight_grad, ref_key_grads, ref_value_grads


def solution(mesh):
    mesh = Mesh(mesh.devices.reshape(4, 4, 2, 4, 2, 2), FRAMES + TENSOR)
    return jax.shard_map(
        per_device,
        mesh=mesh,
        in_specs=(
            P(FRAMES, TENSOR),
            P(FRAMES, None),
            P(None, TENSOR),
            P(None, TENSOR),
            P(None, TENSOR),
            P(None, TENSOR),
            P(FRAMES, TENSOR),
        ),
        out_specs=(P(FRAMES, TENSOR),) * 5,
        check_vma=False,
    )
```
